256 devices in a mesh: section: 2 (over core), stream: 16 (over x, y), slab: 8 (over z).
Axes of the slice: x: 4, y: 4, z: 8, core: 2. Of those that a mesh axis runs over, the one named last changes fastest.
Arguments:
- state: float32 [2, 4, 256, 128, 128], P('section', None, 'stream', 'slab'), may hold values from -6 to 6
- source_mask: int32 [16, 8], P(None, 'slab'), may hold values 0 or 1
- deriv_x: float32 [256, 256], replicated, may hold values from -0.28125 to 0.28125
- deriv_z: float32 [128, 128], replicated, may hold values from -0.397747564 to 0.397747564
- filter_x: float32 [256, 256], replicated, may hold values from -0.375 to 0.375
- filter_z: float32 [128, 128], replicated, may hold values from -0.5 to 0.5
Outputs:
- advanced: float32 [2, 4, 256, 128, 128], P('section', None, 'stream', 'slab')
The draws below stay inside these ranges and needn't reach their ends.
All inputs are finite; a program needn't handle non-finite values. No bound on the sum of `source_mask` on one device may be relied on, other than what follows from the above.
Results may differ from the reference program's by a relative error of at most 0.0001.
Values sent between devices are 32-bit elements; how exact they have to be, the bound alone decides.
No kernel may reach another device: no remote copies, remote signals or barrier semaphores. Data moves between devices by JAX's collectives and lax.ppermute only.
A program may use at most 64 MiB of HBM per device.

```python
import math
import jax
import jax.numpy as jnp
from jax import lax

NX = 256
NZ = 128
SEGMENTS = 8
MBLK = 16
NY = 128


def dense_operator(key, order):
    limit = 4.5 / math.sqrt(order)
    values = jnp.clip(3.0 / math.sqrt(order) * jax.random.normal(key, (order, order), jnp.float32), -limit, limit)
    return values


def draw_deriv_x(key, part):
    return dense_operator(jax.random.fold_in(key, 11), NX)


def draw_deriv_z(key, part):
    return dense_operator(jax.random.fold_in(key, 23), NZ)


def touch_ends(array, stream_key, low, largest):
    dims = array.shape
    place = [jax.random.randint(jax.random.fold_in(stream_key, axis), (), 0, dims[axis]) for axis in range(len(dims))]
    array = array.at[tuple(place)].set(low)
    longest = dims.index(max(dims))
    place[longest] = (place[longest] + 1) % dims[longest]
    return array.at[tuple(place)].set(largest)


def shard_levels(own_key, dims, cuts, least, largest):
    def one(position, blocks):
        steps = jax.random.uniform(jax.random.fold_in(jax.random.fold_in(own_key, 6), position), (blocks,), jnp.float32, least / len(cuts), largest / len(cuts))
        return jnp.repeat(jnp.exp(steps), dims[position] // blocks).reshape((-1,) + (1,) * (len(dims) - position - 1))

    level = one(*cuts[0])
    for cut in cuts[1:]:
        level = level * one(*cut)
    return level


def normal_values(own_key, dims, width, bound, cuts=(), held_as=jnp.bfloat16):
    entries = width * jax.random.normal(own_key, dims, jnp.float32)
    if cuts:
        entries = entries * shard_levels(own_key, dims, cuts, -0.22, 0.18)
    return jnp.clip(entries, -bound, bound).astype(held_as)


def setup_inputs(seed: int = 0) -> dict:
    arg_keys = jax.random.split(jax.random.key(seed), 7)
    return {
        "state": normal_values(arg_keys[0], (2, 4, NX, NY, NZ), 1.0, 6.0, ((0, 2), (2, 16), (3, 8)), jnp.float32),
        "source_mask": touch_ends((jax.random.randint(arg_keys[1], (NX // MBLK, NY // MBLK), 0, 2) < 1).astype(jnp.int32), jax.random.fold_in(arg_keys[1], 1), 0, 1),
        "deriv_x": draw_deriv_x(jax.random.fold_in(arg_keys[6], 71), 0),
        "deriv_z": draw_deriv_z(jax.random.fold_in(arg_keys[6], 71), 0),
        "filter_x": normal_values(arg_keys[4], (NX, NX), NX ** -0.5, 0.375, (), jnp.float32),
        "filter_z": normal_values(arg_keys[5], (NZ, NZ), NZ ** -0.5, 0.5, (), jnp.float32),
    }


mach_number = 0.5
time_step = 0.05
filter_weight = 0.25


def central_slope(values, which_dim):
    widths = [(0, 0), (0, 0), (0, 0)]
    widths[which_dim] = (1, 1)
    padded = jnp.pad(values, widths)
    length = values.shape[which_dim]
    upper_side = lax.slice_in_dim(padded, 2, length + 2, axis=which_dim)
    lower_side = lax.slice_in_dim(padded, 0, length, axis=which_dim)
    return 0.5 * (upper_side - lower_side)


def lamb_vector(velocity):
    speed_x, speed_y, speed_z = velocity[0], velocity[1], velocity[2]
    vortex_x = central_slope(speed_z, 1) - central_slope(speed_y, 2)
    vortex_y = central_slope(speed_x, 2) - central_slope(speed_z, 0)
    vortex_z = central_slope(speed_y, 0) - central_slope(speed_x, 1)
    return jnp.stack([vortex_y * speed_z - vortex_z * speed_y,
                      vortex_z * speed_x - vortex_x * speed_z,
                      vortex_x * speed_y - vortex_y * speed_x])


def along_x(matrix, fields):
    return jnp.einsum("ij,fjyz->fiyz", matrix, fields, precision=lax.Precision.HIGHEST)


def along_z(matrix, fields):
    return jnp.einsum("fxyz,kz->fxyk", fields, matrix, precision=lax.Precision.HIGHEST)


def fourth_slope_y(fields):
    padded = jnp.pad(fields, ((0, 0), (0, 0), (2, 2), (0, 0)))
    length = fields.shape[2]

    def shifted(offset):
        return lax.slice_in_dim(padded, 2 + offset, 2 + offset + length, axis=2)

    return (8.0 * (shifted(1) - shifted(-1)) - (shifted(2) - shifted(-2))) / 12.0


def tendency(fields, slope_x, slope_y, slope_z, forcing):
    press_rate = -mach_number * slope_x[0] - slope_x[1] - slope_y[1] - slope_z[1]
    axial_rate = -mach_number * slope_x[1] - slope_x[0] + forcing[0]
    normal_rate = -mach_number * slope_x[2] - slope_y[0] + forcing[1]
    third_rate = -mach_number * slope_x[3] - slope_z[0] + forcing[2]
    return jnp.stack([press_rate, axial_rate, normal_rate, third_rate])


def substep(fields, forcing, deriv_x, deriv_z):
    slope_x = along_x(deriv_x, fields)
    slope_y = fourth_slope_y(jnp.stack([fields[0], fields[2]]))
    slope_z = along_z(deriv_z, jnp.stack([fields[0], fields[3]]))
    return fields + time_step * tendency(fields, slope_x, slope_y, slope_z, forcing)


def reference(state, source_mask, deriv_x, deriv_z, filter_x, filter_z):
    region = jnp.repeat(jnp.repeat(source_mask, MBLK, axis=0), MBLK, axis=1).astype(jnp.float32)
    flow_now = state[0]
    sound_now = state[1]
    no_forcing = jnp.zeros((3,) + flow_now.shape[1:], jnp.float32)
    forcing = no_forcing
    for segment_index in range(SEGMENTS):
        if segment_index % 2 == 0:
            forcing = -region[None, :, :, None] * lamb_vector(flow_now[1:4])
        flow_now = substep(flow_now, no_forcing, deriv_x, deriv_z)
        sound_now = substep(sound_now, forcing, deriv_x, deriv_z)

    def smooth(fields):
        return fields + filter_weight * along_x(filter_x, fields) + filter_weight * along_z(filter_z, fields)

    return jnp.stack([smooth(flow_now), smooth(sound_now)])
```

```python
import jax
import jax.numpy as jnp
import numpy as np
from jax import lax
from jax.sharding import PartitionSpec as P

mach_number = 0.5
time_step = 0.05
filter_weight = 0.25
REACH = 12
OUT_P, OUT_U, OUT_V, OUT_W = 14, 10, 12, 10
HIGH = lax.Precision.HIGH
BEST = lax.Precision.HIGHEST


def y_operators(count):
    near = np.eye(count, k=1) - np.eye(count, k=-1)
    far = np.eye(count, k=2) - np.eye(count, k=-2)
    return (8.0 * near - far) / 12.0, 0.5 * near


def left(matrix, fields):
    return jnp.einsum("ij,fjz->fiz", matrix, fields, precision=HIGH)


def right(fields, matrix):
    return jnp.einsum("fxz,zk->fxk", fields, matrix, precision=HIGH)


def slope(values, axis):
    widths = [(0, 0)] * values.ndim
    widths[axis] = (1, 1)
    padded = jnp.pad(values, widths)
    length = values.shape[axis]
    return 0.5 * (
        lax.slice_in_dim(padded, 2, length + 2, axis=axis) - lax.slice_in_dim(padded, 0, length, axis=axis)
    )


def to_next(value, count):
    return lax.ppermute(value, "slab", [(i, i + 1) for i in range(count - 1)])


def to_previous(value, count):
    return lax.ppermute(value, "slab", [(i + 1, i) for i in range(count - 1)])


def spread_fields(ext, deriv_z, own, slab, slabs):
    slope4, slope2 = y_operators(own * slabs)
    square = slope4 @ slope4
    powers = [np.eye(own * slabs), square, square @ square]
    rows = [lead @ power for lead in (np.eye(own * slabs), slope2, slope4) for power in powers]
    table = np.stack([np.pad(row, ((0, 0), (REACH, REACH))) for row in rows]).astype(np.float32)
    table_v = np.stack([np.pad(row @ slope4, ((0, 0), (REACH, REACH))) for row in rows]).astype(np.float32)
    start = slab * own
    size = (9, own, own + 2 * REACH)
    mine = lax.dynamic_slice(jnp.asarray(table), (0, start, start), size)
    mine_v = lax.dynamic_slice(jnp.asarray(table_v), (0, start, start), size)
    through_z = jnp.einsum("xyz,kz->xyk", ext[3], deriv_z, precision=HIGH)

    def apply(weights, value):
        return jnp.einsum("vky,xyz->vxkz", weights, value, precision=HIGH)

    centre = ext[:, :, REACH : REACH + own]
    of_p = apply(mine[1:], ext[0])
    of_u = apply(mine[1:], ext[1])
    of_e = apply(
        jnp.concatenate([mine_v, mine], axis=2), jnp.concatenate([ext[2], through_z], axis=1)
    )
    of_w = apply(mine[3:4], ext[3])
    return jnp.concatenate([centre[0:1], of_p, centre[1:2], of_u, of_e, centre[2:4], of_w])


def plane_stage(fields, region, deriv_x, deriv_z, filter_x, filter_z):
    tau = time_step
    square_x = jnp.dot(deriv_x, deriv_x, precision=BEST)
    e1 = -tau * mach_number * deriv_x
    e2 = 2.0 * e1 + (tau * mach_number) ** 2 * square_x
    e4 = 2.0 * e2 + jnp.dot(e2, e2, precision=BEST)
    e6 = e2 + e4 + jnp.dot(e2, e4, precision=BEST)
    e8 = 2.0 * e4 + jnp.dot(e4, e4, precision=BEST)
    m1 = 2.0 * e1
    m2 = tau**2 * square_x - e2
    turned = deriv_z.T
    square_z = tau**2 * jnp.dot(turned, turned, precision=BEST)

    def advance(now, before, raised):
        return (
            2.0 * now - before + left(m1, now) + left(m2, before) + right(before, square_z) + tau**2 * raised
        )

    def apply_a(value):
        return value + left(e1, value)

    nx, nz = fields.shape[1:]
    p0 = fields[0:9]
    u0 = fields[9:18]
    w0, v0 = fields[28:29], fields[27:28]
    slope_w0 = fields[29:30]
    p1 = p0 + left(e1, p0) - tau * (left(deriv_x, u0) + fields[18:27])

    def levels(value, count):
        return value.reshape(3, -1, nx, nz)[:, :count].reshape(3 * count, nx, nz)

    def upper(value, first):
        whole = value.reshape(3, -1, nx, nz)
        return whole[:, first:].reshape(-1, nx, nz)

    p2 = advance(levels(p1, 2), levels(p0, 2), upper(p0, 1))
    p3 = advance(p2, levels(p1, 2), upper(p1, 1))
    p4 = advance(levels(p3, 1), levels(p2, 1), upper(p2, 1))
    p5 = advance(p4, levels(p3, 1), upper(p3, 1))
    h2 = apply_a(levels(p0, 1)) + levels(p1, 1)
    h4 = h2 + left(e2, h2) + apply_a(levels(p2, 1)) + levels(p3, 1)
    h6 = h4 + left(e2, h4) + apply_a(p4) + p5

    start = jnp.concatenate([u0[0:1], u0[3:4], w0, slope_w0, v0])
    times = [start]
    for growth, h in ((e2, h2), (e4, h4), (e6, h6)):
        held = start + left(growth, start)
        pull = jnp.concatenate([left(deriv_x, h[:2]), right(h[:2], turned), h[2:3]])
        times.append(held - tau * pull)
    u, slope_u, w, slope_w, v = [jnp.stack([t[k] for t in times]) for k in range(5)]
    o_x = slope_w - slope(v, 2)
    o_y = slope(u, 2) - slope(w, 1)
    o_z = slope(v, 1) - slope_u
    lamb = jnp.concatenate([o_y * w - o_z * v, o_z * u - o_x * w, o_x * v - o_y * u])
    source = lax.ppermute(-region[None, :, None] * lamb, "section", [(0, 1)])
    s_x, s_y, s_z = source[0:4], source[4:8], source[8:12]
    inner = left(deriv_x, s_x) + right(s_z, turned)

    zero = jnp.zeros((1, nx, nz), jnp.float32)

    def widen(value, count):
        return jnp.concatenate([value] + [zero] * (count - value.shape[0]))

    def driven(now, before, k, which):
        out = 2.0 * widen(now, k) - widen(before, k)
        out += widen(left(m1, now), k) + widen(left(m2, before) + right(before, square_z), k)
        raised = jnp.concatenate([zero, zero, tau**2 * before])
        out += widen(raised[:k], k)
        drive = jnp.concatenate([inner[which : which + 1], s_y[which : which + 1]])
        return out - widen(tau**2 * drive, k)

    drive0 = -(tau**2) * jnp.concatenate([inner[0:1], s_y[0:1]])
    q2 = drive0
    q3 = 2.0 * q2 + left(m1, q2) + drive0
    q4 = driven(q3, q2, 4, 1)
    q5 = driven(q4, q3, 4, 1)
    g4 = apply_a(q2) + q3
    g6 = widen(g4 + left(e2, g4), 4) + apply_a(q4) + q5
    q4 = q4.at[0].add(p4[0])
    q5 = q5.at[0].add(p5[0])
    g6 = g6.at[0].add(h6[0])
    q6 = driven(q5, q4, 6, 2)
    q7 = driven(q6, q5, 6, 2)
    q8 = driven(q7, q6, 8, 3)
    g8 = widen(g6 + left(e2, g6), 6) + apply_a(q6) + q7

    total = jnp.stack([s_x[0], s_y[0], s_z[0]])
    for n in (1, 2, 3):
        total = total + left(e2, total) + jnp.stack([s_x[n], s_y[n], s_z[n]])
    total = total + apply_a(total)
    begin = jnp.concatenate([u0[0:1], v0, w0])
    velocity = begin + left(e8, begin) + tau * total
    axial = widen(velocity[0:1], 6) - tau * left(deriv_x, g8)
    third = widen(velocity[2:3], 6) - tau * right(g8, turned)
    every = jnp.concatenate([q8, axial, velocity[1:2], -tau * g8, third])
    return every + filter_weight * (left(filter_x, every) + right(every, filter_z.T))


def gather_fields(fields, own, slab, slabs):
    slope4, _ = y_operators(own * slabs)
    power = np.eye(own * slabs)
    powers = []
    for _ in range(8):
        powers.append(power)
        power = slope4 @ power

    def block(count, reach):
        rows = powers[1:count]
        table = np.stack([np.pad(row, ((reach, reach), (0, 0))) for row in rows]).astype(np.float32)
        return lax.dynamic_slice(
            jnp.asarray(table), (0, slab * own, slab * own), (count - 1, own + 2 * reach, own)
        )

    def apply(weights, value):
        return jnp.einsum("fky,fxyz->xkz", weights, value, precision=HIGH)

    parts = []
    lead = 0
    for count, reach in ((8, OUT_P), (6, OUT_U), (7, OUT_V), (6, OUT_W)):
        parts.append((apply(block(count, reach), fields[lead + 1 : lead + count]), reach, lead))
        lead += count
    above = jnp.concatenate([value[:, own + reach :] for value, reach, _ in parts], axis=1)
    below = jnp.concatenate([value[:, :reach] for value, reach, _ in parts], axis=1)
    from_below = to_next(above, slabs)
    from_above = to_previous(below, slabs)
    sums = []
    at = 0
    for value, reach, lead in parts:
        centre = value[:, reach : reach + own]
        low = jnp.pad(from_below[:, at : at + reach], ((0, 0), (0, own - reach), (0, 0)))
        high = jnp.pad(from_above[:, at : at + reach], ((0, 0), (own - reach, 0), (0, 0)))
        sums.append(fields[lead] + centre + low + high)
        at += reach
    return jnp.stack(sums)


def shards(state, source_mask, deriv_x, deriv_z, filter_x, filter_z):
    own = state.shape[3]
    slabs = lax.axis_size("slab")
    slab = lax.axis_index("slab")
    raw = state[0]
    ext = jnp.concatenate(
        [to_next(raw[:, :, own - REACH :], slabs), raw, to_previous(raw[:, :, :REACH], slabs)], axis=2
    )
    spread = spread_fields(ext, deriv_z, own, slab, slabs)
    planes = lax.all_to_all(spread, "stream", split_axis=2, concat_axis=1, tiled=True)[:, :, 0]
    nx = planes.shape[1]
    region = jnp.repeat(source_mask[:, 0].astype(jnp.float32), nx // source_mask.shape[0])
    done = plane_stage(planes, region, deriv_x, deriv_z, filter_x, filter_z)
    back = lax.all_to_all(done[:, :, None], "stream", split_axis=1, concat_axis=2, tiled=True)
    return gather_fields(back, own, slab, slabs)[None]


def solution(mesh):
    placed = (P("section", None, "stream", "slab", None), P(None, "slab"), P(), P(), P(), P())
    return jax.shard_map(
        shards,
        mesh=mesh,
        in_specs=placed,
        out_specs=P("section", None, "stream", "slab", None),
        check_vma=False,
    )
```

```python
import functools

import jax
import jax.numpy as jnp
from jax import lax
from jax.experimental import pallas as pl
from jax.experimental.pallas import tpu as pltpu
from jax.sharding import PartitionSpec as P

mach_number = 0.5
tau = 0.05
filter_weight = 0.25
REACH = 10
OUT_P, OUT_U, OUT_V, OUT_W = 14, 10, 12, 10
AXES = ("section", "stream", "slab")
LEFT = ("e1", "ta", "m1", "m2", "e2", "a", "e4", "e6", "e8", "fx")
RIGHT = ("c", "cc", "fz")
f32, bf16 = jnp.float32, jnp.bfloat16


def call(body, out_shape, *args, flops=0, scratch=()):
    moved = sum(a.size * a.dtype.itemsize for a in args)
    return pl.pallas_call(
        body,
        out_shape=out_shape,
        scratch_shapes=scratch,
        compiler_params=pltpu.CompilerParams(vmem_limit_bytes=40 * 2**20),
        cost_estimate=pl.CostEstimate(flops=flops, bytes_accessed=moved, transcendentals=0),
    )(*args)


def halves(value):
    high = value.astype(bf16)
    return high, (value - high.astype(f32)).astype(bf16)


def left_form(matrix):
    high, low = halves(matrix)
    return jnp.concatenate([high, high, low], axis=1)


def right_form(matrix):
    high, low = halves(matrix)
    return jnp.concatenate([high, high, low], axis=0)


def times_left(form, planes):
    high, low = halves(jnp.concatenate(planes, axis=1))
    out = jnp.dot(form, jnp.concatenate([high, low, high], axis=0), preferred_element_type=f32)
    width = planes[0].shape[1]
    return [out[:, i * width : (i + 1) * width] for i in range(len(planes))]


def times_right(planes, form):
    high, low = halves(jnp.concatenate(planes, axis=0))
    out = jnp.dot(jnp.concatenate([high, low, high], axis=1), form, preferred_element_type=f32)
    length = planes[0].shape[0]
    return [out[i * length : (i + 1) * length] for i in range(len(planes))]


def prepare_kernel(dx_ref, dzt_ref, fx_ref, fzt_ref, left_ref, right_ref):
    def dot(one, two):
        return jnp.dot(one, two, precision=lax.Precision.HIGHEST, preferred_element_type=f32)

    dx, dzt = dx_ref[...], dzt_ref[...]
    square = dot(dx, dx)
    e1 = -tau * mach_number * dx
    e2 = 2.0 * e1 + (tau * mach_number) ** 2 * square
    e4 = 2.0 * e2 + dot(e2, e2)
    values = {
        "e1": e1,
        "ta": -tau * dx,
        "m1": 2.0 * e1,
        "m2": tau**2 * square - e2,
        "e2": e2,
        "a": dx,
        "e4": e4,
        "e6": e2 + e4 + dot(e2, e4),
        "e8": 2.0 * e4 + dot(e4, e4),
        "fx": filter_weight * fx_ref[...],
    }
    for i, name in enumerate(LEFT):
        left_ref[i] = left_form(values[name])
    others = {"c": dzt, "cc": tau**2 * dot(dzt, dzt), "fz": filter_weight * fzt_ref[...]}
    for i, name in enumerate(RIGHT):
        right_ref[i] = right_form(others[name])


class Products:
    def __init__(self, left_ref, right_ref):
        self.left_ref, self.right_ref = left_ref, right_ref

    def left(self, name, planes):
        return times_left(self.left_ref[LEFT.index(name)], planes)

    def right(self, planes, name):
        return times_right(planes, self.right_ref[RIGHT.index(name)])


def inside(value, reach, low_ok, high_ok):
    rows = value.shape[0]
    return jnp.concatenate(
        [value[:reach] * low_ok, value[reach : rows - reach], value[rows - reach :] * high_ok], axis=0
    )


def shift_rows(value, steps):
    zeros = jnp.zeros((abs(steps),) + value.shape[1:], f32)
    if steps > 0:
        return jnp.concatenate([value[steps:], zeros], axis=0)
    return jnp.concatenate([zeros, value[:steps]], axis=0)


def slope4(value):
    near = shift_rows(value, 1) - shift_rows(value, -1)
    far = shift_rows(value, 2) - shift_rows(value, -2)
    return (2.0 / 3.0) * near - (1.0 / 12.0) * far


def spread_kernel(edge_ref, ext_ref, right_ref, out_ref):
    low_ok, high_ok = edge_ref[0], edge_ref[1]
    own = ext_ref.shape[1] - 2 * REACH
    rows, xs, nz = ext_ref.shape[1:]

    def twice(value):
        once = inside(slope4(value), REACH, low_ok, high_ok)
        return inside(slope4(once), REACH, low_ok, high_ok)

    def put(place, value):
        out_ref[:, place] = value[REACH : REACH + own]

    def slope2(ref_index):
        return 0.5 * (
            ext_ref[ref_index, REACH + 1 : REACH + 1 + own] - ext_ref[ref_index, REACH - 1 : REACH - 1 + own]
        )

    through = times_right([ext_ref[3].reshape(rows * xs, nz)], right_ref[RIGHT.index("c")])[0]
    rate = through.reshape(rows, xs, nz) + slope4(ext_ref[2])
    rate = inside(rate, REACH, low_ok, high_ok)
    for place, value in ((0, ext_ref[0]), (3, ext_ref[1]), (6, rate)):
        put(place, value)
        value = twice(value)
        put(place + 1, value)
        put(place + 2, twice(value))
    put(9, ext_ref[2])
    put(10, ext_ref[3])
    out_ref[:, 11] = slope2(1)
    out_ref[:, 12] = slope2(3)


def gather_kernel(edge_ref, back_ref, own_ref, high_ref, low_ref):
    low_ok, high_ok = edge_ref[0], edge_ref[1]
    own = back_ref.shape[0]
    lead = 0
    place = 0
    for output, (count, reach) in enumerate(((8, OUT_P), (6, OUT_U), (7, OUT_V), (6, OUT_W))):
        total = back_ref[:, lead + count - 1]
        for k in range(count - 2, -1, -1):
            edge = 2 * (count - 1 - k)
            zeros = jnp.zeros((2,) + total.shape[1:], f32)
            total = slope4(jnp.concatenate([zeros, total, zeros], axis=0))
            total = jnp.concatenate(
                [
                    total[:edge] * low_ok,
                    total[edge : edge + own] + back_ref[:, lead + k],
                    total[edge + own :] * high_ok,
                ],
                axis=0,
            )
        own_ref[output] = total[reach : reach + own]
        low_ref[place : place + reach] = total[:reach]
        high_ref[place : place + reach] = total[reach + own :]
        place += reach
        lead += count


def plane(ref, index):
    blocks, _, xs, nz = ref.shape
    return ref[:, index].reshape(blocks * xs, nz)


def waves_kernel(in_ref, left_ref, right_ref, out_ref):
    do = Products(left_ref, right_ref)
    p0 = [plane(in_ref, i) for i in range(3)]
    u0 = [plane(in_ref, 3 + i) for i in range(3)]

    def advance(now, before):
        count = len(before) - 1
        one = do.left("m1", now[:count])
        two = do.left("m2", before[:count])
        three = do.right(before[:count], "cc")
        return [
            2.0 * now[i] - before[i] + (one[i] + two[i] + three[i] + tau**2 * before[i + 1])
            for i in range(count)
        ]

    moved = do.left("e1", p0)
    driven = do.left("ta", u0)
    p1 = [p0[i] + (moved[i] + driven[i] - tau * plane(in_ref, 6 + i)) for i in range(3)]
    h2 = p0[0] + moved[0] + p1[0]
    out_ref[2] = h2
    p2 = advance(p1, p0)
    p3 = advance(p2, p1)
    h4 = h2 + do.left("e2", [h2])[0] + p2[0] + do.left("e1", p2[:1])[0] + p3[0]
    out_ref[3] = h4
    p4 = advance(p3, p2)
    p5 = advance(p4, p3)
    h6 = h4 + do.left("e2", [h4])[0] + p4[0] + do.left("e1", p4)[0] + p5[0]
    out_ref[0] = p4[0]
    out_ref[1] = p5[0]
    out_ref[4] = h6


def held_kernel(in_ref, waves_ref, left_ref, right_ref, out_ref):
    do = Products(left_ref, right_ref)
    start = [plane(in_ref, i) for i in (3, 10, 11, 12, 9)]
    h = [waves_ref[2 + n] for n in range(3)]
    pull_x = do.left("a", h)
    pull_z = do.right(h, "c")
    for n, growth in enumerate(("e2", "e4", "e6")):
        change = do.left(growth, start)
        out_ref[n, 0] = start[0] + change[0] - tau * pull_x[n]
        out_ref[n, 1] = start[1] + change[1] - tau * pull_z[n]
        for k in (2, 3, 4):
            out_ref[n, k] = start[k] + change[k]


def source_kernel(region_ref, in_ref, held_ref, up1_ref, down1_ref, up2_ref, down2_ref, left_ref, right_ref, out_ref):
    do = Products(left_ref, right_ref)
    nx, nz = up1_ref.shape[1:]
    row = lax.broadcasted_iota(jnp.int32, (nx, nz), 0)
    lane = lax.broadcasted_iota(jnp.int32, (nx, nz), 1)
    region = region_ref[...]

    def slope_x(value):
        ahead = jnp.where(row == nx - 1, 0.0, pltpu.roll(value, nx - 1, 0))
        behind = jnp.where(row == 0, 0.0, pltpu.roll(value, 1, 0))
        return 0.5 * (ahead - behind)

    def slope_z(value):
        ahead = jnp.where(lane == nz - 1, 0.0, pltpu.roll(value, nz - 1, 1))
        behind = jnp.where(lane == 0, 0.0, pltpu.roll(value, 1, 1))
        return 0.5 * (ahead - behind)

    near = [up1_ref[n] - down1_ref[n] for n in range(3)]
    half = [0.5 * value for value in near]
    pull_x = do.left("a", half)
    pull_z = do.right(half, "c")
    for n in range(4):
        if n == 0:
            u, w, slope_u, slope_w, v = [plane(in_ref, i) for i in (3, 10, 11, 12, 9)]
        else:
            u, w = held_ref[n - 1, 0], held_ref[n - 1, 1]
            slope_u = held_ref[n - 1, 2] - tau * pull_x[n - 1]
            slope_w = held_ref[n - 1, 3] - tau * pull_z[n - 1]
            far = up2_ref[n - 1] - down2_ref[n - 1]
            v = held_ref[n - 1, 4] - tau * ((2.0 / 3.0) * near[n - 1] - (1.0 / 12.0) * far)
        o_x = slope_w - slope_z(v)
        o_y = slope_z(u) - slope_x(w)
        o_z = slope_x(v) - slope_u
        out_ref[n, 0] = region * (o_z * v - o_y * w)
        out_ref[n, 1] = region * (o_x * w - o_z * u)
        out_ref[n, 2] = region * (o_y * u - o_x * v)


class Chain:
    def __init__(self, left_ref, right_ref):
        self.do = Products(left_ref, right_ref)

    def advance(self, now, before, drive, count):
        m_now = self.do.left("m1", now)
        m_before = self.do.left("m2", before)
        c_before = self.do.right(before, "cc")
        out = []
        for k in range(count):
            terms = []
            if k < len(now):
                terms.append(2.0 * now[k] + m_now[k])
            if k < len(before):
                terms.append(m_before[k] + c_before[k] - before[k])
            if 0 <= k - 2 < len(before):
                terms.append(tau**2 * before[k - 2])
            if k < len(drive):
                terms.append(drive[k])
            out.append(functools.reduce(lambda one, two: one + two, terms))
        return out

    def grow(self, sums, before, now):
        moved = self.do.left("e1", before)
        kept = self.do.left("e2", sums) if sums else []
        out = [before[k] + moved[k] + now[k] for k in range(len(now))]
        return [out[k] + (sums[k] + kept[k]) if k < len(sums) else out[k] for k in range(len(now))]


def drives(do, source_ref, first, last):
    one = do.left("a", [source_ref[n, 0] for n in range(first, last)])
    two = do.right([source_ref[n, 2] for n in range(first, last)], "c")
    return [
        (-(tau**2) * (one[n - first] + two[n - first]), -(tau**2) * source_ref[n, 1])
        for n in range(first, last)
    ]


def driven_kernel(waves_ref, source_ref, left_ref, right_ref, out_ref):
    chain = Chain(left_ref, right_ref)
    drive = drives(chain.do, source_ref, 0, 2)
    q2 = list(drive[0])
    moved = chain.do.left("m1", q2)
    q3 = [2.0 * q2[k] + moved[k] + drive[0][k] for k in range(2)]
    g4 = chain.grow([], q2, q3)
    q4 = chain.advance(q3, q2, drive[1], 4)
    q5 = chain.advance(q4, q3, drive[1], 4)
    g6 = chain.grow(g4, q4, q5)
    for first, values, wave in ((0, q4, 0), (4, q5, 1), (8, g6, 4)):
        out_ref[first] = values[0] + waves_ref[wave]
        for k in range(1, 4):
            out_ref[first + k] = values[k]


def finish_kernel(in_ref, driven_ref, source_ref, left_ref, right_ref, out_ref):
    chain = Chain(left_ref, right_ref)
    do = chain.do
    drive = drives(do, source_ref, 2, 4)
    q4, q5, g6 = [[driven_ref[first + k] for k in range(4)] for first in (0, 4, 8)]
    q6 = chain.advance(q5, q4, drive[0], 6)
    q7 = chain.advance(q6, q5, drive[0], 6)
    for k, value in enumerate(chain.grow(g6, q6, q7)):
        out_ref[8 + k] = value
    for k, value in enumerate(chain.advance(q7, q6, drive[1], 8)):
        out_ref[k] = value
    total = [source_ref[0, k] for k in range(3)]
    for n in (1, 2, 3):
        kept = do.left("e2", total)
        total = [total[k] + kept[k] + source_ref[n, k] for k in range(3)]
    moved = do.left("e1", total)
    begin = [plane(in_ref, i) for i in (3, 9, 10)]
    kept = do.left("e8", begin)
    for i in range(3):
        out_ref[14 + i] = begin[i] + kept[i] + tau * (2.0 * total[i] + moved[i])


def filter_kernel(last_ref, left_ref, right_ref, out_ref):
    do = Products(left_ref, right_ref)
    blocks, _, xs, nz = out_ref.shape

    def emit(place, values):
        fx, fz = do.left("fx", values), do.right(values, "fz")
        for i, value in enumerate(values):
            out_ref[:, place + i] = (value + fx[i] + fz[i]).reshape(blocks, xs, nz)

    emit(0, [last_ref[k] for k in range(8)])
    g8 = [last_ref[8 + k] for k in range(6)]
    axial = do.left("ta", g8)
    axial[0] = last_ref[14] + axial[0]
    emit(8, axial)
    emit(14, [last_ref[15]] + [-tau * value for value in g8])
    third = [-tau * value for value in do.right(g8, "c")]
    third[0] = last_ref[16] + third[0]
    emit(21, third)


def along_y(steps):
    streams, slabs = lax.axis_size("stream"), lax.axis_size("slab")
    count = streams * slabs

    def device(y):
        return (y % streams) * slabs + y // streams

    return [(device(y), device(y + steps)) for y in range(max(0, -steps), min(count, count - steps))]


def shards(state, source_mask, deriv_x, deriv_z, filter_x, filter_z):
    _, _, xs, own, nz = state.shape
    slabs, streams = lax.axis_size("slab"), lax.axis_size("stream")
    slab = lax.axis_index("slab")
    nx = xs * streams
    upward = [(i, i + 1) for i in range(slabs - 1)]
    downward = [(i + 1, i) for i in range(slabs - 1)]
    edges = jnp.stack([(slab > 0).astype(f32), (slab < slabs - 1).astype(f32)])
    region = jnp.repeat(source_mask[:, 0].astype(f32), nx // source_mask.shape[0])
    region = jnp.broadcast_to(region[:, None], (nx, nz))

    raw = jnp.swapaxes(state[0], 1, 2)
    from_low = lax.ppermute(raw[:, own - REACH :], "slab", upward)
    from_high = lax.ppermute(raw[:, :REACH], "slab", downward)
    left, right = call(
        prepare_kernel,
        (
            jax.ShapeDtypeStruct((len(LEFT), nx, 3 * nx), bf16),
            jax.ShapeDtypeStruct((len(RIGHT), 3 * nz, nz), bf16),
        ),
        deriv_x,
        deriv_z.T,
        filter_x,
        filter_z.T,
        flops=10**9,
    )
    ext = jnp.concatenate([from_low, raw, from_high], axis=1)

    def shape(*dims):
        return jax.ShapeDtypeStruct(dims, f32)

    def with_edges(body, out_shape, *args):
        return pl.pallas_call(
            body,
            out_shape=out_shape,
            in_specs=[pl.BlockSpec(memory_space=pltpu.SMEM)]
            + [pl.BlockSpec(memory_space=pltpu.VMEM)] * len(args),
            compiler_params=pltpu.CompilerParams(vmem_limit_bytes=40 * 2**20),
        )(edges, *args)

    spread = with_edges(spread_kernel, shape(own, 13, xs, nz), ext, right)
    planes = lax.all_to_all(spread, "stream", split_axis=0, concat_axis=0, tiled=True)
    waves = call(waves_kernel, shape(5, nx, nz), planes, left, right, flops=2 * 10**9)
    sums = waves[2:5]
    near = [lax.ppermute(sums, AXES, along_y(steps)) for steps in (-1, 1, -2, 2)]
    held = call(held_kernel, shape(3, 5, nx, nz), planes, waves, left, right, flops=10**9)
    source = call(
        source_kernel, shape(4, 3, nx, nz), region, planes, held, *near, left, right, flops=10**9
    )
    source = lax.ppermute(source, "section", [(0, 1)])
    driven = call(driven_kernel, shape(12, nx, nz), waves, source, left, right, flops=2 * 10**9)
    last = call(finish_kernel, shape(17, nx, nz), planes, driven, source, left, right, flops=3 * 10**9)
    done = call(filter_kernel, shape(streams, 27, xs, nz), last, left, right, flops=10**9)
    back = lax.all_to_all(done, "stream", split_axis=0, concat_axis=0, tiled=True)
    border = OUT_P + OUT_U + OUT_V + OUT_W
    mine, high, low = with_edges(
        gather_kernel, (shape(4, own, xs, nz), shape(border, xs, nz), shape(border, xs, nz)), back
    )
    from_low = lax.ppermute(high, "slab", upward)
    from_high = lax.ppermute(low, "slab", downward)
    place = 0
    outs = []
    for i, reach in enumerate((OUT_P, OUT_U, OUT_V, OUT_W)):
        rest = ((0, own - reach), (0, 0), (0, 0))
        from_below = jnp.pad(from_low[place : place + reach], rest)
        from_above = jnp.pad(from_high[place : place + reach], ((own - reach, 0), (0, 0), (0, 0)))
        outs.append(mine[i] + from_below + from_above)
        place += reach
    return jnp.swapaxes(jnp.stack(outs), 1, 2)[None]


def solution(mesh):
    placed = (P("section", None, "stream", "slab", None), P(None, "slab"), P(), P(), P(), P())
    return jax.shard_map(
        shards,
        mesh=mesh,
        in_specs=placed,
        out_specs=P("section", None, "stream", "slab", None),
        check_vma=False,
    )
```

```python
import functools

import jax
import jax.numpy as jnp
from jax import lax
from jax.experimental import pallas as pl
from jax.experimental.pallas import tpu as pltpu
from jax.sharding import PartitionSpec as P

mach_number = 0.5
tau = 0.05
filter_weight = 0.25
IN_P, IN_U, IN_V, IN_W = 8, 8, 10, 8
SLOTS = 19
OUT_P, OUT_U, OUT_V, OUT_W = 14, 10, 12, 10
AXES = ("section", "stream", "slab")
LEFT = ("e1", "ta", "m1", "m2", "e2", "a", "e4", "e6", "e8", "fx")
RIGHT = ("c", "cc", "fz")
f32, bf16 = jnp.float32, jnp.bfloat16


def call(body, out_shape, *args, flops=0, scratch=()):
    moved = sum(a.size * a.dtype.itemsize for a in args)
    return pl.pallas_call(
        body,
        out_shape=out_shape,
        scratch_shapes=scratch,
        compiler_params=pltpu.CompilerParams(vmem_limit_bytes=40 * 2**20),
        cost_estimate=pl.CostEstimate(flops=flops, bytes_accessed=moved, transcendentals=0),
    )(*args)


def order_of(count):
    places = []
    for j in range(count):
        step, rung = j // 2, j % 2
        x, y = (rung, step) if step < 4 else (3 - rung, 7 - step)
        places.append(4 * x + y)
    return places


def halves(value):
    high = value.astype(bf16)
    return high, (value - high.astype(f32)).astype(bf16)


def left_form(matrix):
    high, low = halves(matrix)
    return jnp.concatenate([high, high, low], axis=1)


def right_form(matrix):
    high, low = halves(matrix)
    return jnp.concatenate([high, high, low], axis=0)


def times_left(form, planes):
    high, low = halves(jnp.concatenate(planes, axis=1))
    out = jnp.dot(form, jnp.concatenate([high, low, high], axis=0), preferred_element_type=f32)
    width = planes[0].shape[1]
    return [out[:, i * width : (i + 1) * width] for i in range(len(planes))]


def times_right(planes, form):
    high, low = halves(jnp.concatenate(planes, axis=0))
    out = jnp.dot(jnp.concatenate([high, low, high], axis=1), form, preferred_element_type=f32)
    length = planes[0].shape[0]
    return [out[i * length : (i + 1) * length] for i in range(len(planes))]


def prepare_kernel(dx_ref, dzt_ref, fx_ref, fzt_ref, left_ref, right_ref):
    def dot(one, two):
        return jnp.dot(one, two, precision=lax.Precision.HIGHEST, preferred_element_type=f32)

    dx, dzt = dx_ref[...], dzt_ref[...]
    square = dot(dx, dx)
    e1 = -tau * mach_number * dx
    e2 = 2.0 * e1 + (tau * mach_number) ** 2 * square
    e4 = 2.0 * e2 + dot(e2, e2)
    values = {
        "e1": e1,
        "ta": -tau * dx,
        "m1": 2.0 * e1,
        "m2": tau**2 * square - e2,
        "e2": e2,
        "a": dx,
        "e4": e4,
        "e6": e2 + e4 + dot(e2, e4),
        "e8": 2.0 * e4 + dot(e4, e4),
        "fx": filter_weight * fx_ref[...],
    }
    for i, name in enumerate(LEFT):
        left_ref[i] = left_form(values[name])
    others = {"c": dzt, "cc": tau**2 * dot(dzt, dzt), "fz": filter_weight * fzt_ref[...]}
    for i, name in enumerate(RIGHT):
        right_ref[i] = right_form(others[name])


class Products:
    def __init__(self, left_ref, right_ref):
        self.left_ref, self.right_ref = left_ref, right_ref

    def left(self, name, planes):
        return times_left(self.left_ref[LEFT.index(name)], planes)

    def right(self, planes, name):
        return times_right(planes, self.right_ref[RIGHT.index(name)])


def inside(value, reach, low_ok, high_ok):
    rows = value.shape[0]
    return jnp.concatenate(
        [value[:reach] * low_ok, value[reach : rows - reach], value[rows - reach :] * high_ok], axis=0
    )


def shift_rows(value, steps):
    zeros = jnp.zeros((abs(steps),) + value.shape[1:], f32)
    if steps > 0:
        return jnp.concatenate([value[steps:], zeros], axis=0)
    return jnp.concatenate([zeros, value[:steps]], axis=0)


def slope4(value):
    near = shift_rows(value, 1) - shift_rows(value, -1)
    far = shift_rows(value, 2) - shift_rows(value, -2)
    return (2.0 / 3.0) * near - (1.0 / 12.0) * far


def spread_kernel(edge_ref, raw_ref, low_ref, high_ref, right_ref, out_ref):
    low_ok, high_ok = edge_ref[0], edge_ref[1]
    own, xs, nz = raw_ref.shape[1:]
    order = order_of(own)
    ext = []
    lead = 0
    for i, reach in enumerate((IN_P, IN_U, IN_V, IN_W)):
        ext.append(
            jnp.concatenate([low_ref[lead : lead + reach], raw_ref[i], high_ref[lead : lead + reach]], axis=0)
        )
        lead += reach

    def twice(value):
        once = inside(slope4(value), IN_P, low_ok, high_ok)
        return inside(slope4(once), IN_P, low_ok, high_ok)

    def put(place, value):
        reach = (value.shape[0] - own) // 2
        for j in range(own):
            out_ref[order[j], place] = value[reach + j]

    def slope2(value):
        return 0.5 * (value[IN_P + 1 : IN_P + 1 + own] - value[IN_P - 1 : IN_P - 1 + own])

    rows = ext[3].shape[0]
    through = times_right([ext[3].reshape(rows * xs, nz)], right_ref[RIGHT.index("c")])[0]
    cut = IN_V - IN_W
    rate = through.reshape(rows, xs, nz) + slope4(ext[2])[cut : cut + rows]
    rate = inside(rate, IN_W, low_ok, high_ok)
    for place, value in ((0, ext[0]), (3, ext[1]), (6, rate)):
        put(place, value)
        value = twice(value)
        put(place + 1, value)
        put(place + 2, twice(value))
    put(9, raw_ref[2])
    put(10, raw_ref[3])
    put(11, slope2(ext[1]))
    put(12, slope2(ext[3]))


class Raiser:
    def __init__(self, edge_ref, back_ref):
        self.low_ok, self.high_ok = edge_ref[0], edge_ref[1]
        self.back_ref = back_ref
        self.own = back_ref.shape[0]
        self.order = order_of(self.own)

    def load(self, slot):
        return jnp.stack([self.back_ref[self.order[j], slot] for j in range(self.own)])

    def total(self, fields):
        total = fields[-1]
        for value in fields[-2::-1]:
            edge = (total.shape[0] - self.own) // 2 + 2
            zeros = jnp.zeros((2,) + total.shape[1:], f32)
            total = slope4(jnp.concatenate([zeros, total, zeros], axis=0))
            centre = total[edge : edge + self.own]
            if value is not None:
                centre = centre + value
            total = jnp.concatenate(
                [total[:edge] * self.low_ok, centre, total[edge + self.own :] * self.high_ok], axis=0
            )
        return total


def gather_odd_kernel(edge_ref, back_ref, out_ref):
    @pl.when(edge_ref[2] > 0)
    def _():
        raiser = Raiser(edge_ref, back_ref)
        p = [raiser.load(10 + i) for i in range(4)]
        u = [raiser.load(14 + i) for i in range(3)]
        lead = 0
        for value in (
            raiser.total([None, p[0], None, p[1], None, p[2], None, p[3]]),
            raiser.total([None, u[0], None, u[1], None, u[2]]),
            raiser.total([None, raiser.load(17)]),
        ):
            out_ref[lead : lead + value.shape[0]] = value
            lead += value.shape[0]


def gather_kernel(edge_ref, back_ref, own_ref, high_ref, low_ref):
    raiser = Raiser(edge_ref, back_ref)
    own = raiser.own
    sound = 1.0 - edge_ref[2]

    def extra(i):
        return sound * raiser.load(10 + i)

    p = [raiser.load(0), None, raiser.load(1), None, raiser.load(2), None, extra(0)]
    u = [raiser.load(3), None, raiser.load(4), None, extra(1)]
    w = [raiser.load(5), None, raiser.load(6), extra(4), extra(2), extra(5)]
    v = [raiser.load(7), raiser.load(8), extra(6), raiser.load(9), extra(7), extra(3), extra(8)]
    place = 0
    for output, (fields, room) in enumerate(((p, OUT_P), (u, OUT_U), (v, OUT_V), (w, OUT_W))):
        total = raiser.total(fields)
        reach = 2 * (len(fields) - 1)
        own_ref[output] = total[reach : reach + own]
        if room > reach:
            low_ref[place : place + room - reach] = jnp.zeros((room - reach,) + total.shape[1:], f32)
            high_ref[place + reach : place + room] = jnp.zeros((room - reach,) + total.shape[1:], f32)
        low_ref[place + room - reach : place + room] = total[:reach]
        high_ref[place : place + reach] = total[reach + own :]
        place += room


def plane(ref, index):
    blocks, _, xs, nz = ref.shape
    return ref[:, index].reshape(blocks * xs, nz)


def waves_kernel(in_ref, left_ref, right_ref, out_ref):
    do = Products(left_ref, right_ref)
    p0 = [plane(in_ref, i) for i in range(3)]
    u0 = [plane(in_ref, 3 + i) for i in range(3)]

    def advance(now, before):
        count = len(before) - 1
        one = do.left("m1", now[:count])
        two = do.left("m2", before[:count])
        three = do.right(before[:count], "cc")
        return [
            2.0 * now[i] - before[i] + (one[i] + two[i] + three[i] + tau**2 * before[i + 1])
            for i in range(count)
        ]

    moved = do.left("e1", p0)
    driven = do.left("ta", u0)
    p1 = [p0[i] + (moved[i] + driven[i] - tau * plane(in_ref, 6 + i)) for i in range(3)]
    h2 = p0[0] + moved[0] + p1[0]
    out_ref[2] = h2
    p2 = advance(p1, p0)
    p3 = advance(p2, p1)
    h4 = h2 + do.left("e2", [h2])[0] + p2[0] + do.left("e1", p2[:1])[0] + p3[0]
    out_ref[3] = h4
    p4 = advance(p3, p2)
    p5 = advance(p4, p3)
    h6 = h4 + do.left("e2", [h4])[0] + p4[0] + do.left("e1", p4)[0] + p5[0]
    out_ref[0] = p4[0]
    out_ref[1] = p5[0]
    out_ref[4] = h6


def held_kernel(in_ref, waves_ref, left_ref, right_ref, out_ref):
    do = Products(left_ref, right_ref)
    start = [plane(in_ref, i) for i in (3, 10, 11, 12, 9)]
    h = [waves_ref[2 + n] for n in range(3)]
    pull_x = do.left("a", h)
    pull_z = do.right(h, "c")
    for n, growth in enumerate(("e2", "e4", "e6")):
        change = do.left(growth, start)
        out_ref[n, 0] = start[0] + change[0] - tau * pull_x[n]
        out_ref[n, 1] = start[1] + change[1] - tau * pull_z[n]
        for k in (2, 3, 4):
            out_ref[n, k] = start[k] + change[k]


def source_kernel(region_ref, in_ref, held_ref, up1_ref, down1_ref, up2_ref, down2_ref, left_ref, right_ref, out_ref):
    do = Products(left_ref, right_ref)
    nx, nz = up1_ref.shape[1:]
    row = lax.broadcasted_iota(jnp.int32, (nx, nz), 0)
    lane = lax.broadcasted_iota(jnp.int32, (nx, nz), 1)
    region = region_ref[...]

    def slope_x(value):
        ahead = jnp.where(row == nx - 1, 0.0, pltpu.roll(value, nx - 1, 0))
        behind = jnp.where(row == 0, 0.0, pltpu.roll(value, 1, 0))
        return 0.5 * (ahead - behind)

    def slope_z(value):
        ahead = jnp.where(lane == nz - 1, 0.0, pltpu.roll(value, nz - 1, 1))
        behind = jnp.where(lane == 0, 0.0, pltpu.roll(value, 1, 1))
        return 0.5 * (ahead - behind)

    near = [up1_ref[n] - down1_ref[n] for n in range(3)]
    half = [0.5 * value for value in near]
    pull_x = do.left("a", half)
    pull_z = do.right(half, "c")
    for n in range(4):
        if n == 0:
            u, w, slope_u, slope_w, v = [plane(in_ref, i) for i in (3, 10, 11, 12, 9)]
        else:
            u, w = held_ref[n - 1, 0], held_ref[n - 1, 1]
            slope_u = held_ref[n - 1, 2] - tau * pull_x[n - 1]
            slope_w = held_ref[n - 1, 3] - tau * pull_z[n - 1]
            far = up2_ref[n - 1] - down2_ref[n - 1]
            v = held_ref[n - 1, 4] - tau * ((2.0 / 3.0) * near[n - 1] - (1.0 / 12.0) * far)
        o_x = slope_w - slope_z(v)
        o_y = slope_z(u) - slope_x(w)
        o_z = slope_x(v) - slope_u
        out_ref[n, 0] = region * (o_z * v - o_y * w)
        out_ref[n, 1] = region * (o_x * w - o_z * u)
        out_ref[n, 2] = region * (o_y * u - o_x * v)


class Chain:
    def __init__(self, left_ref, right_ref):
        self.do = Products(left_ref, right_ref)

    def advance(self, now, before, drive, count):
        m_now = self.do.left("m1", now)
        m_before = self.do.left("m2", before)
        c_before = self.do.right(before, "cc")
        out = []
        for k in range(count):
            terms = []
            if k < len(now):
                terms.append(2.0 * now[k] + m_now[k])
            if k < len(before):
                terms.append(m_before[k] + c_before[k] - before[k])
            if 0 <= k - 2 < len(before):
                terms.append(tau**2 * before[k - 2])
            if k < len(drive):
                terms.append(drive[k])
            out.append(functools.reduce(lambda one, two: one + two, terms))
        return out

    def grow(self, sums, before, now):
        moved = self.do.left("e1", before)
        kept = self.do.left("e2", sums) if sums else []
        out = [before[k] + moved[k] + now[k] for k in range(len(now))]
        return [out[k] + (sums[k] + kept[k]) if k < len(sums) else out[k] for k in range(len(now))]


def drives(do, flag_ref, own_ref, source_ref, first, last):
    flow = flag_ref[2] > 0
    one = do.left("a", [source_ref[n, 0] for n in range(first, last)])
    two = do.right([source_ref[n, 2] for n in range(first, last)], "c")
    return [
        (
            -(tau**2) * (one[n - first] + two[n - first]),
            -(tau**2) * jnp.where(flow, own_ref[n, 1], source_ref[n, 1]),
        )
        for n in range(first, last)
    ]


def driven_kernel(flag_ref, waves_ref, own_ref, source_ref, left_ref, right_ref, out_ref):
    chain = Chain(left_ref, right_ref)
    drive = drives(chain.do, flag_ref, own_ref, source_ref, 0, 2)
    q2 = list(drive[0])
    moved = chain.do.left("m1", q2)
    q3 = [2.0 * q2[k] + moved[k] + drive[0][k] for k in range(2)]
    g4 = chain.grow([], q2, q3)
    q4 = chain.advance(q3, q2, drive[1], 4)
    q5 = chain.advance(q4, q3, drive[1], 4)
    g6 = chain.grow(g4, q4, q5)
    for first, values, wave in ((0, q4, 0), (4, q5, 1), (8, g6, 4)):
        out_ref[first] = values[0] + waves_ref[wave]
        for k in range(1, 4):
            out_ref[first + k] = values[k]


def finish_kernel(flag_ref, in_ref, driven_ref, own_ref, source_ref, left_ref, right_ref, out_ref):
    chain = Chain(left_ref, right_ref)
    do = chain.do
    drive = drives(do, flag_ref, own_ref, source_ref, 2, 4)
    q4, q5, g6 = [[driven_ref[first + k] for k in range(4)] for first in (0, 4, 8)]
    q6 = chain.advance(q5, q4, drive[0], 6)
    q7 = chain.advance(q6, q5, drive[0], 6)
    for k, value in enumerate(chain.grow(g6, q6, q7)):
        out_ref[8 + k] = value
    for k, value in enumerate(chain.advance(q7, q6, drive[1], 8)):
        out_ref[k] = value
    total = [source_ref[0, k] for k in range(3)]
    for n in (1, 2, 3):
        kept = do.left("e2", total)
        total = [total[k] + kept[k] + source_ref[n, k] for k in range(3)]
    moved = do.left("e1", total)
    begin = [plane(in_ref, i) for i in (3, 9, 10)]
    kept = do.left("e8", begin)
    for i in range(3):
        out_ref[14 + i] = begin[i] + kept[i] + tau * (2.0 * total[i] + moved[i])


def filter_kernel(flag_ref, last_ref, left_ref, right_ref, out_ref):
    do = Products(left_ref, right_ref)
    blocks, _, xs, nz = out_ref.shape

    def emit(place, values):
        fx, fz = do.left("fx", values), do.right(values, "fz")
        for i, value in enumerate(values):
            out_ref[:, place + i] = (value + fx[i] + fz[i]).reshape(blocks, xs, nz)

    def p(k):
        return last_ref[k]

    def h(k):
        return last_ref[8 + k]

    def third(*which):
        return [-tau * value for value in do.right([h(k) for k in which], "c")]

    axial = do.left("ta", [h(0), h(2)])
    depth = third(0, 2)
    emit(0, [p(0), p(2), p(4), last_ref[14] + axial[0], axial[1], last_ref[16] + depth[0], depth[1]])
    emit(7, [last_ref[15], -tau * h(0), -tau * h(2)])

    @pl.when(flag_ref[2] > 0)
    def _():
        axial = do.left("ta", [h(1), h(3), h(5)])
        emit(10, [p(1), p(3), p(5), p(7)] + axial + third(1))
        out_ref[:, 18] = jnp.zeros((blocks, xs, nz), f32)

    @pl.when(flag_ref[2] <= 0)
    def _():
        axial = do.left("ta", [h(4)])
        depth = third(4, 3, 5)
        emit(10, [p(6), axial[0], depth[0], -tau * h(4), depth[1], depth[2]])
        emit(16, [-tau * h(1), -tau * h(3), -tau * h(5)])


def along_y(steps):
    streams, slabs = lax.axis_size("stream"), lax.axis_size("slab")
    count = streams * slabs
    order = order_of(streams)

    def device(y):
        return order[y % streams] * slabs + y // streams

    return [(device(y), device(y + steps)) for y in range(max(0, -steps), min(count, count - steps))]


def shards(state, source_mask, deriv_x, deriv_z, filter_x, filter_z):
    _, _, xs, own, nz = state.shape
    slabs, streams = lax.axis_size("slab"), lax.axis_size("stream")
    slab = lax.axis_index("slab")
    nx = xs * streams
    upward = [(i, i + 1) for i in range(slabs - 1)]
    downward = [(i + 1, i) for i in range(slabs - 1)]
    edges = jnp.stack(
        [slab > 0, slab < slabs - 1, lax.axis_index("section") == 0]
    ).astype(f32)
    region = jnp.repeat(source_mask[:, 0].astype(f32), nx // source_mask.shape[0])
    region = jnp.broadcast_to(region[:, None], (nx, nz))

    raw = jnp.swapaxes(state[0], 1, 2)
    reaches = (IN_P, IN_U, IN_V, IN_W)
    from_low = lax.ppermute(
        jnp.concatenate([raw[i, own - reach :] for i, reach in enumerate(reaches)]), "slab", upward
    )
    from_high = lax.ppermute(
        jnp.concatenate([raw[i, :reach] for i, reach in enumerate(reaches)]), "slab", downward
    )
    left, right = call(
        prepare_kernel,
        (
            jax.ShapeDtypeStruct((len(LEFT), nx, 3 * nx), bf16),
            jax.ShapeDtypeStruct((len(RIGHT), 3 * nz, nz), bf16),
        ),
        deriv_x,
        deriv_z.T,
        filter_x,
        filter_z.T,
        flops=10**9,
    )

    def shape(*dims):
        return jax.ShapeDtypeStruct(dims, f32)

    def with_edges(body, out_shape, *args):
        return pl.pallas_call(
            body,
            out_shape=out_shape,
            in_specs=[pl.BlockSpec(memory_space=pltpu.SMEM)]
            + [pl.BlockSpec(memory_space=pltpu.VMEM)] * len(args),
            compiler_params=pltpu.CompilerParams(vmem_limit_bytes=40 * 2**20),
        )(edges, *args)

    spread = with_edges(spread_kernel, shape(own, 13, xs, nz), raw, from_low, from_high, right)
    planes = lax.all_to_all(spread, "stream", split_axis=0, concat_axis=0, tiled=True)
    waves = call(waves_kernel, shape(5, nx, nz), planes, left, right, flops=2 * 10**9)
    sums = waves[2:5]
    near = [lax.ppermute(sums, AXES, along_y(steps)) for steps in (-1, 1, -2, 2)]
    held = call(held_kernel, shape(3, 5, nx, nz), planes, waves, left, right, flops=10**9)
    source = call(
        source_kernel, shape(4, 3, nx, nz), region, planes, held, *near, left, right, flops=10**9
    )
    moved = lax.ppermute(source, "section", [(0, 1)])
    driven = with_edges(driven_kernel, shape(12, nx, nz), waves, source, moved, left, right)
    last = with_edges(finish_kernel, shape(17, nx, nz), planes, driven, source, moved, left, right)
    done = with_edges(filter_kernel, shape(streams, SLOTS, xs, nz), last, left, right)
    back = lax.all_to_all(done, "stream", split_axis=0, concat_axis=0, tiled=True)
    border = OUT_P + OUT_U + OUT_V + OUT_W
    rows = ((OUT_P, 0), (OUT_U, 1), (2, 3))
    odd = with_edges(gather_odd_kernel, shape(sum(own + 2 * reach for reach, _ in rows), xs, nz), back)
    odd = lax.ppermute(odd, "section", [(0, 1)])
    mine, high, low = with_edges(
        gather_kernel, (shape(4, own, xs, nz), shape(border, xs, nz), shape(border, xs, nz)), back
    )
    starts = (0, OUT_P, OUT_P + OUT_U, OUT_P + OUT_U + OUT_V)
    reaches = (OUT_P, OUT_U, OUT_V, OUT_W)
    lead = 0
    more_high, more_low, more_own = [], [], [jnp.zeros((own, xs, nz), f32)] * 4
    for reach, output in rows:
        part = odd[lead : lead + own + 2 * reach]
        start, room = starts[output], reaches[output]
        more_low.append(jnp.pad(part[:reach], ((start + room - reach, border - start - room), (0, 0), (0, 0))))
        more_high.append(jnp.pad(part[reach + own :], ((start, border - start - reach), (0, 0), (0, 0))))
        more_own[output] = part[reach : reach + own]
        lead += own + 2 * reach
    from_low = lax.ppermute(high + sum(more_high), "slab", upward)
    from_high = lax.ppermute(low + sum(more_low), "slab", downward)
    outs = []
    for i, (start, reach) in enumerate(zip(starts, reaches)):
        from_below = jnp.pad(from_low[start : start + reach], ((0, own - reach), (0, 0), (0, 0)))
        from_above = jnp.pad(from_high[start : start + reach], ((own - reach, 0), (0, 0), (0, 0)))
        outs.append(mine[i] + more_own[i] + from_below + from_above)
    return jnp.swapaxes(jnp.stack(outs), 1, 2)[None]


def solution(mesh):
    placed = (P("section", None, "stream", "slab", None), P(None, "slab"), P(), P(), P(), P())
    return jax.shard_map(
        shards,
        mesh=mesh,
        in_specs=placed,
        out_specs=P("section", None, "stream", "slab", None),
        check_vma=False,
    )
```

```python
import functools

import jax
import jax.numpy as jnp
from jax import lax
from jax.experimental import pallas as pl
from jax.experimental.pallas import tpu as pltpu
from jax.sharding import PartitionSpec as P

mach_number = 0.5
tau = 0.05
filter_weight = 0.25
IN_P, IN_U, IN_V, IN_W = 8, 8, 10, 8
SLOTS = 19
OUT_P, OUT_U, OUT_V, OUT_W = 14, 10, 12, 10
AXES = ("section", "stream", "slab")
LEFT = ("e1", "ta", "m1", "m2", "e2", "a", "e4", "e6", "e8", "fx")
RIGHT = ("c", "cc", "fz")
f32, bf16 = jnp.float32, jnp.bfloat16


def call(body, out_shape, *args, flops=0, scratch=()):
    moved = sum(a.size * a.dtype.itemsize for a in args)
    return pl.pallas_call(
        body,
        out_shape=out_shape,
        scratch_shapes=scratch,
        compiler_params=pltpu.CompilerParams(vmem_limit_bytes=40 * 2**20),
        cost_estimate=pl.CostEstimate(flops=flops, bytes_accessed=moved, transcendentals=0),
    )(*args)


def order_of(count):
    places = []
    for j in range(count):
        step, rung = j // 2, j % 2
        x, y = (rung, step) if step < 4 else (3 - rung, 7 - step)
        places.append(4 * x + y)
    return places


def halves(value):
    high = value.astype(bf16)
    return high, (value - high.astype(f32)).astype(bf16)


def left_form(matrix):
    high, low = halves(matrix)
    return jnp.concatenate([high, high, low], axis=1)


def right_form(matrix):
    high, low = halves(matrix)
    return jnp.concatenate([high, high, low], axis=0)


def times_left(form, planes):
    high, low = halves(jnp.concatenate(planes, axis=1))
    out = jnp.dot(form, jnp.concatenate([high, low, high], axis=0), preferred_element_type=f32)
    width = planes[0].shape[1]
    return [out[:, i * width : (i + 1) * width] for i in range(len(planes))]


def times_right(planes, form):
    high, low = halves(jnp.concatenate(planes, axis=0))
    out = jnp.dot(jnp.concatenate([high, low, high], axis=1), form, preferred_element_type=f32)
    length = planes[0].shape[0]
    return [out[i * length : (i + 1) * length] for i in range(len(planes))]


def prepare_kernel(dx_ref, dzt_ref, fx_ref, fzt_ref, left_ref, right_ref):
    def dot(one, two):
        return jnp.dot(one, two, precision=lax.Precision.HIGHEST, preferred_element_type=f32)

    dx, dzt = dx_ref[...], dzt_ref[...]
    square = dot(dx, dx)
    e1 = -tau * mach_number * dx
    e2 = 2.0 * e1 + (tau * mach_number) ** 2 * square
    e4 = 2.0 * e2 + dot(e2, e2)
    values = {
        "e1": e1,
        "ta": -tau * dx,
        "m1": 2.0 * e1,
        "m2": tau**2 * square - e2,
        "e2": e2,
        "a": dx,
        "e4": e4,
        "e6": e2 + e4 + dot(e2, e4),
        "e8": 2.0 * e4 + dot(e4, e4),
        "fx": filter_weight * fx_ref[...],
    }
    for i, name in enumerate(LEFT):
        left_ref[i] = left_form(values[name])
    others = {"c": dzt, "cc": tau**2 * dot(dzt, dzt), "fz": filter_weight * fzt_ref[...]}
    for i, name in enumerate(RIGHT):
        right_ref[i] = right_form(others[name])


class Products:
    def __init__(self, left_ref, right_ref):
        self.left_ref, self.right_ref = left_ref, right_ref

    def left(self, name, planes):
        return times_left(self.left_ref[LEFT.index(name)], planes)

    def right(self, planes, name):
        return times_right(planes, self.right_ref[RIGHT.index(name)])


def inside(value, reach, low_ok, high_ok):
    rows = value.shape[0]
    return jnp.concatenate(
        [value[:reach] * low_ok, value[reach : rows - reach], value[rows - reach :] * high_ok], axis=0
    )


def shift_rows(value, steps):
    zeros = jnp.zeros((abs(steps),) + value.shape[1:], f32)
    if steps > 0:
        return jnp.concatenate([value[steps:], zeros], axis=0)
    return jnp.concatenate([zeros, value[:steps]], axis=0)


def slope4(value):
    near = shift_rows(value, 1) - shift_rows(value, -1)
    far = shift_rows(value, 2) - shift_rows(value, -2)
    return (2.0 / 3.0) * near - (1.0 / 12.0) * far


def spread_kernel(edge_ref, raw_ref, low_ref, high_ref, right_ref, out_ref):
    low_ok, high_ok = edge_ref[0], edge_ref[1]
    own, xs, nz = raw_ref.shape[1:]
    order = order_of(own)
    ext = []
    lead = 0
    for i, reach in enumerate((IN_P, IN_U, IN_V, IN_W)):
        ext.append(
            jnp.concatenate(
                [low_ref[lead : lead + reach] * low_ok, raw_ref[i], high_ref[lead : lead + reach] * high_ok],
                axis=0,
            )
        )
        lead += reach

    def twice(value):
        once = inside(slope4(value), IN_P, low_ok, high_ok)
        return inside(slope4(once), IN_P, low_ok, high_ok)

    def put(place, value):
        reach = (value.shape[0] - own) // 2
        for j in range(own):
            out_ref[order[j], place] = value[reach + j]

    def slope2(value):
        return 0.5 * (value[IN_P + 1 : IN_P + 1 + own] - value[IN_P - 1 : IN_P - 1 + own])

    rows = ext[3].shape[0]
    through = times_right([ext[3].reshape(rows * xs, nz)], right_ref[RIGHT.index("c")])[0]
    cut = IN_V - IN_W
    rate = through.reshape(rows, xs, nz) + slope4(ext[2])[cut : cut + rows]
    rate = inside(rate, IN_W, low_ok, high_ok)
    for place, value in ((0, ext[0]), (3, ext[1]), (6, rate)):
        put(place, value)
        value = twice(value)
        put(place + 1, value)
        put(place + 2, twice(value))
    put(9, raw_ref[2])
    put(10, raw_ref[3])
    put(11, slope2(ext[1]))
    put(12, slope2(ext[3]))


class Raiser:
    def __init__(self, edge_ref, back_ref):
        self.low_ok, self.high_ok = edge_ref[0], edge_ref[1]
        self.back_ref = back_ref
        self.own = back_ref.shape[0]
        self.order = order_of(self.own)

    def load(self, slot):
        return jnp.stack([self.back_ref[self.order[j], slot] for j in range(self.own)])

    def total(self, fields):
        total = fields[-1]
        for value in fields[-2::-1]:
            edge = (total.shape[0] - self.own) // 2 + 2
            zeros = jnp.zeros((2,) + total.shape[1:], f32)
            total = slope4(jnp.concatenate([zeros, total, zeros], axis=0))
            centre = total[edge : edge + self.own]
            if value is not None:
                centre = centre + value
            total = jnp.concatenate(
                [total[:edge] * self.low_ok, centre, total[edge + self.own :] * self.high_ok], axis=0
            )
        return total


def gather_odd_kernel(edge_ref, back_ref, out_ref):
    @pl.when(edge_ref[2] > 0)
    def _():
        raiser = Raiser(edge_ref, back_ref)
        p = [raiser.load(10 + i) for i in range(4)]
        u = [raiser.load(14 + i) for i in range(3)]
        lead = 0
        for value in (
            raiser.total([None, p[0], None, p[1], None, p[2], None, p[3]]),
            raiser.total([None, u[0], None, u[1], None, u[2]]),
            raiser.total([None, raiser.load(17)]),
        ):
            out_ref[lead : lead + value.shape[0]] = value
            lead += value.shape[0]

    @pl.when(edge_ref[2] <= 0)
    def _():
        out_ref[...] = jnp.zeros(out_ref.shape, f32)


def gather_kernel(edge_ref, back_ref, own_ref, high_ref, low_ref):
    raiser = Raiser(edge_ref, back_ref)
    own = raiser.own
    sound = 1.0 - edge_ref[2]

    def extra(i):
        return sound * raiser.load(10 + i)

    p = [raiser.load(0), None, raiser.load(1), None, raiser.load(2), None, extra(0)]
    u = [raiser.load(3), None, raiser.load(4), None, extra(1)]
    w = [raiser.load(5), None, raiser.load(6), extra(4), extra(2), extra(5)]
    v = [raiser.load(7), raiser.load(8), extra(6), raiser.load(9), extra(7), extra(3), extra(8)]
    place = 0
    for output, (fields, room) in enumerate(((p, OUT_P), (u, OUT_U), (v, OUT_V), (w, OUT_W))):
        total = raiser.total(fields)
        reach = 2 * (len(fields) - 1)
        own_ref[output] = total[reach : reach + own]
        if room > reach:
            low_ref[place : place + room - reach] = jnp.zeros((room - reach,) + total.shape[1:], f32)
            high_ref[place + reach : place + room] = jnp.zeros((room - reach,) + total.shape[1:], f32)
        low_ref[place + room - reach : place + room] = total[:reach]
        high_ref[place : place + reach] = total[reach + own :]
        place += room


def plane(ref, index):
    blocks, _, xs, nz = ref.shape
    return ref[:, index].reshape(blocks * xs, nz)


def waves_kernel(in_ref, left_ref, right_ref, out_ref):
    do = Products(left_ref, right_ref)
    p0 = [plane(in_ref, i) for i in range(3)]
    u0 = [plane(in_ref, 3 + i) for i in range(3)]

    def advance(now, before):
        count = len(before) - 1
        one = do.left("m1", now[:count])
        two = do.left("m2", before[:count])
        three = do.right(before[:count], "cc")
        return [
            2.0 * now[i] - before[i] + (one[i] + two[i] + three[i] + tau**2 * before[i + 1])
            for i in range(count)
        ]

    moved = do.left("e1", p0)
    driven = do.left("ta", u0)
    p1 = [p0[i] + (moved[i] + driven[i] - tau * plane(in_ref, 6 + i)) for i in range(3)]
    h2 = p0[0] + moved[0] + p1[0]
    out_ref[2] = h2
    p2 = advance(p1, p0)
    p3 = advance(p2, p1)
    h4 = h2 + do.left("e2", [h2])[0] + p2[0] + do.left("e1", p2[:1])[0] + p3[0]
    out_ref[3] = h4
    p4 = advance(p3, p2)
    p5 = advance(p4, p3)
    h6 = h4 + do.left("e2", [h4])[0] + p4[0] + do.left("e1", p4)[0] + p5[0]
    out_ref[0] = p4[0]
    out_ref[1] = p5[0]
    out_ref[4] = h6


def held_kernel(in_ref, waves_ref, left_ref, right_ref, out_ref):
    do = Products(left_ref, right_ref)
    start = [plane(in_ref, i) for i in (3, 10, 11, 12, 9)]
    h = [waves_ref[2 + n] for n in range(3)]
    pull_x = do.left("a", h)
    pull_z = do.right(h, "c")
    for n, growth in enumerate(("e2", "e4", "e6")):
        change = do.left(growth, start)
        out_ref[n, 0] = start[0] + change[0] - tau * pull_x[n]
        out_ref[n, 1] = start[1] + change[1] - tau * pull_z[n]
        for k in (2, 3, 4):
            out_ref[n, k] = start[k] + change[k]


def source_kernel(flag_ref, region_ref, in_ref, held_ref, up1_ref, down1_ref, up2_ref, down2_ref, left_ref, right_ref, out_ref):
    do = Products(left_ref, right_ref)
    nx, nz = up1_ref.shape[1:]
    row = lax.broadcasted_iota(jnp.int32, (nx, nz), 0)
    lane = lax.broadcasted_iota(jnp.int32, (nx, nz), 1)
    region = region_ref[...]

    def slope_x(value):
        ahead = jnp.where(row == nx - 1, 0.0, pltpu.roll(value, nx - 1, 0))
        behind = jnp.where(row == 0, 0.0, pltpu.roll(value, 1, 0))
        return 0.5 * (ahead - behind)

    def slope_z(value):
        ahead = jnp.where(lane == nz - 1, 0.0, pltpu.roll(value, nz - 1, 1))
        behind = jnp.where(lane == 0, 0.0, pltpu.roll(value, 1, 1))
        return 0.5 * (ahead - behind)

    up1, down1, up2, down2 = flag_ref[3], flag_ref[4], flag_ref[5], flag_ref[6]
    near = [up1 * up1_ref[n] - down1 * down1_ref[n] for n in range(3)]
    half = [0.5 * value for value in near]
    pull_x = do.left("a", half)
    pull_z = do.right(half, "c")
    for n in range(4):
        if n == 0:
            u, w, slope_u, slope_w, v = [plane(in_ref, i) for i in (3, 10, 11, 12, 9)]
        else:
            u, w = held_ref[n - 1, 0], held_ref[n - 1, 1]
            slope_u = held_ref[n - 1, 2] - tau * pull_x[n - 1]
            slope_w = held_ref[n - 1, 3] - tau * pull_z[n - 1]
            far = up2 * up2_ref[n - 1] - down2 * down2_ref[n - 1]
            v = held_ref[n - 1, 4] - tau * ((2.0 / 3.0) * near[n - 1] - (1.0 / 12.0) * far)
        o_x = slope_w - slope_z(v)
        o_y = slope_z(u) - slope_x(w)
        o_z = slope_x(v) - slope_u
        out_ref[n, 0] = region * (o_z * v - o_y * w)
        out_ref[n, 1] = region * (o_x * w - o_z * u)
        out_ref[n, 2] = region * (o_y * u - o_x * v)


class Chain:
    def __init__(self, left_ref, right_ref):
        self.do = Products(left_ref, right_ref)

    def advance(self, now, before, drive, count):
        m_now = self.do.left("m1", now)
        m_before = self.do.left("m2", before)
        c_before = self.do.right(before, "cc")
        out = []
        for k in range(count):
            terms = []
            if k < len(now):
                terms.append(2.0 * now[k] + m_now[k])
            if k < len(before):
                terms.append(m_before[k] + c_before[k] - before[k])
            if 0 <= k - 2 < len(before):
                terms.append(tau**2 * before[k - 2])
            if k < len(drive):
                terms.append(drive[k])
            out.append(functools.reduce(lambda one, two: one + two, terms))
        return out

    def grow(self, sums, before, now):
        moved = self.do.left("e1", before)
        kept = self.do.left("e2", sums) if sums else []
        out = [before[k] + moved[k] + now[k] for k in range(len(now))]
        return [out[k] + (sums[k] + kept[k]) if k < len(sums) else out[k] for k in range(len(now))]


def drives(do, flag_ref, own_ref, source_ref, first, last):
    flow = flag_ref[2] > 0
    one = do.left("a", [source_ref[n, 0] for n in range(first, last)])
    two = do.right([source_ref[n, 2] for n in range(first, last)], "c")
    return [
        (
            jnp.where(flow, 0.0, -(tau**2) * (one[n - first] + two[n - first])),
            -(tau**2) * jnp.where(flow, own_ref[n, 1], source_ref[n, 1]),
        )
        for n in range(first, last)
    ]


def driven_kernel(flag_ref, waves_ref, own_ref, source_ref, left_ref, right_ref, out_ref):
    chain = Chain(left_ref, right_ref)
    drive = drives(chain.do, flag_ref, own_ref, source_ref, 0, 2)
    q2 = list(drive[0])
    moved = chain.do.left("m1", q2)
    q3 = [2.0 * q2[k] + moved[k] + drive[0][k] for k in range(2)]
    g4 = chain.grow([], q2, q3)
    q4 = chain.advance(q3, q2, drive[1], 4)
    q5 = chain.advance(q4, q3, drive[1], 4)
    g6 = chain.grow(g4, q4, q5)
    for first, values, wave in ((0, q4, 0), (4, q5, 1), (8, g6, 4)):
        out_ref[first] = values[0] + waves_ref[wave]
        for k in range(1, 4):
            out_ref[first + k] = values[k]


def finish_kernel(flag_ref, in_ref, driven_ref, own_ref, source_ref, left_ref, right_ref, out_ref):
    chain = Chain(left_ref, right_ref)
    do = chain.do
    drive = drives(do, flag_ref, own_ref, source_ref, 2, 4)
    q4, q5, g6 = [[driven_ref[first + k] for k in range(4)] for first in (0, 4, 8)]
    q6 = chain.advance(q5, q4, drive[0], 6)
    q7 = chain.advance(q6, q5, drive[0], 6)
    for k, value in enumerate(chain.grow(g6, q6, q7)):
        out_ref[8 + k] = value
    for k, value in enumerate(chain.advance(q7, q6, drive[1], 8)):
        out_ref[k] = value
    flow = flag_ref[2] > 0

    def arrived(n):
        return [jnp.where(flow, 0.0, source_ref[n, k]) for k in range(3)]

    total = arrived(0)
    for n in (1, 2, 3):
        kept = do.left("e2", total)
        fresh = arrived(n)
        total = [total[k] + kept[k] + fresh[k] for k in range(3)]
    moved = do.left("e1", total)
    begin = [plane(in_ref, i) for i in (3, 9, 10)]
    kept = do.left("e8", begin)
    for i in range(3):
        out_ref[14 + i] = begin[i] + kept[i] + tau * (2.0 * total[i] + moved[i])


def filter_kernel(flag_ref, last_ref, left_ref, right_ref, out_ref):
    do = Products(left_ref, right_ref)
    blocks, _, xs, nz = out_ref.shape

    def emit(place, values):
        fx, fz = do.left("fx", values), do.right(values, "fz")
        for i, value in enumerate(values):
            out_ref[:, place + i] = (value + fx[i] + fz[i]).reshape(blocks, xs, nz)

    def p(k):
        return last_ref[k]

    def h(k):
        return last_ref[8 + k]

    def third(*which):
        return [-tau * value for value in do.right([h(k) for k in which], "c")]

    axial = do.left("ta", [h(0), h(2)])
    depth = third(0, 2)
    emit(0, [p(0), p(2), p(4), last_ref[14] + axial[0], axial[1], last_ref[16] + depth[0], depth[1]])
    emit(7, [last_ref[15], -tau * h(0), -tau * h(2)])

    @pl.when(flag_ref[2] > 0)
    def _():
        axial = do.left("ta", [h(1), h(3), h(5)])
        emit(10, [p(1), p(3), p(5), p(7)] + axial + third(1))
        out_ref[:, 18] = jnp.zeros((blocks, xs, nz), f32)

    @pl.when(flag_ref[2] <= 0)
    def _():
        axial = do.left("ta", [h(4)])
        depth = third(4, 3, 5)
        emit(10, [p(6), axial[0], depth[0], -tau * h(4), depth[1], depth[2]])
        emit(16, [-tau * h(1), -tau * h(3), -tau * h(5)])


def along_y(steps):
    streams, slabs = lax.axis_size("stream"), lax.axis_size("slab")
    count = streams * slabs
    order = order_of(streams)

    def device(y):
        return order[y % streams] * slabs + y // streams

    flow = [(device(y), device((y + steps) % count)) for y in range(count)]
    return flow + [(i, i) for i in range(count, count * lax.axis_size("section"))]


def shards(state, source_mask, deriv_x, deriv_z, filter_x, filter_z):
    _, _, xs, own, nz = state.shape
    slabs, streams = lax.axis_size("slab"), lax.axis_size("stream")
    slab = lax.axis_index("slab")
    nx = xs * streams
    upward = [(i, (i + 1) % slabs) for i in range(slabs)]
    downward = [((i + 1) % slabs, i) for i in range(slabs)]
    swap = [(0, 1), (1, 0)]
    inverse = [0] * streams
    for j, stream in enumerate(order_of(streams)):
        inverse[stream] = j
    y = slab * streams + jnp.asarray(inverse, jnp.int32)[lax.axis_index("stream")]
    last_y = slabs * streams - 1
    edges = jnp.stack(
        [slab > 0, slab < slabs - 1, lax.axis_index("section") == 0]
        + [y < last_y, y > 0, y < last_y - 1, y > 1]
    ).astype(f32)
    region = jnp.repeat(source_mask[:, 0].astype(f32), nx // source_mask.shape[0])
    region = jnp.broadcast_to(region[:, None], (nx, nz))

    raw = jnp.swapaxes(state[0], 1, 2)
    reaches = (IN_P, IN_U, IN_V, IN_W)
    from_low = lax.ppermute(
        jnp.concatenate([raw[i, own - reach :] for i, reach in enumerate(reaches)]), "slab", upward
    )
    from_high = lax.ppermute(
        jnp.concatenate([raw[i, :reach] for i, reach in enumerate(reaches)]), "slab", downward
    )
    left, right = call(
        prepare_kernel,
        (
            jax.ShapeDtypeStruct((len(LEFT), nx, 3 * nx), bf16),
            jax.ShapeDtypeStruct((len(RIGHT), 3 * nz, nz), bf16),
        ),
        deriv_x,
        deriv_z.T,
        filter_x,
        filter_z.T,
        flops=10**9,
    )

    def shape(*dims):
        return jax.ShapeDtypeStruct(dims, f32)

    def with_edges(body, out_shape, *args):
        return pl.pallas_call(
            body,
            out_shape=out_shape,
            in_specs=[pl.BlockSpec(memory_space=pltpu.SMEM)]
            + [pl.BlockSpec(memory_space=pltpu.VMEM)] * len(args),
            compiler_params=pltpu.CompilerParams(vmem_limit_bytes=40 * 2**20),
        )(edges, *args)

    spread = with_edges(spread_kernel, shape(own, 13, xs, nz), raw, from_low, from_high, right)
    planes = lax.all_to_all(spread, "stream", split_axis=0, concat_axis=0, tiled=True)
    waves = call(waves_kernel, shape(5, nx, nz), planes, left, right, flops=2 * 10**9)
    sums = waves[2:5]
    near = [lax.ppermute(sums, AXES, along_y(steps)) for steps in (-1, 1, -2, 2)]
    held = call(held_kernel, shape(3, 5, nx, nz), planes, waves, left, right, flops=10**9)
    source = with_edges(
        source_kernel, shape(4, 3, nx, nz), region, planes, held, *near, left, right
    )
    moved = lax.ppermute(source, "section", swap)
    driven = with_edges(driven_kernel, shape(12, nx, nz), waves, source, moved, left, right)
    last = with_edges(finish_kernel, shape(17, nx, nz), planes, driven, source, moved, left, right)
    done = with_edges(filter_kernel, shape(streams, SLOTS, xs, nz), last, left, right)
    back = lax.all_to_all(done, "stream", split_axis=0, concat_axis=0, tiled=True)
    border = OUT_P + OUT_U + OUT_V + OUT_W
    rows = ((OUT_P, 0), (OUT_U, 1), (2, 3))
    odd = with_edges(gather_odd_kernel, shape(sum(own + 2 * reach for reach, _ in rows), xs, nz), back)
    odd = lax.ppermute(odd, "section", swap)
    mine, high, low = with_edges(
        gather_kernel, (shape(4, own, xs, nz), shape(border, xs, nz), shape(border, xs, nz)), back
    )
    starts = (0, OUT_P, OUT_P + OUT_U, OUT_P + OUT_U + OUT_V)
    reaches = (OUT_P, OUT_U, OUT_V, OUT_W)
    lead = 0
    more_high, more_low, more_own = [], [], [jnp.zeros((own, xs, nz), f32)] * 4
    for reach, output in rows:
        part = odd[lead : lead + own + 2 * reach]
        start, room = starts[output], reaches[output]
        more_low.append(jnp.pad(part[:reach], ((start + room - reach, border - start - room), (0, 0), (0, 0))))
        more_high.append(jnp.pad(part[reach + own :], ((start, border - start - reach), (0, 0), (0, 0))))
        more_own[output] = part[reach : reach + own]
        lead += own + 2 * reach
    from_low = lax.ppermute(high + sum(more_high), "slab", upward)
    from_high = lax.ppermute(low + sum(more_low), "slab", downward)
    outs = []
    for i, (start, reach) in enumerate(zip(starts, reaches)):
        from_below = jnp.pad(from_low[start : start + reach], ((0, own - reach), (0, 0), (0, 0)))
        from_above = jnp.pad(from_high[start : start + reach], ((own - reach, 0), (0, 0), (0, 0)))
        outs.append(mine[i] + more_own[i] + from_below + from_above)
    return jnp.swapaxes(jnp.stack(outs), 1, 2)[None]


def solution(mesh):
    placed = (P("section", None, "stream", "slab", None), P(None, "slab"), P(), P(), P(), P())
    return jax.shard_map(
        shards,
        mesh=mesh,
        in_specs=placed,
        out_specs=P("section", None, "stream", "slab", None),
        check_vma=False,
    )
```

```python
import functools

import jax
import jax.numpy as jnp
from jax import lax
from jax.experimental import pallas as pl
from jax.experimental.pallas import tpu as pltpu
from jax.sharding import PartitionSpec as P

mach_number = 0.5
tau = 0.05
filter_weight = 0.25
IN_P, IN_U, IN_V, IN_W = 8, 8, 10, 8
SLOTS = 19
OUT_P, OUT_U, OUT_V, OUT_W = 14, 10, 12, 10
AXES = ("section", "stream", "slab")
LEFT = ("e1", "ta", "m1", "m2", "e2", "a", "e4", "e6", "e8", "fx")
RIGHT = ("c", "cc", "fz")
f32, bf16 = jnp.float32, jnp.bfloat16


def call(body, out_shape, *args, flops=0, scratch=()):
    moved = sum(a.size * a.dtype.itemsize for a in args)
    return pl.pallas_call(
        body,
        out_shape=out_shape,
        scratch_shapes=scratch,
        compiler_params=pltpu.CompilerParams(vmem_limit_bytes=40 * 2**20),
        cost_estimate=pl.CostEstimate(flops=flops, bytes_accessed=moved, transcendentals=0),
    )(*args)


def order_of(count):
    places = []
    for j in range(count):
        step, rung = j // 2, j % 2
        x, y = (rung, step) if step < 4 else (3 - rung, 7 - step)
        places.append(4 * x + y)
    return places


def halves(value):
    high = value.astype(bf16)
    return high, (value - high.astype(f32)).astype(bf16)


def left_form(matrix):
    high, low = halves(matrix)
    return jnp.concatenate([high, high, low], axis=1)


def right_form(matrix):
    high, low = halves(matrix)
    return jnp.concatenate([high, high, low], axis=0)


def times_left(form, planes):
    high, low = halves(jnp.concatenate(planes, axis=1))
    out = jnp.dot(form, jnp.concatenate([high, low, high], axis=0), preferred_element_type=f32)
    width = planes[0].shape[1]
    return [out[:, i * width : (i + 1) * width] for i in range(len(planes))]


def times_right(planes, form):
    high, low = halves(jnp.concatenate(planes, axis=0))
    out = jnp.dot(jnp.concatenate([high, low, high], axis=1), form, preferred_element_type=f32)
    length = planes[0].shape[0]
    return [out[i * length : (i + 1) * length] for i in range(len(planes))]


def prepare_kernel(dx_ref, dzt_ref, fx_ref, fzt_ref, left_ref, right_ref):
    def dot(one, two):
        return jnp.dot(one, two, precision=lax.Precision.HIGHEST, preferred_element_type=f32)

    dx, dzt = dx_ref[...], dzt_ref[...]
    square = dot(dx, dx)
    e1 = -tau * mach_number * dx
    e2 = 2.0 * e1 + (tau * mach_number) ** 2 * square
    e4 = 2.0 * e2 + dot(e2, e2)
    values = {
        "e1": e1,
        "ta": -tau * dx,
        "m1": 2.0 * e1,
        "m2": tau**2 * square - e2,
        "e2": e2,
        "a": dx,
        "e4": e4,
        "e6": e2 + e4 + dot(e2, e4),
        "e8": 2.0 * e4 + dot(e4, e4),
        "fx": filter_weight * fx_ref[...],
    }
    for i, name in enumerate(LEFT):
        left_ref[i] = left_form(values[name])
    others = {"c": dzt, "cc": tau**2 * dot(dzt, dzt), "fz": filter_weight * fzt_ref[...]}
    for i, name in enumerate(RIGHT):
        right_ref[i] = right_form(others[name])


class Products:
    def __init__(self, left_ref, right_ref):
        self.left_ref, self.right_ref = left_ref, right_ref

    def left(self, name, planes):
        return times_left(self.left_ref[LEFT.index(name)], planes)

    def right(self, planes, name):
        return times_right(planes, self.right_ref[RIGHT.index(name)])


def inside(value, reach, low_ok, high_ok):
    rows = value.shape[0]
    return jnp.concatenate(
        [value[:reach] * low_ok, value[reach : rows - reach], value[rows - reach :] * high_ok], axis=0
    )


def shift_rows(value, steps):
    zeros = jnp.zeros((abs(steps),) + value.shape[1:], f32)
    if steps > 0:
        return jnp.concatenate([value[steps:], zeros], axis=0)
    return jnp.concatenate([zeros, value[:steps]], axis=0)


def slope4(value):
    near = shift_rows(value, 1) - shift_rows(value, -1)
    far = shift_rows(value, 2) - shift_rows(value, -2)
    return (2.0 / 3.0) * near - (1.0 / 12.0) * far


def turn_kernel(state_ref, raw_ref, first_ref, top_ref, bottom_ref):
    own = state_ref.shape[2]
    order = order_of(own)
    lead = 0
    for i, reach in enumerate((IN_P, IN_U, IN_V, IN_W)):
        turned = jnp.swapaxes(state_ref[i], 0, 1)
        raw_ref[i] = turned
        for j in range(own):
            first_ref[order[j], i] = turned[j]
        top_ref[lead : lead + reach] = turned[own - reach :]
        bottom_ref[lead : lead + reach] = turned[:reach]
        lead += reach


def spread_kernel(edge_ref, raw_ref, low_ref, high_ref, right_ref, out_ref):
    low_ok, high_ok = edge_ref[0], edge_ref[1]
    own, xs, nz = raw_ref.shape[1:]
    order = order_of(own)
    ext = []
    lead = 0
    for i, reach in enumerate((IN_P, IN_U, IN_V, IN_W)):
        ext.append(
            jnp.concatenate(
                [low_ref[lead : lead + reach] * low_ok, raw_ref[i], high_ref[lead : lead + reach] * high_ok],
                axis=0,
            )
        )
        lead += reach

    def twice(value):
        once = inside(slope4(value), IN_P, low_ok, high_ok)
        return inside(slope4(once), IN_P, low_ok, high_ok)

    def put(place, value):
        which, place = PLACES[place]
        if which == 1:
            reach = (value.shape[0] - own) // 2
            for j in range(own):
                out_ref[order[j], place] = value[reach + j]

    def slope2(value):
        return 0.5 * (value[IN_P + 1 : IN_P + 1 + own] - value[IN_P - 1 : IN_P - 1 + own])

    rows = ext[3].shape[0]
    through = times_right([ext[3].reshape(rows * xs, nz)], right_ref[RIGHT.index("c")])[0]
    cut = IN_V - IN_W
    rate = through.reshape(rows, xs, nz) + slope4(ext[2])[cut : cut + rows]
    rate = inside(rate, IN_W, low_ok, high_ok)
    for place, value in ((0, ext[0]), (3, ext[1]), (6, rate)):
        put(place, value)
        value = twice(value)
        put(place + 1, value)
        put(place + 2, twice(value))
    put(11, slope2(ext[1]))
    put(12, slope2(ext[3]))


class Raiser:
    def __init__(self, edge_ref, back_ref):
        self.low_ok, self.high_ok = edge_ref[0], edge_ref[1]
        self.back_ref = back_ref
        self.own = back_ref.shape[0]
        self.order = order_of(self.own)

    def load(self, slot):
        return jnp.stack([self.back_ref[self.order[j], slot] for j in range(self.own)])

    def total(self, fields):
        total = fields[-1]
        for value in fields[-2::-1]:
            edge = (total.shape[0] - self.own) // 2 + 2
            zeros = jnp.zeros((2,) + total.shape[1:], f32)
            total = slope4(jnp.concatenate([zeros, total, zeros], axis=0))
            centre = total[edge : edge + self.own]
            if value is not None:
                centre = centre + value
            total = jnp.concatenate(
                [total[:edge] * self.low_ok, centre, total[edge + self.own :] * self.high_ok], axis=0
            )
        return total


def gather_odd_kernel(edge_ref, back_ref, out_ref):
    @pl.when(edge_ref[2] > 0)
    def _():
        raiser = Raiser(edge_ref, back_ref)
        p = [raiser.load(10 + i) for i in range(4)]
        u = [raiser.load(14 + i) for i in range(3)]
        lead = 0
        for value in (
            raiser.total([None, p[0], None, p[1], None, p[2], None, p[3]]),
            raiser.total([None, u[0], None, u[1], None, u[2]]),
            raiser.total([None, raiser.load(17)]),
        ):
            out_ref[lead : lead + value.shape[0]] = value
            lead += value.shape[0]

    @pl.when(edge_ref[2] <= 0)
    def _():
        out_ref[...] = jnp.zeros(out_ref.shape, f32)


def gather_kernel(edge_ref, back_ref, own_ref, high_ref, low_ref):
    raiser = Raiser(edge_ref, back_ref)
    own = raiser.own
    sound = 1.0 - edge_ref[2]

    def extra(i):
        return sound * raiser.load(10 + i)

    p = [raiser.load(0), None, raiser.load(1), None, raiser.load(2), None, extra(0)]
    u = [raiser.load(3), None, raiser.load(4), None, extra(1)]
    w = [raiser.load(5), None, raiser.load(6), extra(4), extra(2), extra(5)]
    v = [raiser.load(7), raiser.load(8), extra(6), raiser.load(9), extra(7), extra(3), extra(8)]
    place = 0
    for output, (fields, room) in enumerate(((p, OUT_P), (u, OUT_U), (v, OUT_V), (w, OUT_W))):
        total = raiser.total(fields)
        reach = 2 * (len(fields) - 1)
        own_ref[output] = total[reach : reach + own]
        if room > reach:
            low_ref[place : place + room - reach] = jnp.zeros((room - reach,) + total.shape[1:], f32)
            high_ref[place + reach : place + room] = jnp.zeros((room - reach,) + total.shape[1:], f32)
        low_ref[place + room - reach : place + room] = total[:reach]
        high_ref[place : place + reach] = total[reach + own :]
        place += room


PLACES = ((0, 0), (1, 0), (1, 1), (0, 1), (1, 2), (1, 3), (1, 4), (1, 5), (1, 6), (0, 2), (0, 3), (1, 7), (1, 8))


def plane(refs, index):
    which, place = PLACES[index]
    blocks, _, xs, nz = refs[which].shape
    return refs[which][:, place].reshape(blocks * xs, nz)


def waves_kernel(raw_ref, more_ref, left_ref, right_ref, out_ref):
    do = Products(left_ref, right_ref)
    p0 = [plane((raw_ref, more_ref), i) for i in range(3)]
    u0 = [plane((raw_ref, more_ref), 3 + i) for i in range(3)]

    def advance(now, before):
        count = len(before) - 1
        one = do.left("m1", now[:count])
        two = do.left("m2", before[:count])
        three = do.right(before[:count], "cc")
        return [
            2.0 * now[i] - before[i] + (one[i] + two[i] + three[i] + tau**2 * before[i + 1])
            for i in range(count)
        ]

    moved = do.left("e1", p0)
    driven = do.left("ta", u0)
    p1 = [p0[i] + (moved[i] + driven[i] - tau * plane((raw_ref, more_ref), 6 + i)) for i in range(3)]
    h2 = p0[0] + moved[0] + p1[0]
    out_ref[2] = h2
    p2 = advance(p1, p0)
    p3 = advance(p2, p1)
    h4 = h2 + do.left("e2", [h2])[0] + p2[0] + do.left("e1", p2[:1])[0] + p3[0]
    out_ref[3] = h4
    p4 = advance(p3, p2)
    p5 = advance(p4, p3)
    h6 = h4 + do.left("e2", [h4])[0] + p4[0] + do.left("e1", p4)[0] + p5[0]
    out_ref[0] = p4[0]
    out_ref[1] = p5[0]
    out_ref[4] = h6


def held_kernel(raw_ref, more_ref, waves_ref, left_ref, right_ref, out_ref):
    do = Products(left_ref, right_ref)
    start = [plane((raw_ref, more_ref), i) for i in (3, 10, 11, 12, 9)]
    h = [waves_ref[2 + n] for n in range(3)]
    pull_x = do.left("a", h)
    pull_z = do.right(h, "c")
    for n, growth in enumerate(("e2", "e4", "e6")):
        change = do.left(growth, start)
        out_ref[n, 0] = start[0] + change[0] - tau * pull_x[n]
        out_ref[n, 1] = start[1] + change[1] - tau * pull_z[n]
        for k in (2, 3, 4):
            out_ref[n, k] = start[k] + change[k]


def source_kernel(flag_ref, region_ref, raw_ref, more_ref, held_ref, up1_ref, down1_ref, up2_ref, down2_ref, left_ref, right_ref, out_ref):
    do = Products(left_ref, right_ref)
    nx, nz = up1_ref.shape[1:]
    row = lax.broadcasted_iota(jnp.int32, (nx, nz), 0)
    lane = lax.broadcasted_iota(jnp.int32, (nx, nz), 1)
    region = region_ref[...]

    def slope_x(value):
        ahead = jnp.where(row == nx - 1, 0.0, pltpu.roll(value, nx - 1, 0))
        behind = jnp.where(row == 0, 0.0, pltpu.roll(value, 1, 0))
        return 0.5 * (ahead - behind)

    def slope_z(value):
        ahead = jnp.where(lane == nz - 1, 0.0, pltpu.roll(value, nz - 1, 1))
        behind = jnp.where(lane == 0, 0.0, pltpu.roll(value, 1, 1))
        return 0.5 * (ahead - behind)

    up1, down1, up2, down2 = flag_ref[3], flag_ref[4], flag_ref[5], flag_ref[6]
    near = [up1 * up1_ref[n] - down1 * down1_ref[n] for n in range(3)]
    half = [0.5 * value for value in near]
    pull_x = do.left("a", half)
    pull_z = do.right(half, "c")
    for n in range(4):
        if n == 0:
            u, w, slope_u, slope_w, v = [plane((raw_ref, more_ref), i) for i in (3, 10, 11, 12, 9)]
        else:
            u, w = held_ref[n - 1, 0], held_ref[n - 1, 1]
            slope_u = held_ref[n - 1, 2] - tau * pull_x[n - 1]
            slope_w = held_ref[n - 1, 3] - tau * pull_z[n - 1]
            far = up2 * up2_ref[n - 1] - down2 * down2_ref[n - 1]
            v = held_ref[n - 1, 4] - tau * ((2.0 / 3.0) * near[n - 1] - (1.0 / 12.0) * far)
        o_x = slope_w - slope_z(v)
        o_y = slope_z(u) - slope_x(w)
        o_z = slope_x(v) - slope_u
        out_ref[n, 0] = region * (o_z * v - o_y * w)
        out_ref[n, 1] = region * (o_x * w - o_z * u)
        out_ref[n, 2] = region * (o_y * u - o_x * v)


class Chain:
    def __init__(self, left_ref, right_ref):
        self.do = Products(left_ref, right_ref)

    def advance(self, now, before, drive, count):
        m_now = self.do.left("m1", now)
        m_before = self.do.left("m2", before)
        c_before = self.do.right(before, "cc")
        out = []
        for k in range(count):
            terms = []
            if k < len(now):
                terms.append(2.0 * now[k] + m_now[k])
            if k < len(before):
                terms.append(m_before[k] + c_before[k] - before[k])
            if 0 <= k - 2 < len(before):
                terms.append(tau**2 * before[k - 2])
            if k < len(drive):
                terms.append(drive[k])
            out.append(functools.reduce(lambda one, two: one + two, terms))
        return out

    def grow(self, sums, before, now):
        moved = self.do.left("e1", before)
        kept = self.do.left("e2", sums) if sums else []
        out = [before[k] + moved[k] + now[k] for k in range(len(now))]
        return [out[k] + (sums[k] + kept[k]) if k < len(sums) else out[k] for k in range(len(now))]


def drives(do, flag_ref, own_ref, source_ref, first, last):
    flow = flag_ref[2] > 0
    one = do.left("a", [source_ref[n, 0] for n in range(first, last)])
    two = do.right([source_ref[n, 2] for n in range(first, last)], "c")
    return [
        (
            jnp.where(flow, 0.0, -(tau**2) * (one[n - first] + two[n - first])),
            -(tau**2) * jnp.where(flow, own_ref[n, 1], source_ref[n, 1]),
        )
        for n in range(first, last)
    ]


def driven_kernel(flag_ref, waves_ref, own_ref, source_ref, left_ref, right_ref, out_ref):
    chain = Chain(left_ref, right_ref)
    drive = drives(chain.do, flag_ref, own_ref, source_ref, 0, 2)
    q2 = list(drive[0])
    moved = chain.do.left("m1", q2)
    q3 = [2.0 * q2[k] + moved[k] + drive[0][k] for k in range(2)]
    g4 = chain.grow([], q2, q3)
    q4 = chain.advance(q3, q2, drive[1], 4)
    q5 = chain.advance(q4, q3, drive[1], 4)
    g6 = chain.grow(g4, q4, q5)
    for first, values, wave in ((0, q4, 0), (4, q5, 1), (8, g6, 4)):
        out_ref[first] = values[0] + waves_ref[wave]
        for k in range(1, 4):
            out_ref[first + k] = values[k]


def finish_kernel(flag_ref, raw_ref, more_ref, driven_ref, own_ref, source_ref, left_ref, right_ref, out_ref):
    chain = Chain(left_ref, right_ref)
    do = chain.do
    drive = drives(do, flag_ref, own_ref, source_ref, 2, 4)
    q4, q5, g6 = [[driven_ref[first + k] for k in range(4)] for first in (0, 4, 8)]
    q6 = chain.advance(q5, q4, drive[0], 6)
    q7 = chain.advance(q6, q5, drive[0], 6)
    for k, value in enumerate(chain.grow(g6, q6, q7)):
        out_ref[8 + k] = value
    for k, value in enumerate(chain.advance(q7, q6, drive[1], 8)):
        out_ref[k] = value
    flow = flag_ref[2] > 0

    def arrived(n):
        return [jnp.where(flow, 0.0, source_ref[n, k]) for k in range(3)]

    total = arrived(0)
    for n in (1, 2, 3):
        kept = do.left("e2", total)
        fresh = arrived(n)
        total = [total[k] + kept[k] + fresh[k] for k in range(3)]
    moved = do.left("e1", total)
    begin = [plane((raw_ref, more_ref), i) for i in (3, 9, 10)]
    kept = do.left("e8", begin)
    for i in range(3):
        out_ref[14 + i] = begin[i] + kept[i] + tau * (2.0 * total[i] + moved[i])


def filter_kernel(flag_ref, last_ref, left_ref, right_ref, out_ref):
    do = Products(left_ref, right_ref)
    blocks, _, xs, nz = out_ref.shape

    def emit(place, values):
        fx, fz = do.left("fx", values), do.right(values, "fz")
        for i, value in enumerate(values):
            out_ref[:, place + i] = (value + fx[i] + fz[i]).reshape(blocks, xs, nz)

    def p(k):
        return last_ref[k]

    def h(k):
        return last_ref[8 + k]

    def third(*which):
        return [-tau * value for value in do.right([h(k) for k in which], "c")]

    axial = do.left("ta", [h(0), h(2)])
    depth = third(0, 2)
    emit(0, [p(0), p(2), p(4), last_ref[14] + axial[0], axial[1], last_ref[16] + depth[0], depth[1]])
    emit(7, [last_ref[15], -tau * h(0), -tau * h(2)])

    @pl.when(flag_ref[2] > 0)
    def _():
        axial = do.left("ta", [h(1), h(3), h(5)])
        emit(10, [p(1), p(3), p(5), p(7)] + axial + third(1))
        out_ref[:, 18] = jnp.zeros((blocks, xs, nz), f32)

    @pl.when(flag_ref[2] <= 0)
    def _():
        axial = do.left("ta", [h(4)])
        depth = third(4, 3, 5)
        emit(10, [p(6), axial[0], depth[0], -tau * h(4), depth[1], depth[2]])
        emit(16, [-tau * h(1), -tau * h(3), -tau * h(5)])


def along_y(steps):
    streams, slabs = lax.axis_size("stream"), lax.axis_size("slab")
    count = streams * slabs
    order = order_of(streams)

    def device(y):
        return order[y % streams] * slabs + y // streams

    flow = [(device(y), device((y + steps) % count)) for y in range(count)]
    return flow + [(i, i) for i in range(count, count * lax.axis_size("section"))]


def shards(state, source_mask, deriv_x, deriv_z, filter_x, filter_z):
    _, _, xs, own, nz = state.shape
    slabs, streams = lax.axis_size("slab"), lax.axis_size("stream")
    slab = lax.axis_index("slab")
    nx = xs * streams
    upward = [(i, (i + 1) % slabs) for i in range(slabs)]
    downward = [((i + 1) % slabs, i) for i in range(slabs)]
    swap = [(0, 1), (1, 0)]
    inverse = [0] * streams
    for j, stream in enumerate(order_of(streams)):
        inverse[stream] = j
    y = slab * streams + jnp.asarray(inverse, jnp.int32)[lax.axis_index("stream")]
    last_y = slabs * streams - 1
    edges = jnp.stack(
        [slab > 0, slab < slabs - 1, lax.axis_index("section") == 0]
        + [y < last_y, y > 0, y < last_y - 1, y > 1]
    ).astype(f32)
    region = jnp.repeat(source_mask[:, 0].astype(f32), nx // source_mask.shape[0])
    region = jnp.broadcast_to(region[:, None], (nx, nz))

    def shape(*dims):
        return jax.ShapeDtypeStruct(dims, f32)

    border = IN_P + IN_U + IN_V + IN_W
    raw, ordered, top, bottom = call(
        turn_kernel,
        (shape(4, own, xs, nz), shape(streams, 4, xs, nz), shape(border, xs, nz), shape(border, xs, nz)),
        state[0],
    )
    from_low = lax.ppermute(top, "slab", upward)
    from_high = lax.ppermute(bottom, "slab", downward)
    first = lax.all_to_all(ordered, "stream", split_axis=0, concat_axis=0, tiled=True)
    left, right = call(
        prepare_kernel,
        (
            jax.ShapeDtypeStruct((len(LEFT), nx, 3 * nx), bf16),
            jax.ShapeDtypeStruct((len(RIGHT), 3 * nz, nz), bf16),
        ),
        deriv_x,
        deriv_z.T,
        filter_x,
        filter_z.T,
        flops=10**9,
    )

    def with_edges(body, out_shape, *args):
        return pl.pallas_call(
            body,
            out_shape=out_shape,
            in_specs=[pl.BlockSpec(memory_space=pltpu.SMEM)]
            + [pl.BlockSpec(memory_space=pltpu.VMEM)] * len(args),
            compiler_params=pltpu.CompilerParams(vmem_limit_bytes=40 * 2**20),
        )(edges, *args)

    spread = with_edges(spread_kernel, shape(own, 9, xs, nz), raw, from_low, from_high, right)
    planes = (first, lax.all_to_all(spread, "stream", split_axis=0, concat_axis=0, tiled=True))
    waves = call(waves_kernel, shape(5, nx, nz), *planes, left, right, flops=2 * 10**9)
    sums = waves[2:5]
    near = [lax.ppermute(sums, AXES, along_y(steps)) for steps in (-1, 1, -2, 2)]
    held = call(held_kernel, shape(3, 5, nx, nz), *planes, waves, left, right, flops=10**9)
    source = with_edges(
        source_kernel, shape(4, 3, nx, nz), region, *planes, held, *near, left, right
    )
    moved = lax.ppermute(source, "section", swap)
    driven = with_edges(driven_kernel, shape(12, nx, nz), waves, source, moved, left, right)
    last = with_edges(finish_kernel, shape(17, nx, nz), *planes, driven, source, moved, left, right)
    done = with_edges(filter_kernel, shape(streams, SLOTS, xs, nz), last, left, right)
    back = lax.all_to_all(done, "stream", split_axis=0, concat_axis=0, tiled=True)
    border = OUT_P + OUT_U + OUT_V + OUT_W
    rows = ((OUT_P, 0), (OUT_U, 1), (2, 3))
    odd = with_edges(gather_odd_kernel, shape(sum(own + 2 * reach for reach, _ in rows), xs, nz), back)
    odd = lax.ppermute(odd, "section", swap)
    mine, high, low = with_edges(
        gather_kernel, (shape(4, own, xs, nz), shape(border, xs, nz), shape(border, xs, nz)), back
    )
    starts = (0, OUT_P, OUT_P + OUT_U, OUT_P + OUT_U + OUT_V)
    reaches = (OUT_P, OUT_U, OUT_V, OUT_W)
    lead = 0
    more_high, more_low, more_own = [], [], [jnp.zeros((own, xs, nz), f32)] * 4
    for reach, output in rows:
        part = odd[lead : lead + own + 2 * reach]
        start, room = starts[output], reaches[output]
        more_low.append(jnp.pad(part[:reach], ((start + room - reach, border - start - room), (0, 0), (0, 0))))
        more_high.append(jnp.pad(part[reach + own :], ((start, border - start - reach), (0, 0), (0, 0))))
        more_own[output] = part[reach : reach + own]
        lead += own + 2 * reach
    from_low = lax.ppermute(high + sum(more_high), "slab", upward)
    from_high = lax.ppermute(low + sum(more_low), "slab", downward)
    outs = []
    for i, (start, reach) in enumerate(zip(starts, reaches)):
        from_below = jnp.pad(from_low[start : start + reach], ((0, own - reach), (0, 0), (0, 0)))
        from_above = jnp.pad(from_high[start : start + reach], ((own - reach, 0), (0, 0), (0, 0)))
        outs.append(mine[i] + more_own[i] + from_below + from_above)
    return jnp.swapaxes(jnp.stack(outs), 1, 2)[None]


def solution(mesh):
    placed = (P("section", None, "stream", "slab", None), P(None, "slab"), P(), P(), P(), P())
    return jax.shard_map(
        shards,
        mesh=mesh,
        in_specs=placed,
        out_specs=P("section", None, "stream", "slab", None),
        check_vma=False,
    )
```

```python
import functools

import jax
import jax.numpy as jnp
from jax import lax
from jax.experimental import pallas as pl
from jax.experimental.pallas import tpu as pltpu
from jax.sharding import PartitionSpec as P

mach_number = 0.5
tau = 0.05
filter_weight = 0.25
IN_P, IN_U, IN_V, IN_W = 8, 8, 10, 8
SLOTS = 19
OUT_P, OUT_U, OUT_V, OUT_W = 14, 10, 12, 10
AXES = ("section", "stream", "slab")
LEFT = ("e1", "ta", "m1", "m2", "e2", "a", "e4", "e6", "e8", "fx")
RIGHT = ("c", "cc", "fz")
f32, bf16 = jnp.float32, jnp.bfloat16


def call(body, out_shape, *args, flops=0, scratch=()):
    moved = sum(a.size * a.dtype.itemsize for a in args)
    return pl.pallas_call(
        body,
        out_shape=out_shape,
        scratch_shapes=scratch,
        compiler_params=pltpu.CompilerParams(vmem_limit_bytes=40 * 2**20),
        cost_estimate=pl.CostEstimate(flops=flops, bytes_accessed=moved, transcendentals=0),
    )(*args)


def order_of(count):
    places = []
    for j in range(count):
        step, rung = j // 2, j % 2
        x, y = (rung, step) if step < 4 else (3 - rung, 7 - step)
        places.append(4 * x + y)
    return places


def halves(value):
    high = value.astype(bf16)
    return high, (value - high.astype(f32)).astype(bf16)


def left_form(matrix):
    high, low = halves(matrix)
    return jnp.concatenate([high, high, low], axis=1)


def right_form(matrix):
    high, low = halves(matrix)
    return jnp.concatenate([high, high, low], axis=0)


def times_left(form, planes):
    high, low = halves(jnp.concatenate(planes, axis=1))
    out = jnp.dot(form, jnp.concatenate([high, low, high], axis=0), preferred_element_type=f32)
    width = planes[0].shape[1]
    return [out[:, i * width : (i + 1) * width] for i in range(len(planes))]


def times_right(planes, form):
    high, low = halves(jnp.concatenate(planes, axis=0))
    out = jnp.dot(jnp.concatenate([high, low, high], axis=1), form, preferred_element_type=f32)
    length = planes[0].shape[0]
    return [out[i * length : (i + 1) * length] for i in range(len(planes))]


def prepare_kernel(dx_ref, dzt_ref, fx_ref, fzt_ref, left_ref, right_ref):
    def dot(one, two):
        return jnp.dot(one, two, precision=lax.Precision.HIGHEST, preferred_element_type=f32)

    dx, dzt = dx_ref[...], dzt_ref[...]
    square = dot(dx, dx)
    e1 = -tau * mach_number * dx
    e2 = 2.0 * e1 + (tau * mach_number) ** 2 * square
    e4 = 2.0 * e2 + dot(e2, e2)
    values = {
        "e1": e1,
        "ta": -tau * dx,
        "m1": 2.0 * e1,
        "m2": tau**2 * square - e2,
        "e2": e2,
        "a": dx,
        "e4": e4,
        "e6": e2 + e4 + dot(e2, e4),
        "e8": 2.0 * e4 + dot(e4, e4),
        "fx": filter_weight * fx_ref[...],
    }
    for i, name in enumerate(LEFT):
        left_ref[i] = left_form(values[name])
    others = {"c": dzt, "cc": tau**2 * dot(dzt, dzt), "fz": filter_weight * fzt_ref[...]}
    for i, name in enumerate(RIGHT):
        right_ref[i] = right_form(others[name])


class Products:
    def __init__(self, left_ref, right_ref):
        self.left_ref, self.right_ref = left_ref, right_ref

    def left(self, name, planes):
        return times_left(self.left_ref[LEFT.index(name)], planes)

    def right(self, planes, name):
        return times_right(planes, self.right_ref[RIGHT.index(name)])


def inside(value, reach, low_ok, high_ok):
    rows = value.shape[0]
    return jnp.concatenate(
        [value[:reach] * low_ok, value[reach : rows - reach], value[rows - reach :] * high_ok], axis=0
    )


def shift_rows(value, steps):
    zeros = jnp.zeros((abs(steps),) + value.shape[1:], f32)
    if steps > 0:
        return jnp.concatenate([value[steps:], zeros], axis=0)
    return jnp.concatenate([zeros, value[:steps]], axis=0)


def slope4(value):
    near = shift_rows(value, 1) - shift_rows(value, -1)
    far = shift_rows(value, 2) - shift_rows(value, -2)
    return (2.0 / 3.0) * near - (1.0 / 12.0) * far


def spread_kernel(edge_ref, raw_ref, low_ref, high_ref, right_ref, out_ref):
    low_ok, high_ok = edge_ref[0], edge_ref[1]
    own, xs, nz = raw_ref.shape[1:]
    order = order_of(own)
    ext = []
    lead = 0
    for i, reach in enumerate((IN_P, IN_U, IN_V, IN_W)):
        ext.append(
            jnp.concatenate(
                [low_ref[lead : lead + reach] * low_ok, raw_ref[i], high_ref[lead : lead + reach] * high_ok],
                axis=0,
            )
        )
        lead += reach

    def twice(value):
        once = inside(slope4(value), IN_P, low_ok, high_ok)
        return inside(slope4(once), IN_P, low_ok, high_ok)

    def put(place, value):
        reach = (value.shape[0] - own) // 2
        for j in range(own):
            out_ref[order[j], place] = value[reach + j]

    def slope2(value):
        return 0.5 * (value[IN_P + 1 : IN_P + 1 + own] - value[IN_P - 1 : IN_P - 1 + own])

    rows = ext[3].shape[0]
    through = times_right([ext[3].reshape(rows * xs, nz)], right_ref[RIGHT.index("c")])[0]
    cut = IN_V - IN_W
    rate = through.reshape(rows, xs, nz) + slope4(ext[2])[cut : cut + rows]
    rate = inside(rate, IN_W, low_ok, high_ok)
    for place, value in ((0, ext[0]), (3, ext[1]), (6, rate)):
        put(place, value)
        value = twice(value)
        put(place + 1, value)
        put(place + 2, twice(value))
    put(9, raw_ref[2])
    put(10, raw_ref[3])
    put(11, slope2(ext[1]))
    put(12, slope2(ext[3]))


class Raiser:
    def __init__(self, edge_ref, back_ref):
        self.low_ok, self.high_ok = edge_ref[0], edge_ref[1]
        self.back_ref = back_ref
        self.own = back_ref.shape[0]
        self.order = order_of(self.own)

    def load(self, slot):
        return jnp.stack([self.back_ref[self.order[j], slot] for j in range(self.own)])

    def total(self, fields):
        total = fields[-1]
        for value in fields[-2::-1]:
            edge = (total.shape[0] - self.own) // 2 + 2
            zeros = jnp.zeros((2,) + total.shape[1:], f32)
            total = slope4(jnp.concatenate([zeros, total, zeros], axis=0))
            centre = total[edge : edge + self.own]
            if value is not None:
                centre = centre + value
            total = jnp.concatenate(
                [total[:edge] * self.low_ok, centre, total[edge + self.own :] * self.high_ok], axis=0
            )
        return total


def gather_odd_kernel(edge_ref, back_ref, out_ref):
    @pl.when(edge_ref[2] > 0)
    def _():
        raiser = Raiser(edge_ref, back_ref)
        p = [raiser.load(10 + i) for i in range(4)]
        u = [raiser.load(14 + i) for i in range(3)]
        lead = 0
        for value in (
            raiser.total([None, p[0], None, p[1], None, p[2], None, p[3]]),
            raiser.total([None, u[0], None, u[1], None, u[2]]),
            raiser.total([None, raiser.load(17)]),
        ):
            out_ref[lead : lead + value.shape[0]] = value
            lead += value.shape[0]

    @pl.when(edge_ref[2] <= 0)
    def _():
        out_ref[...] = jnp.zeros(out_ref.shape, f32)


def gather_kernel(edge_ref, back_ref, own_ref, high_ref, low_ref):
    raiser = Raiser(edge_ref, back_ref)
    own = raiser.own
    sound = 1.0 - edge_ref[2]

    def extra(i):
        return sound * raiser.load(10 + i)

    p = [raiser.load(0), None, raiser.load(1), None, raiser.load(2), None, extra(0)]
    u = [raiser.load(3), None, raiser.load(4), None, extra(1)]
    w = [raiser.load(5), None, raiser.load(6), extra(4), extra(2), extra(5)]
    v = [raiser.load(7), raiser.load(8), extra(6), raiser.load(9), extra(7), extra(3), extra(8)]
    place = 0
    for output, (fields, room) in enumerate(((p, OUT_P), (u, OUT_U), (v, OUT_V), (w, OUT_W))):
        total = raiser.total(fields)
        reach = 2 * (len(fields) - 1)
        own_ref[output] = total[reach : reach + own]
        if room > reach:
            low_ref[place : place + room - reach] = jnp.zeros((room - reach,) + total.shape[1:], f32)
            high_ref[place + reach : place + room] = jnp.zeros((room - reach,) + total.shape[1:], f32)
        low_ref[place + room - reach : place + room] = total[:reach]
        high_ref[place : place + reach] = total[reach + own :]
        place += room


def plane(ref, index):
    blocks, _, xs, nz = ref.shape
    return ref[:, index].reshape(blocks * xs, nz)


def waves_kernel(in_ref, left_ref, right_ref, out_ref, sums_ref):
    do = Products(left_ref, right_ref)
    p0 = [plane(in_ref, i) for i in range(3)]
    u0 = [plane(in_ref, 3 + i) for i in range(3)]

    def advance(now, before):
        count = len(before) - 1
        one = do.left("m1", now[:count])
        two = do.left("m2", before[:count])
        three = do.right(before[:count], "cc")
        return [
            2.0 * now[i] - before[i] + (one[i] + two[i] + three[i] + tau**2 * before[i + 1])
            for i in range(count)
        ], one[0]

    moved = do.left("e1", p0)
    driven = do.left("ta", u0)
    p1 = [p0[i] + (moved[i] + driven[i] - tau * plane(in_ref, 6 + i)) for i in range(3)]
    h2 = p0[0] + moved[0] + p1[0]
    sums_ref[0] = h2
    p2, _ = advance(p1, p0)
    p3, twice = advance(p2, p1)
    h4 = h2 + do.left("e2", [h2])[0] + p2[0] + 0.5 * twice + p3[0]
    sums_ref[1] = h4
    p4, _ = advance(p3, p2)
    p5, twice = advance(p4, p3)
    sums_ref[2] = h4 + do.left("e2", [h4])[0] + p4[0] + 0.5 * twice + p5[0]
    out_ref[0] = p4[0]
    out_ref[1] = p5[0]


def held_kernel(in_ref, sums_ref, left_ref, right_ref, out_ref):
    do = Products(left_ref, right_ref)
    start = [plane(in_ref, i) for i in (3, 10, 11, 12, 9)]
    h = [sums_ref[n] for n in range(3)]
    pull_x = do.left("a", h)
    pull_z = do.right(h, "c")
    for n, growth in enumerate(("e2", "e4", "e6")):
        change = do.left(growth, start)
        out_ref[n, 0] = start[0] + change[0] - tau * pull_x[n]
        out_ref[n, 1] = start[1] + change[1] - tau * pull_z[n]
        for k in (2, 3, 4):
            out_ref[n, k] = start[k] + change[k]


def source_kernel(flag_ref, region_ref, in_ref, held_ref, up_ref, down_ref, far_ref, left_ref, right_ref, out_ref):
    do = Products(left_ref, right_ref)
    nx, nz = up_ref.shape[1:]
    row = lax.broadcasted_iota(jnp.int32, (nx, nz), 0)
    lane = lax.broadcasted_iota(jnp.int32, (nx, nz), 1)
    region = region_ref[...]

    def slope_x(value):
        ahead = jnp.where(row == nx - 1, 0.0, pltpu.roll(value, nx - 1, 0))
        behind = jnp.where(row == 0, 0.0, pltpu.roll(value, 1, 0))
        return 0.5 * (ahead - behind)

    def slope_z(value):
        ahead = jnp.where(lane == nz - 1, 0.0, pltpu.roll(value, nz - 1, 1))
        behind = jnp.where(lane == 0, 0.0, pltpu.roll(value, 1, 1))
        return 0.5 * (ahead - behind)

    near = [flag_ref[3] * up_ref[n] - flag_ref[4] * down_ref[n] for n in range(3)]
    half = [0.5 * value for value in near]
    pull_x = do.left("a", half)
    pull_z = do.right(half, "c")
    for n in range(4):
        if n == 0:
            u, w, slope_u, slope_w, v = [plane(in_ref, i) for i in (3, 10, 11, 12, 9)]
        else:
            u, w = held_ref[n - 1, 0], held_ref[n - 1, 1]
            slope_u = held_ref[n - 1, 2] - tau * pull_x[n - 1]
            slope_w = held_ref[n - 1, 3] - tau * pull_z[n - 1]
            far = far_ref[n - 1]
            v = held_ref[n - 1, 4] - tau * ((2.0 / 3.0) * near[n - 1] - (1.0 / 12.0) * far)
        o_x = slope_w - slope_z(v)
        o_y = slope_z(u) - slope_x(w)
        o_z = slope_x(v) - slope_u
        out_ref[n, 0] = region * (o_z * v - o_y * w)
        out_ref[n, 1] = region * (o_x * w - o_z * u)
        out_ref[n, 2] = region * (o_y * u - o_x * v)


class Chain:
    def __init__(self, left_ref, right_ref):
        self.do = Products(left_ref, right_ref)

    def advance(self, now, before, drive, count):
        m_now = self.do.left("m1", now)
        m_before = self.do.left("m2", before)
        c_before = self.do.right(before, "cc")
        out = []
        for k in range(count):
            terms = []
            if k < len(now):
                terms.append(2.0 * now[k] + m_now[k])
            if k < len(before):
                terms.append(m_before[k] + c_before[k] - before[k])
            if 0 <= k - 2 < len(before):
                terms.append(tau**2 * before[k - 2])
            if k < len(drive):
                terms.append(drive[k])
            out.append(functools.reduce(lambda one, two: one + two, terms))
        return out, m_now

    def grow(self, sums, before, twice, now):
        kept = self.do.left("e2", sums) if sums else []
        out = [before[k] + 0.5 * twice[k] + now[k] for k in range(len(now))]
        return [out[k] + (sums[k] + kept[k]) if k < len(sums) else out[k] for k in range(len(now))]


def drives(do, flag_ref, own_ref, source_ref, first, last):
    flow = flag_ref[2] > 0
    one = do.left("a", [source_ref[n, 0] for n in range(first, last)])
    two = do.right([source_ref[n, 2] for n in range(first, last)], "c")
    return [
        (
            jnp.where(flow, 0.0, -(tau**2) * (one[n - first] + two[n - first])),
            -(tau**2) * jnp.where(flow, own_ref[n, 1], source_ref[n, 1]),
        )
        for n in range(first, last)
    ]


def driven_kernel(flag_ref, waves_ref, sums_ref, own_ref, source_ref, left_ref, right_ref, out_ref):
    chain = Chain(left_ref, right_ref)
    drive = drives(chain.do, flag_ref, own_ref, source_ref, 0, 2)
    q2 = list(drive[0])
    moved = chain.do.left("m1", q2)
    q3 = [2.0 * q2[k] + moved[k] + drive[0][k] for k in range(2)]
    g4 = chain.grow([], q2, moved, q3)
    q4, _ = chain.advance(q3, q2, drive[1], 4)
    q5, moved = chain.advance(q4, q3, drive[1], 4)
    g6 = chain.grow(g4, q4, moved, q5)
    for first, values, wave in ((0, q4, waves_ref[0]), (4, q5, waves_ref[1]), (8, g6, sums_ref[2])):
        out_ref[first] = values[0] + wave
        for k in range(1, 4):
            out_ref[first + k] = values[k]


def finish_kernel(flag_ref, in_ref, driven_ref, own_ref, source_ref, left_ref, right_ref, out_ref):
    chain = Chain(left_ref, right_ref)
    do = chain.do
    drive = drives(do, flag_ref, own_ref, source_ref, 2, 4)
    q4, q5, g6 = [[driven_ref[first + k] for k in range(4)] for first in (0, 4, 8)]
    q6, _ = chain.advance(q5, q4, drive[0], 6)
    q7, moved = chain.advance(q6, q5, drive[0], 6)
    for k, value in enumerate(chain.grow(g6, q6, moved, q7)):
        out_ref[8 + k] = value
    for k, value in enumerate(chain.advance(q7, q6, drive[1], 8)[0]):
        out_ref[k] = value
    flow = flag_ref[2] > 0

    def arrived(n):
        return [jnp.where(flow, 0.0, source_ref[n, k]) for k in range(3)]

    total = arrived(0)
    for n in (1, 2, 3):
        kept = do.left("e2", total)
        fresh = arrived(n)
        total = [total[k] + kept[k] + fresh[k] for k in range(3)]
    moved = do.left("e1", total)
    begin = [plane(in_ref, i) for i in (3, 9, 10)]
    kept = do.left("e8", begin)
    for i in range(3):
        out_ref[14 + i] = begin[i] + kept[i] + tau * (2.0 * total[i] + moved[i])


def filter_kernel(flag_ref, last_ref, left_ref, right_ref, out_ref):
    do = Products(left_ref, right_ref)
    blocks, _, xs, nz = out_ref.shape

    def emit(place, values):
        fx, fz = do.left("fx", values), do.right(values, "fz")
        for i, value in enumerate(values):
            out_ref[:, place + i] = (value + fx[i] + fz[i]).reshape(blocks, xs, nz)

    def p(k):
        return last_ref[k]

    def h(k):
        return last_ref[8 + k]

    def third(*which):
        return [-tau * value for value in do.right([h(k) for k in which], "c")]

    axial = do.left("ta", [h(0), h(2)])
    depth = third(0, 2)
    emit(0, [p(0), p(2), p(4), last_ref[14] + axial[0], axial[1], last_ref[16] + depth[0], depth[1]])
    emit(7, [last_ref[15], -tau * h(0), -tau * h(2)])

    @pl.when(flag_ref[2] > 0)
    def _():
        axial = do.left("ta", [h(1), h(3), h(5)])
        emit(10, [p(1), p(3), p(5), p(7)] + axial + third(1))
        out_ref[:, 18] = jnp.zeros((blocks, xs, nz), f32)

    @pl.when(flag_ref[2] <= 0)
    def _():
        axial = do.left("ta", [h(4)])
        depth = third(4, 3, 5)
        emit(10, [p(6), axial[0], depth[0], -tau * h(4), depth[1], depth[2]])
        emit(16, [-tau * h(1), -tau * h(3), -tau * h(5)])


def along_y(steps):
    streams, slabs = lax.axis_size("stream"), lax.axis_size("slab")
    count = streams * slabs
    order = order_of(streams)

    def device(y):
        return order[y % streams] * slabs + (y // streams) % slabs

    return [
        (section * count + device(y), section * count + device((y + far) % count))
        for section, far in ((0, steps), (1, 2 * steps))
        for y in range(count)
    ]


def shards(state, source_mask, deriv_x, deriv_z, filter_x, filter_z):
    _, _, xs, own, nz = state.shape
    slabs, streams = lax.axis_size("slab"), lax.axis_size("stream")
    slab = lax.axis_index("slab")
    nx = xs * streams
    upward = [(i, (i + 1) % slabs) for i in range(slabs)]
    downward = [((i + 1) % slabs, i) for i in range(slabs)]
    swap = [(0, 1), (1, 0)]
    inverse = [0] * streams
    for j, stream in enumerate(order_of(streams)):
        inverse[stream] = j
    y = slab * streams + jnp.asarray(inverse, jnp.int32)[lax.axis_index("stream")]
    last_y = slabs * streams - 1
    edges = jnp.stack(
        [slab > 0, slab < slabs - 1, lax.axis_index("section") == 0]
        + [y < last_y, y > 0, y < last_y - 1, y > 1]
    ).astype(f32)
    region = jnp.repeat(source_mask[:, 0].astype(f32), nx // source_mask.shape[0])
    region = jnp.broadcast_to(region[:, None], (nx, nz))

    raw = jnp.swapaxes(state[0], 1, 2)
    reaches = (IN_P, IN_U, IN_V, IN_W)
    from_low = lax.ppermute(
        jnp.concatenate([raw[i, own - reach :] for i, reach in enumerate(reaches)]), "slab", upward
    )
    from_high = lax.ppermute(
        jnp.concatenate([raw[i, :reach] for i, reach in enumerate(reaches)]), "slab", downward
    )
    left, right = call(
        prepare_kernel,
        (
            jax.ShapeDtypeStruct((len(LEFT), nx, 3 * nx), bf16),
            jax.ShapeDtypeStruct((len(RIGHT), 3 * nz, nz), bf16),
        ),
        deriv_x,
        deriv_z.T,
        filter_x,
        filter_z.T,
        flops=10**9,
    )

    def shape(*dims):
        return jax.ShapeDtypeStruct(dims, f32)

    def with_edges(body, out_shape, *args):
        return pl.pallas_call(
            body,
            out_shape=out_shape,
            in_specs=[pl.BlockSpec(memory_space=pltpu.SMEM)]
            + [pl.BlockSpec(memory_space=pltpu.VMEM)] * len(args),
            compiler_params=pltpu.CompilerParams(vmem_limit_bytes=40 * 2**20),
        )(edges, *args)

    spread = with_edges(spread_kernel, shape(own, 13, xs, nz), raw, from_low, from_high, right)
    planes = lax.all_to_all(spread, "stream", split_axis=0, concat_axis=0, tiled=True)
    waves, sums = call(
        waves_kernel, (shape(2, nx, nz), shape(3, nx, nz)), planes, left, right, flops=2 * 10**9
    )
    across = lax.ppermute(sums, "section", swap)
    carried = jnp.where(edges[2] > 0, sums, across)
    up, down = [lax.ppermute(carried, AXES, along_y(steps)) for steps in (-1, 1)]
    far = lax.ppermute(edges[5] * up - edges[6] * down, "section", swap)
    held = call(held_kernel, shape(3, 5, nx, nz), planes, sums, left, right, flops=10**9)
    source = with_edges(
        source_kernel, shape(4, 3, nx, nz), region, planes, held, up, down, far, left, right
    )
    moved = lax.ppermute(source, "section", swap)
    driven = with_edges(driven_kernel, shape(12, nx, nz), waves, sums, source, moved, left, right)
    last = with_edges(finish_kernel, shape(17, nx, nz), planes, driven, source, moved, left, right)
    done = with_edges(filter_kernel, shape(streams, SLOTS, xs, nz), last, left, right)
    back = lax.all_to_all(done, "stream", split_axis=0, concat_axis=0, tiled=True)
    border = OUT_P + OUT_U + OUT_V + OUT_W
    rows = ((OUT_P, 0), (OUT_U, 1), (2, 3))
    odd = with_edges(gather_odd_kernel, shape(sum(own + 2 * reach for reach, _ in rows), xs, nz), back)
    odd = lax.ppermute(odd, "section", swap)
    mine, high, low = with_edges(
        gather_kernel, (shape(4, own, xs, nz), shape(border, xs, nz), shape(border, xs, nz)), back
    )
    starts = (0, OUT_P, OUT_P + OUT_U, OUT_P + OUT_U + OUT_V)
    reaches = (OUT_P, OUT_U, OUT_V, OUT_W)
    lead = 0
    more_high, more_low, more_own = [], [], [jnp.zeros((own, xs, nz), f32)] * 4
    for reach, output in rows:
        part = odd[lead : lead + own + 2 * reach]
        start, room = starts[output], reaches[output]
        more_low.append(jnp.pad(part[:reach], ((start + room - reach, border - start - room), (0, 0), (0, 0))))
        more_high.append(jnp.pad(part[reach + own :], ((start, border - start - reach), (0, 0), (0, 0))))
        more_own[output] = part[reach : reach + own]
        lead += own + 2 * reach
    from_low = lax.ppermute(high + sum(more_high), "slab", upward)
    from_high = lax.ppermute(low + sum(more_low), "slab", downward)
    outs = []
    for i, (start, reach) in enumerate(zip(starts, reaches)):
        from_below = jnp.pad(from_low[start : start + reach], ((0, own - reach), (0, 0), (0, 0)))
        from_above = jnp.pad(from_high[start : start + reach], ((own - reach, 0), (0, 0), (0, 0)))
        outs.append(mine[i] + more_own[i] + from_below + from_above)
    return jnp.swapaxes(jnp.stack(outs), 1, 2)[None]


def solution(mesh):
    placed = (P("section", None, "stream", "slab", None), P(None, "slab"), P(), P(), P(), P())
    return jax.shard_map(
        shards,
        mesh=mesh,
        in_specs=placed,
        out_specs=P("section", None, "stream", "slab", None),
        check_vma=False,
    )
```

```python
import functools

import jax
import jax.numpy as jnp
from jax import lax
from jax.experimental import pallas as pl
from jax.experimental.pallas import tpu as pltpu
from jax.sharding import PartitionSpec as P

mach_number = 0.5
tau = 0.05
filter_weight = 0.25
IN_P, IN_U, IN_V, IN_W = 8, 8, 10, 8
SLOTS = 19
OUT_P, OUT_U, OUT_V, OUT_W = 14, 10, 12, 10
AXES = ("section", "stream", "slab")
LEFT = ("e1", "ta", "m1", "m2", "e2", "a", "e4", "e6", "e8", "fx")
RIGHT = ("c", "cc", "fz")
f32, bf16 = jnp.float32, jnp.bfloat16


def call(body, out_shape, *args, flops=0, scratch=()):
    moved = sum(a.size * a.dtype.itemsize for a in args)
    return pl.pallas_call(
        body,
        out_shape=out_shape,
        scratch_shapes=scratch,
        compiler_params=pltpu.CompilerParams(vmem_limit_bytes=24 * 2**20),
        cost_estimate=pl.CostEstimate(flops=flops, bytes_accessed=moved, transcendentals=0),
    )(*args)


def order_of(count):
    places = []
    for j in range(count):
        step, rung = j // 2, j % 2
        x, y = (rung, step) if step < 4 else (3 - rung, 7 - step)
        places.append(4 * x + y)
    return places


def halves(value):
    high = value.astype(bf16)
    return high, (value - high.astype(f32)).astype(bf16)


def left_form(matrix):
    high, low = halves(matrix)
    return jnp.concatenate([high, high, low], axis=1)


def right_form(matrix):
    high, low = halves(matrix)
    return jnp.concatenate([high, high, low], axis=0)


def times_left(form, planes):
    high, low = halves(jnp.concatenate(planes, axis=1))
    out = jnp.dot(form, jnp.concatenate([high, low, high], axis=0), preferred_element_type=f32)
    width = planes[0].shape[1]
    return [out[:, i * width : (i + 1) * width] for i in range(len(planes))]


def times_right(planes, form):
    high, low = halves(jnp.concatenate(planes, axis=0))
    out = jnp.dot(jnp.concatenate([high, low, high], axis=1), form, preferred_element_type=f32)
    length = planes[0].shape[0]
    return [out[i * length : (i + 1) * length] for i in range(len(planes))]


def prepare_kernel(dx_ref, dzt_ref, fx_ref, fzt_ref, left_ref, right_ref):
    def dot(one, two):
        return jnp.dot(one, two, precision=lax.Precision.HIGHEST, preferred_element_type=f32)

    dx, dzt = dx_ref[...], dzt_ref[...]
    square = dot(dx, dx)
    e1 = -tau * mach_number * dx
    e2 = 2.0 * e1 + (tau * mach_number) ** 2 * square
    e4 = 2.0 * e2 + dot(e2, e2)
    values = {
        "e1": e1,
        "ta": -tau * dx,
        "m1": 2.0 * e1,
        "m2": tau**2 * square - e2,
        "e2": e2,
        "a": dx,
        "e4": e4,
        "e6": e2 + e4 + dot(e2, e4),
        "e8": 2.0 * e4 + dot(e4, e4),
        "fx": filter_weight * fx_ref[...],
    }
    for i, name in enumerate(LEFT):
        left_ref[i] = left_form(values[name])
    others = {"c": dzt, "cc": tau**2 * dot(dzt, dzt), "fz": filter_weight * fzt_ref[...]}
    for i, name in enumerate(RIGHT):
        right_ref[i] = right_form(others[name])


def prepare_later_kernel(after_ref, *refs):
    prepare_kernel(*refs)


def far_kernel(flag_ref, up_ref, down_ref, after_ref, out_ref):
    for n in range(out_ref.shape[0]):
        out_ref[n] = flag_ref[5] * up_ref[n] - flag_ref[6] * down_ref[n]


class Products:
    def __init__(self, left_ref, right_ref):
        self.left_ref, self.right_ref = left_ref, right_ref

    def left(self, name, planes):
        return times_left(self.left_ref[LEFT.index(name)], planes)

    def right(self, planes, name):
        return times_right(planes, self.right_ref[RIGHT.index(name)])


def inside(value, reach, low_ok, high_ok):
    rows = value.shape[0]
    return jnp.concatenate(
        [value[:reach] * low_ok, value[reach : rows - reach], value[rows - reach :] * high_ok], axis=0
    )


def shift_rows(value, steps):
    zeros = jnp.zeros((abs(steps),) + value.shape[1:], f32)
    if steps > 0:
        return jnp.concatenate([value[steps:], zeros], axis=0)
    return jnp.concatenate([zeros, value[:steps]], axis=0)


def slope4(value):
    near = shift_rows(value, 1) - shift_rows(value, -1)
    far = shift_rows(value, 2) - shift_rows(value, -2)
    return (2.0 / 3.0) * near - (1.0 / 12.0) * far


def spread_kernel(edge_ref, raw_ref, low_ref, high_ref, right_ref, out_ref):
    low_ok, high_ok = edge_ref[0], edge_ref[1]
    own, xs, nz = raw_ref.shape[1:]
    order = order_of(own)
    ext = []
    lead = 0
    for i, reach in enumerate((IN_P, IN_U, IN_V, IN_W)):
        ext.append(
            jnp.concatenate(
                [low_ref[lead : lead + reach] * low_ok, raw_ref[i], high_ref[lead : lead + reach] * high_ok],
                axis=0,
            )
        )
        lead += reach

    def twice(value):
        once = inside(slope4(value), IN_P, low_ok, high_ok)
        return inside(slope4(once), IN_P, low_ok, high_ok)

    def put(place, value):
        reach = (value.shape[0] - own) // 2
        for j in range(own):
            out_ref[order[j], place] = value[reach + j]

    def slope2(value):
        return 0.5 * (value[IN_P + 1 : IN_P + 1 + own] - value[IN_P - 1 : IN_P - 1 + own])

    rows = ext[3].shape[0]
    through = times_right([ext[3].reshape(rows * xs, nz)], right_ref[RIGHT.index("c")])[0]
    cut = IN_V - IN_W
    rate = through.reshape(rows, xs, nz) + slope4(ext[2])[cut : cut + rows]
    rate = inside(rate, IN_W, low_ok, high_ok)
    for place, value in ((0, ext[0]), (3, ext[1]), (6, rate)):
        put(place, value)
        value = twice(value)
        put(place + 1, value)
        put(place + 2, twice(value))
    put(9, raw_ref[2])
    put(10, raw_ref[3])
    put(11, slope2(ext[1]))
    put(12, slope2(ext[3]))


class Raiser:
    def __init__(self, edge_ref, back_ref):
        self.low_ok, self.high_ok = edge_ref[0], edge_ref[1]
        self.back_ref = back_ref
        self.own = back_ref.shape[0]
        self.order = order_of(self.own)

    def load(self, slot):
        return jnp.stack([self.back_ref[self.order[j], slot] for j in range(self.own)])

    def total(self, fields):
        total = fields[-1]
        for value in fields[-2::-1]:
            edge = (total.shape[0] - self.own) // 2 + 2
            zeros = jnp.zeros((2,) + total.shape[1:], f32)
            total = slope4(jnp.concatenate([zeros, total, zeros], axis=0))
            centre = total[edge : edge + self.own]
            if value is not None:
                centre = centre + value
            total = jnp.concatenate(
                [total[:edge] * self.low_ok, centre, total[edge + self.own :] * self.high_ok], axis=0
            )
        return total


def gather_odd_kernel(edge_ref, back_ref, out_ref):
    @pl.when(edge_ref[2] > 0)
    def _():
        raiser = Raiser(edge_ref, back_ref)
        p = [raiser.load(10 + i) for i in range(4)]
        u = [raiser.load(14 + i) for i in range(3)]
        lead = 0
        for value in (
            raiser.total([None, p[0], None, p[1], None, p[2], None, p[3]]),
            raiser.total([None, u[0], None, u[1], None, u[2]]),
            raiser.total([None, raiser.load(17)]),
        ):
            out_ref[lead : lead + value.shape[0]] = value
            lead += value.shape[0]

    @pl.when(edge_ref[2] <= 0)
    def _():
        out_ref[...] = jnp.zeros(out_ref.shape, f32)


def gather_kernel(edge_ref, back_ref, own_ref, high_ref, low_ref):
    raiser = Raiser(edge_ref, back_ref)
    own = raiser.own
    sound = 1.0 - edge_ref[2]

    def extra(i):
        return sound * raiser.load(10 + i)

    p = [raiser.load(0), None, raiser.load(1), None, raiser.load(2), None, extra(0)]
    u = [raiser.load(3), None, raiser.load(4), None, extra(1)]
    w = [raiser.load(5), None, raiser.load(6), extra(4), extra(2), extra(5)]
    v = [raiser.load(7), raiser.load(8), extra(6), raiser.load(9), extra(7), extra(3), extra(8)]
    place = 0
    for output, (fields, room) in enumerate(((p, OUT_P), (u, OUT_U), (v, OUT_V), (w, OUT_W))):
        total = raiser.total(fields)
        reach = 2 * (len(fields) - 1)
        own_ref[output] = total[reach : reach + own]
        if room > reach:
            low_ref[place : place + room - reach] = jnp.zeros((room - reach,) + total.shape[1:], f32)
            high_ref[place + reach : place + room] = jnp.zeros((room - reach,) + total.shape[1:], f32)
        low_ref[place + room - reach : place + room] = total[:reach]
        high_ref[place : place + reach] = total[reach + own :]
        place += room


def plane(ref, index):
    blocks, _, xs, nz = ref.shape
    return ref[:, index].reshape(blocks * xs, nz)


def waves_kernel(in_ref, left_ref, right_ref, out_ref, sums_ref):
    do = Products(left_ref, right_ref)
    p0 = [plane(in_ref, i) for i in range(3)]
    u0 = [plane(in_ref, 3 + i) for i in range(3)]

    def advance(now, before):
        count = len(before) - 1
        one = do.left("m1", now[:count])
        two = do.left("m2", before[:count])
        three = do.right(before[:count], "cc")
        return [
            2.0 * now[i] - before[i] + (one[i] + two[i] + three[i] + tau**2 * before[i + 1])
            for i in range(count)
        ], one[0]

    moved = do.left("e1", p0)
    driven = do.left("ta", u0)
    p1 = [p0[i] + (moved[i] + driven[i] - tau * plane(in_ref, 6 + i)) for i in range(3)]
    h2 = p0[0] + moved[0] + p1[0]
    sums_ref[0] = h2
    p2, _ = advance(p1, p0)
    p3, twice = advance(p2, p1)
    h4 = h2 + do.left("e2", [h2])[0] + p2[0] + 0.5 * twice + p3[0]
    sums_ref[1] = h4
    p4, _ = advance(p3, p2)
    p5, twice = advance(p4, p3)
    sums_ref[2] = h4 + do.left("e2", [h4])[0] + p4[0] + 0.5 * twice + p5[0]
    out_ref[0] = p4[0]
    out_ref[1] = p5[0]


def held_kernel(in_ref, sums_ref, left_ref, right_ref, out_ref):
    do = Products(left_ref, right_ref)
    start = [plane(in_ref, i) for i in (3, 10, 11, 12, 9)]
    h = [sums_ref[n] for n in range(3)]
    pull_x = do.left("a", h)
    pull_z = do.right(h, "c")
    for n, growth in enumerate(("e2", "e4", "e6")):
        change = do.left(growth, start)
        out_ref[n, 0] = start[0] + change[0] - tau * pull_x[n]
        out_ref[n, 1] = start[1] + change[1] - tau * pull_z[n]
        for k in (2, 3, 4):
            out_ref[n, k] = start[k] + change[k]


def source_kernel(flag_ref, in_ref, held_ref, up_ref, down_ref, far_ref, left_ref, right_ref, out_ref):
    do = Products(left_ref, right_ref)
    nx, nz = up_ref.shape[1:]
    row = lax.broadcasted_iota(jnp.int32, (nx, nz), 0)
    lane = lax.broadcasted_iota(jnp.int32, (nx, nz), 1)
    blocks = flag_ref.shape[0] - 7
    region = jnp.concatenate([jnp.full((nx // blocks, nz), flag_ref[7 + i], f32) for i in range(blocks)], axis=0)

    def slope_x(value):
        ahead = jnp.where(row == nx - 1, 0.0, pltpu.roll(value, nx - 1, 0))
        behind = jnp.where(row == 0, 0.0, pltpu.roll(value, 1, 0))
        return 0.5 * (ahead - behind)

    def slope_z(value):
        ahead = jnp.where(lane == nz - 1, 0.0, pltpu.roll(value, nz - 1, 1))
        behind = jnp.where(lane == 0, 0.0, pltpu.roll(value, 1, 1))
        return 0.5 * (ahead - behind)

    near = [flag_ref[3] * up_ref[n] - flag_ref[4] * down_ref[n] for n in range(3)]
    half = [0.5 * value for value in near]
    pull_x = do.left("a", half)
    pull_z = do.right(half, "c")
    for n in range(4):
        if n == 0:
            u, w, slope_u, slope_w, v = [plane(in_ref, i) for i in (3, 10, 11, 12, 9)]
        else:
            u, w = held_ref[n - 1, 0], held_ref[n - 1, 1]
            slope_u = held_ref[n - 1, 2] - tau * pull_x[n - 1]
            slope_w = held_ref[n - 1, 3] - tau * pull_z[n - 1]
            far = far_ref[n - 1]
            v = held_ref[n - 1, 4] - tau * ((2.0 / 3.0) * near[n - 1] - (1.0 / 12.0) * far)
        o_x = slope_w - slope_z(v)
        o_y = slope_z(u) - slope_x(w)
        o_z = slope_x(v) - slope_u
        out_ref[n, 0] = region * (o_z * v - o_y * w)
        out_ref[n, 1] = region * (o_x * w - o_z * u)
        out_ref[n, 2] = region * (o_y * u - o_x * v)


class Chain:
    def __init__(self, left_ref, right_ref):
        self.do = Products(left_ref, right_ref)

    def advance(self, now, before, drive, count):
        m_now = self.do.left("m1", now)
        m_before = self.do.left("m2", before)
        c_before = self.do.right(before, "cc")
        out = []
        for k in range(count):
            terms = []
            if k < len(now):
                terms.append(2.0 * now[k] + m_now[k])
            if k < len(before):
                terms.append(m_before[k] + c_before[k] - before[k])
            if 0 <= k - 2 < len(before):
                terms.append(tau**2 * before[k - 2])
            if k < len(drive):
                terms.append(drive[k])
            out.append(functools.reduce(lambda one, two: one + two, terms))
        return out, m_now

    def grow(self, sums, before, twice, now):
        kept = self.do.left("e2", sums) if sums else []
        out = [before[k] + 0.5 * twice[k] + now[k] for k in range(len(now))]
        return [out[k] + (sums[k] + kept[k]) if k < len(sums) else out[k] for k in range(len(now))]


def drives(do, flag_ref, own_ref, source_ref, first, last):
    flow = flag_ref[2] > 0
    one = do.left("a", [source_ref[n, 0] for n in range(first, last)])
    two = do.right([source_ref[n, 2] for n in range(first, last)], "c")
    return [
        (
            jnp.where(flow, 0.0, -(tau**2) * (one[n - first] + two[n - first])),
            -(tau**2) * jnp.where(flow, own_ref[n, 1], source_ref[n, 1]),
        )
        for n in range(first, last)
    ]


def driven_kernel(flag_ref, waves_ref, sums_ref, own_ref, source_ref, left_ref, right_ref, out_ref):
    chain = Chain(left_ref, right_ref)
    drive = drives(chain.do, flag_ref, own_ref, source_ref, 0, 2)
    q2 = list(drive[0])
    moved = chain.do.left("m1", q2)
    q3 = [2.0 * q2[k] + moved[k] + drive[0][k] for k in range(2)]
    g4 = chain.grow([], q2, moved, q3)
    q4, _ = chain.advance(q3, q2, drive[1], 4)
    q5, moved = chain.advance(q4, q3, drive[1], 4)
    g6 = chain.grow(g4, q4, moved, q5)
    for first, values, wave in ((0, q4, waves_ref[0]), (4, q5, waves_ref[1]), (8, g6, sums_ref[2])):
        out_ref[first] = values[0] + wave
        for k in range(1, 4):
            out_ref[first + k] = values[k]


def finish_kernel(flag_ref, in_ref, driven_ref, own_ref, source_ref, left_ref, right_ref, out_ref):
    chain = Chain(left_ref, right_ref)
    do = chain.do
    drive = drives(do, flag_ref, own_ref, source_ref, 2, 4)
    q4, q5, g6 = [[driven_ref[first + k] for k in range(4)] for first in (0, 4, 8)]
    q6, _ = chain.advance(q5, q4, drive[0], 6)
    q7, moved = chain.advance(q6, q5, drive[0], 6)
    for k, value in enumerate(chain.grow(g6, q6, moved, q7)):
        out_ref[8 + k] = value
    for k, value in enumerate(chain.advance(q7, q6, drive[1], 8)[0]):
        out_ref[k] = value
    flow = flag_ref[2] > 0

    def arrived(n):
        return [jnp.where(flow, 0.0, source_ref[n, k]) for k in range(3)]

    total = arrived(0)
    for n in (1, 2, 3):
        kept = do.left("e2", total)
        fresh = arrived(n)
        total = [total[k] + kept[k] + fresh[k] for k in range(3)]
    moved = do.left("e1", total)
    begin = [plane(in_ref, i) for i in (3, 9, 10)]
    kept = do.left("e8", begin)
    for i in range(3):
        out_ref[14 + i] = begin[i] + kept[i] + tau * (2.0 * total[i] + moved[i])


def filter_kernel(flag_ref, last_ref, left_ref, right_ref, out_ref):
    do = Products(left_ref, right_ref)
    blocks, _, xs, nz = out_ref.shape

    def emit(place, values):
        fx, fz = do.left("fx", values), do.right(values, "fz")
        for i, value in enumerate(values):
            out_ref[:, place + i] = (value + fx[i] + fz[i]).reshape(blocks, xs, nz)

    def p(k):
        return last_ref[k]

    def h(k):
        return last_ref[8 + k]

    def third(*which):
        return [-tau * value for value in do.right([h(k) for k in which], "c")]

    axial = do.left("ta", [h(0), h(2)])
    depth = third(0, 2)
    emit(0, [p(0), p(2), p(4), last_ref[14] + axial[0], axial[1], last_ref[16] + depth[0], depth[1]])
    emit(7, [last_ref[15], -tau * h(0), -tau * h(2)])

    @pl.when(flag_ref[2] > 0)
    def _():
        axial = do.left("ta", [h(1), h(3), h(5)])
        emit(10, [p(1), p(3), p(5), p(7)] + axial + third(1))
        out_ref[:, 18] = jnp.zeros((blocks, xs, nz), f32)

    @pl.when(flag_ref[2] <= 0)
    def _():
        axial = do.left("ta", [h(4)])
        depth = third(4, 3, 5)
        emit(10, [p(6), axial[0], depth[0], -tau * h(4), depth[1], depth[2]])
        emit(16, [-tau * h(1), -tau * h(3), -tau * h(5)])


def along_y(steps):
    streams, slabs = lax.axis_size("stream"), lax.axis_size("slab")
    count = streams * slabs
    order = order_of(streams)

    def device(y):
        return order[y % streams] * slabs + (y // streams) % slabs

    return [
        (section * count + device(y), section * count + device((y + far) % count))
        for section, far in ((0, steps), (1, 2 * steps))
        for y in range(count)
    ]


def shards(state, source_mask, deriv_x, deriv_z, filter_x, filter_z):
    _, _, xs, own, nz = state.shape
    slabs, streams = lax.axis_size("slab"), lax.axis_size("stream")
    slab = lax.axis_index("slab")
    nx = xs * streams
    upward = [(i, (i + 1) % slabs) for i in range(slabs)]
    downward = [((i + 1) % slabs, i) for i in range(slabs)]
    swap = [(0, 1), (1, 0)]
    inverse = [0] * streams
    for j, stream in enumerate(order_of(streams)):
        inverse[stream] = j
    y = slab * streams + jnp.asarray(inverse, jnp.int32)[lax.axis_index("stream")]
    last_y = slabs * streams - 1
    flags = [slab > 0, slab < slabs - 1, lax.axis_index("section") == 0]
    flags += [y < last_y, y > 0, y < last_y - 1, y > 1]
    edges = jnp.concatenate([jnp.stack(flags).astype(f32), source_mask[:, 0].astype(f32)])
    raw = jnp.swapaxes(state[0], 1, 2)
    reaches = (IN_P, IN_U, IN_V, IN_W)
    from_low = lax.ppermute(
        jnp.concatenate([raw[i, own - reach :] for i, reach in enumerate(reaches)]), "slab", upward
    )
    from_high = lax.ppermute(
        jnp.concatenate([raw[i, :reach] for i, reach in enumerate(reaches)]), "slab", downward
    )
    forms = (
        jax.ShapeDtypeStruct((len(LEFT), nx, 3 * nx), bf16),
        jax.ShapeDtypeStruct((len(RIGHT), 3 * nz, nz), bf16),
    )
    matrices = (deriv_x, deriv_z.T, filter_x, filter_z.T)
    left, right = call(prepare_kernel, forms, *matrices, flops=10**9)

    def shape(*dims):
        return jax.ShapeDtypeStruct(dims, f32)

    def with_edges(body, out_shape, *args):
        return pl.pallas_call(
            body,
            out_shape=out_shape,
            in_specs=[pl.BlockSpec(memory_space=pltpu.SMEM)]
            + [pl.BlockSpec(memory_space=pltpu.VMEM)] * len(args),
            compiler_params=pltpu.CompilerParams(vmem_limit_bytes=24 * 2**20),
        )(edges, *args)

    spread = with_edges(spread_kernel, shape(own, 13, xs, nz), raw, from_low, from_high, right)
    planes = lax.all_to_all(spread, "stream", split_axis=0, concat_axis=0, tiled=True)
    waves, sums = call(
        waves_kernel, (shape(2, nx, nz), shape(3, nx, nz)), planes, left, right, flops=2 * 10**9
    )
    across = lax.ppermute(sums, "section", swap)
    carried = jnp.where(edges[2] > 0, sums, across)
    up, down = [lax.ppermute(carried, AXES, along_y(steps)) for steps in (-1, 1)]
    vmem, anywhere = pl.BlockSpec(memory_space=pltpu.VMEM), pl.BlockSpec(memory_space=pl.ANY)
    left, right = pl.pallas_call(
        prepare_later_kernel,
        out_shape=forms,
        in_specs=[anywhere] + [vmem] * 4,
        compiler_params=pltpu.CompilerParams(vmem_limit_bytes=24 * 2**20),
        cost_estimate=pl.CostEstimate(flops=10**9, bytes_accessed=8 * 10**6, transcendentals=0),
    )(sums, *matrices)
    held = call(held_kernel, shape(3, 5, nx, nz), planes, sums, left, right, flops=10**9)
    far = pl.pallas_call(
        far_kernel,
        out_shape=shape(3, nx, nz),
        in_specs=[pl.BlockSpec(memory_space=pltpu.SMEM), vmem, vmem, anywhere],
        compiler_params=pltpu.CompilerParams(vmem_limit_bytes=8 * 2**20),
    )(edges, up, down, held)
    far = lax.ppermute(far, "section", swap)
    source = with_edges(
        source_kernel, shape(4, 3, nx, nz), planes, held, up, down, far, left, right
    )
    moved = lax.ppermute(source, "section", swap)
    driven = with_edges(driven_kernel, shape(12, nx, nz), waves, sums, source, moved, left, right)
    last = with_edges(finish_kernel, shape(17, nx, nz), planes, driven, source, moved, left, right)
    done = with_edges(filter_kernel, shape(streams, SLOTS, xs, nz), last, left, right)
    back = lax.all_to_all(done, "stream", split_axis=0, concat_axis=0, tiled=True)
    border = OUT_P + OUT_U + OUT_V + OUT_W
    rows = ((OUT_P, 0), (OUT_U, 1), (2, 3))
    odd = with_edges(gather_odd_kernel, shape(sum(own + 2 * reach for reach, _ in rows), xs, nz), back)
    odd = lax.ppermute(odd, "section", swap)
    mine, high, low = with_edges(
        gather_kernel, (shape(4, own, xs, nz), shape(border, xs, nz), shape(border, xs, nz)), back
    )
    starts = (0, OUT_P, OUT_P + OUT_U, OUT_P + OUT_U + OUT_V)
    reaches = (OUT_P, OUT_U, OUT_V, OUT_W)
    lead = 0
    more_high, more_low, more_own = [], [], [jnp.zeros((own, xs, nz), f32)] * 4
    for reach, output in rows:
        part = odd[lead : lead + own + 2 * reach]
        start, room = starts[output], reaches[output]
        more_low.append(jnp.pad(part[:reach], ((start + room - reach, border - start - room), (0, 0), (0, 0))))
        more_high.append(jnp.pad(part[reach + own :], ((start, border - start - reach), (0, 0), (0, 0))))
        more_own[output] = part[reach : reach + own]
        lead += own + 2 * reach
    from_low = lax.ppermute(high + sum(more_high), "slab", upward)
    from_high = lax.ppermute(low + sum(more_low), "slab", downward)
    outs = []
    for i, (start, reach) in enumerate(zip(starts, reaches)):
        from_below = jnp.pad(from_low[start : start + reach], ((0, own - reach), (0, 0), (0, 0)))
        from_above = jnp.pad(from_high[start : start + reach], ((own - reach, 0), (0, 0), (0, 0)))
        outs.append(mine[i] + more_own[i] + from_below + from_above)
    return jnp.swapaxes(jnp.stack(outs), 1, 2)[None]


def solution(mesh):
    placed = (P("section", None, "stream", "slab", None), P(None, "slab"), P(), P(), P(), P())
    return jax.shard_map(
        shards,
        mesh=mesh,
        in_specs=placed,
        out_specs=P("section", None, "stream", "slab", None),
        check_vma=False,
    )
```

```python
import functools

import jax
import jax.numpy as jnp
from jax import lax
from jax.experimental import pallas as pl
from jax.experimental.pallas import tpu as pltpu
from jax.sharding import PartitionSpec as P

mach_number = 0.5
tau = 0.05
filter_weight = 0.25
IN_P, IN_U, IN_V, IN_W = 8, 8, 10, 8
SLOTS = 19
OUT_P, OUT_U, OUT_V, OUT_W = 14, 10, 12, 10
AXES = ("section", "stream", "slab")
LEFT = ("e1", "ta", "m1", "m2", "e2", "a", "e4", "e6", "e8", "fx")
RIGHT = ("c", "cc", "fz")
f32, bf16 = jnp.float32, jnp.bfloat16


def call(body, out_shape, *args, flops=0, scratch=()):
    moved = sum(a.size * a.dtype.itemsize for a in args)
    return pl.pallas_call(
        body,
        out_shape=out_shape,
        scratch_shapes=scratch,
        compiler_params=pltpu.CompilerParams(vmem_limit_bytes=24 * 2**20),
        cost_estimate=pl.CostEstimate(flops=flops, bytes_accessed=moved, transcendentals=0),
    )(*args)


def order_of(count):
    places = []
    for j in range(count):
        step, rung = j // 2, j % 2
        x, y = (rung, step) if step < 4 else (3 - rung, 7 - step)
        places.append(4 * x + y)
    return places


def halves(value):
    high = value.astype(bf16)
    return high, (value - high.astype(f32)).astype(bf16)


def left_form(matrix):
    high, low = halves(matrix)
    return jnp.concatenate([high, high, low], axis=1)


def right_form(matrix):
    high, low = halves(matrix)
    return jnp.concatenate([high, high, low], axis=0)


def times_left(form, high, low):
    high, low = jnp.concatenate(high, axis=1), jnp.concatenate(low, axis=1)
    return jnp.dot(form, jnp.concatenate([high, low, high], axis=0), preferred_element_type=f32)


def times_right(high, low, form):
    high, low = jnp.concatenate(high, axis=0), jnp.concatenate(low, axis=0)
    return jnp.dot(jnp.concatenate([high, low, high], axis=1), form, preferred_element_type=f32)


def prepare_kernel(dx_ref, dzt_ref, fx_ref, fzt_ref, left_ref, right_ref):
    def dot(one, two):
        return jnp.dot(one, two, precision=lax.Precision.HIGHEST, preferred_element_type=f32)

    dx, dzt = dx_ref[...], dzt_ref[...]
    square = dot(dx, dx)
    e1 = -tau * mach_number * dx
    e2 = 2.0 * e1 + (tau * mach_number) ** 2 * square
    e4 = 2.0 * e2 + dot(e2, e2)
    values = {
        "e1": e1,
        "ta": -tau * dx,
        "m1": 2.0 * e1,
        "m2": tau**2 * square - e2,
        "e2": e2,
        "a": dx,
        "e4": e4,
        "e6": e2 + e4 + dot(e2, e4),
        "e8": 2.0 * e4 + dot(e4, e4),
        "fx": filter_weight * fx_ref[...],
    }
    for i, name in enumerate(LEFT):
        left_ref[i] = left_form(values[name])
    others = {"c": dzt, "cc": tau**2 * dot(dzt, dzt), "fz": filter_weight * fzt_ref[...]}
    for i, name in enumerate(RIGHT):
        right_ref[i] = right_form(others[name])


def prepare_later_kernel(after_ref, *refs):
    prepare_kernel(*refs)


def far_kernel(flag_ref, up_ref, down_ref, after_ref, out_ref):
    for n in range(out_ref.shape[0]):
        out_ref[n] = flag_ref[5] * up_ref[n] - flag_ref[6] * down_ref[n]


class Products:
    def __init__(self, left_ref, right_ref):
        self.left_ref, self.right_ref = left_ref, right_ref
        self.split = {}

    def halves(self, planes):
        for value in planes:
            if id(value) not in self.split:
                self.split[id(value)] = (value, *halves(value))
        found = [self.split[id(value)] for value in planes]
        return [one[1] for one in found], [one[2] for one in found]

    def left(self, name, planes):
        out = times_left(self.left_ref[LEFT.index(name)], *self.halves(planes))
        width = planes[0].shape[1]
        return [out[:, i * width : (i + 1) * width] for i in range(len(planes))]

    def right(self, planes, name):
        out = times_right(*self.halves(planes), self.right_ref[RIGHT.index(name)])
        length = planes[0].shape[0]
        return [out[i * length : (i + 1) * length] for i in range(len(planes))]


def inside(value, reach, low_ok, high_ok):
    rows = value.shape[0]
    return jnp.concatenate(
        [value[:reach] * low_ok, value[reach : rows - reach], value[rows - reach :] * high_ok], axis=0
    )


def shift_rows(value, steps):
    zeros = jnp.zeros((abs(steps),) + value.shape[1:], f32)
    if steps > 0:
        return jnp.concatenate([value[steps:], zeros], axis=0)
    return jnp.concatenate([zeros, value[:steps]], axis=0)


def slope4(value):
    near = shift_rows(value, 1) - shift_rows(value, -1)
    far = shift_rows(value, 2) - shift_rows(value, -2)
    return (2.0 / 3.0) * near - (1.0 / 12.0) * far


def spread_kernel(edge_ref, raw_ref, low_ref, high_ref, right_ref, out_ref):
    low_ok, high_ok = edge_ref[0], edge_ref[1]
    own, xs, nz = raw_ref.shape[1:]
    order = order_of(own)
    ext = []
    lead = 0
    for i, reach in enumerate((IN_P, IN_U, IN_V, IN_W)):
        ext.append(
            jnp.concatenate(
                [low_ref[lead : lead + reach] * low_ok, raw_ref[i], high_ref[lead : lead + reach] * high_ok],
                axis=0,
            )
        )
        lead += reach

    def twice(value):
        once = inside(slope4(value), IN_P, low_ok, high_ok)
        return inside(slope4(once), IN_P, low_ok, high_ok)

    def put(place, value):
        reach = (value.shape[0] - own) // 2
        for j in range(own):
            out_ref[order[j], place] = value[reach + j]

    def slope2(value):
        return 0.5 * (value[IN_P + 1 : IN_P + 1 + own] - value[IN_P - 1 : IN_P - 1 + own])

    rows = ext[3].shape[0]
    high, low = halves(ext[3].reshape(rows * xs, nz))
    through = times_right([high], [low], right_ref[RIGHT.index("c")])
    cut = IN_V - IN_W
    rate = through.reshape(rows, xs, nz) + slope4(ext[2])[cut : cut + rows]
    rate = inside(rate, IN_W, low_ok, high_ok)
    for place, value in ((0, ext[0]), (3, ext[1]), (6, rate)):
        put(place, value)
        value = twice(value)
        put(place + 1, value)
        put(place + 2, twice(value))
    put(9, raw_ref[2])
    put(10, raw_ref[3])
    put(11, slope2(ext[1]))
    put(12, slope2(ext[3]))


class Raiser:
    def __init__(self, edge_ref, back_ref):
        self.low_ok, self.high_ok = edge_ref[0], edge_ref[1]
        self.back_ref = back_ref
        self.own = back_ref.shape[0]
        self.order = order_of(self.own)

    def load(self, slot):
        return jnp.stack([self.back_ref[self.order[j], slot] for j in range(self.own)])

    def total(self, fields):
        total = fields[-1]
        for value in fields[-2::-1]:
            edge = (total.shape[0] - self.own) // 2 + 2
            zeros = jnp.zeros((2,) + total.shape[1:], f32)
            total = slope4(jnp.concatenate([zeros, total, zeros], axis=0))
            centre = total[edge : edge + self.own]
            if value is not None:
                centre = centre + value
            total = jnp.concatenate(
                [total[:edge] * self.low_ok, centre, total[edge + self.own :] * self.high_ok], axis=0
            )
        return total


def gather_odd_kernel(edge_ref, back_ref, out_ref):
    @pl.when(edge_ref[2] > 0)
    def _():
        raiser = Raiser(edge_ref, back_ref)
        p = [raiser.load(10 + i) for i in range(4)]
        u = [raiser.load(14 + i) for i in range(3)]
        lead = 0
        for value in (
            raiser.total([None, p[0], None, p[1], None, p[2], None, p[3]]),
            raiser.total([None, u[0], None, u[1], None, u[2]]),
            raiser.total([None, raiser.load(17)]),
        ):
            out_ref[lead : lead + value.shape[0]] = value
            lead += value.shape[0]

    @pl.when(edge_ref[2] <= 0)
    def _():
        out_ref[...] = jnp.zeros(out_ref.shape, f32)


def gather_kernel(edge_ref, back_ref, own_ref, high_ref, low_ref):
    raiser = Raiser(edge_ref, back_ref)
    own = raiser.own
    sound = 1.0 - edge_ref[2]

    def extra(i):
        return sound * raiser.load(10 + i)

    p = [raiser.load(0), None, raiser.load(1), None, raiser.load(2), None, extra(0)]
    u = [raiser.load(3), None, raiser.load(4), None, extra(1)]
    w = [raiser.load(5), None, raiser.load(6), extra(4), extra(2), extra(5)]
    v = [raiser.load(7), raiser.load(8), extra(6), raiser.load(9), extra(7), extra(3), extra(8)]
    place = 0
    for output, (fields, room) in enumerate(((p, OUT_P), (u, OUT_U), (v, OUT_V), (w, OUT_W))):
        total = raiser.total(fields)
        reach = 2 * (len(fields) - 1)
        own_ref[output] = total[reach : reach + own]
        if room > reach:
            low_ref[place : place + room - reach] = jnp.zeros((room - reach,) + total.shape[1:], f32)
            high_ref[place + reach : place + room] = jnp.zeros((room - reach,) + total.shape[1:], f32)
        low_ref[place + room - reach : place + room] = total[:reach]
        high_ref[place : place + reach] = total[reach + own :]
        place += room


def plane(ref, index):
    blocks, _, xs, nz = ref.shape
    return ref[:, index].reshape(blocks * xs, nz)


def waves_kernel(in_ref, left_ref, right_ref, out_ref, sums_ref):
    do = Products(left_ref, right_ref)
    p0 = [plane(in_ref, i) for i in range(3)]
    u0 = [plane(in_ref, 3 + i) for i in range(3)]

    def advance(now, before):
        count = len(before) - 1
        one = do.left("m1", now[:count])
        two = do.left("m2", before[:count])
        three = do.right(before[:count], "cc")
        return [
            2.0 * now[i] - before[i] + (one[i] + two[i] + three[i] + tau**2 * before[i + 1])
            for i in range(count)
        ], one[0]

    moved = do.left("e1", p0)
    driven = do.left("ta", u0)
    p1 = [p0[i] + (moved[i] + driven[i] - tau * plane(in_ref, 6 + i)) for i in range(3)]
    h2 = p0[0] + moved[0] + p1[0]
    sums_ref[0] = h2
    p2, _ = advance(p1, p0)
    p3, twice = advance(p2, p1)
    h4 = h2 + do.left("e2", [h2])[0] + p2[0] + 0.5 * twice + p3[0]
    sums_ref[1] = h4
    p4, _ = advance(p3, p2)
    p5, twice = advance(p4, p3)
    sums_ref[2] = h4 + do.left("e2", [h4])[0] + p4[0] + 0.5 * twice + p5[0]
    out_ref[0] = p4[0]
    out_ref[1] = p5[0]


def held_kernel(in_ref, sums_ref, left_ref, right_ref, out_ref, later_ref):
    do = Products(left_ref, right_ref)
    start = [plane(in_ref, i) for i in (3, 10, 11, 12, 9)]
    h = [sums_ref[n] for n in range(3)]
    pull_x = do.left("a", h)
    pull_z = do.right(h, "c")
    begin = [start[0], start[4], start[1]]
    kept = do.left("e8", begin)
    for i in range(3):
        later_ref[i] = begin[i] + kept[i]
    for n, growth in enumerate(("e2", "e4", "e6")):
        change = do.left(growth, start)
        out_ref[n, 0] = start[0] + change[0] - tau * pull_x[n]
        out_ref[n, 1] = start[1] + change[1] - tau * pull_z[n]
        for k in (2, 3, 4):
            out_ref[n, k] = start[k] + change[k]


def source_kernel(flag_ref, in_ref, held_ref, up_ref, down_ref, far_ref, left_ref, right_ref, out_ref):
    do = Products(left_ref, right_ref)
    nx, nz = up_ref.shape[1:]
    row = lax.broadcasted_iota(jnp.int32, (nx, nz), 0)
    lane = lax.broadcasted_iota(jnp.int32, (nx, nz), 1)
    blocks = flag_ref.shape[0] - 7
    region = jnp.concatenate([jnp.full((nx // blocks, nz), flag_ref[7 + i], f32) for i in range(blocks)], axis=0)

    def slope_x(value):
        ahead = jnp.where(row == nx - 1, 0.0, pltpu.roll(value, nx - 1, 0))
        behind = jnp.where(row == 0, 0.0, pltpu.roll(value, 1, 0))
        return 0.5 * (ahead - behind)

    def slope_z(value):
        ahead = jnp.where(lane == nz - 1, 0.0, pltpu.roll(value, nz - 1, 1))
        behind = jnp.where(lane == 0, 0.0, pltpu.roll(value, 1, 1))
        return 0.5 * (ahead - behind)

    near = [flag_ref[3] * up_ref[n] - flag_ref[4] * down_ref[n] for n in range(3)]
    half = [0.5 * value for value in near]
    pull_x = do.left("a", half)
    pull_z = do.right(half, "c")
    for n in range(4):
        if n == 0:
            u, w, slope_u, slope_w, v = [plane(in_ref, i) for i in (3, 10, 11, 12, 9)]
        else:
            u, w = held_ref[n - 1, 0], held_ref[n - 1, 1]
            slope_u = held_ref[n - 1, 2] - tau * pull_x[n - 1]
            slope_w = held_ref[n - 1, 3] - tau * pull_z[n - 1]
            far = far_ref[n - 1]
            v = held_ref[n - 1, 4] - tau * ((2.0 / 3.0) * near[n - 1] - (1.0 / 12.0) * far)
        o_x = slope_w - slope_z(v)
        o_y = slope_z(u) - slope_x(w)
        o_z = slope_x(v) - slope_u
        out_ref[n, 0] = region * (o_z * v - o_y * w)
        out_ref[n, 1] = region * (o_x * w - o_z * u)
        out_ref[n, 2] = region * (o_y * u - o_x * v)


class Chain:
    def __init__(self, left_ref, right_ref):
        self.do = Products(left_ref, right_ref)

    def advance(self, now, before, drive, count):
        m_now = self.do.left("m1", now)
        m_before = self.do.left("m2", before)
        c_before = self.do.right(before, "cc")
        out = []
        for k in range(count):
            terms = []
            if k < len(now):
                terms.append(2.0 * now[k] + m_now[k])
            if k < len(before):
                terms.append(m_before[k] + c_before[k] - before[k])
            if 0 <= k - 2 < len(before):
                terms.append(tau**2 * before[k - 2])
            if k < len(drive):
                terms.append(drive[k])
            out.append(functools.reduce(lambda one, two: one + two, terms))
        return out, m_now

    def grow(self, sums, before, twice, now):
        kept = self.do.left("e2", sums) if sums else []
        out = [before[k] + 0.5 * twice[k] + now[k] for k in range(len(now))]
        return [out[k] + (sums[k] + kept[k]) if k < len(sums) else out[k] for k in range(len(now))]


def drives(do, flag_ref, own_ref, source_ref, first, last):
    flow = flag_ref[2] > 0
    one = do.left("a", [source_ref[n, 0] for n in range(first, last)])
    two = do.right([source_ref[n, 2] for n in range(first, last)], "c")
    return [
        (
            jnp.where(flow, 0.0, -(tau**2) * (one[n - first] + two[n - first])),
            -(tau**2) * jnp.where(flow, own_ref[n, 1], source_ref[n, 1]),
        )
        for n in range(first, last)
    ]


def driven_kernel(flag_ref, waves_ref, sums_ref, own_ref, source_ref, left_ref, right_ref, out_ref):
    chain = Chain(left_ref, right_ref)
    drive = drives(chain.do, flag_ref, own_ref, source_ref, 0, 2)
    q2 = list(drive[0])
    moved = chain.do.left("m1", q2)
    q3 = [2.0 * q2[k] + moved[k] + drive[0][k] for k in range(2)]
    g4 = chain.grow([], q2, moved, q3)
    q4, _ = chain.advance(q3, q2, drive[1], 4)
    q5, moved = chain.advance(q4, q3, drive[1], 4)
    g6 = chain.grow(g4, q4, moved, q5)
    for first, values, wave in ((0, q4, waves_ref[0]), (4, q5, waves_ref[1]), (8, g6, sums_ref[2])):
        out_ref[first] = values[0] + wave
        for k in range(1, 4):
            out_ref[first + k] = values[k]


def finish_kernel(flag_ref, later_ref, driven_ref, own_ref, source_ref, left_ref, right_ref, out_ref):
    chain = Chain(left_ref, right_ref)
    do = chain.do
    drive = drives(do, flag_ref, own_ref, source_ref, 2, 4)
    q4, q5, g6 = [[driven_ref[first + k] for k in range(4)] for first in (0, 4, 8)]
    q6, _ = chain.advance(q5, q4, drive[0], 6)
    q7, moved = chain.advance(q6, q5, drive[0], 6)
    for k, value in enumerate(chain.grow(g6, q6, moved, q7)):
        out_ref[8 + k] = value
    for k, value in enumerate(chain.advance(q7, q6, drive[1], 8)[0]):
        out_ref[k] = value
    flow = flag_ref[2] > 0

    def arrived(n):
        return [jnp.where(flow, 0.0, source_ref[n, k]) for k in range(3)]

    total = arrived(0)
    for n in (1, 2, 3):
        kept = do.left("e2", total)
        fresh = arrived(n)
        total = [total[k] + kept[k] + fresh[k] for k in range(3)]
    moved = do.left("e1", total)
    for i in range(3):
        out_ref[14 + i] = later_ref[i] + tau * (2.0 * total[i] + moved[i])


def filter_kernel(flag_ref, last_ref, left_ref, right_ref, out_ref):
    do = Products(left_ref, right_ref)
    blocks, _, xs, nz = out_ref.shape

    def emit(place, values):
        fx, fz = do.left("fx", values), do.right(values, "fz")
        for i, value in enumerate(values):
            out_ref[:, place + i] = (value + fx[i] + fz[i]).reshape(blocks, xs, nz)

    loaded = {}

    def load(k):
        if k not in loaded:
            loaded[k] = last_ref[k]
        return loaded[k]

    def p(k):
        return last_ref[k]

    def h(k):
        return load(8 + k)

    def third(*which):
        return [-tau * value for value in do.right([h(k) for k in which], "c")]

    axial = do.left("ta", [h(0), h(2)])
    depth = third(0, 2)
    emit(0, [p(0), p(2), p(4), last_ref[14] + axial[0], axial[1], last_ref[16] + depth[0], depth[1]])
    emit(7, [last_ref[15], -tau * h(0), -tau * h(2)])

    @pl.when(flag_ref[2] > 0)
    def _():
        loaded.clear()
        do.split.clear()
        axial = do.left("ta", [h(1), h(3), h(5)])
        emit(10, [p(1), p(3), p(5), p(7)] + axial + third(1))
        out_ref[:, 18] = jnp.zeros((blocks, xs, nz), f32)

    @pl.when(flag_ref[2] <= 0)
    def _():
        loaded.clear()
        do.split.clear()
        axial = do.left("ta", [h(4)])
        depth = third(4, 3, 5)
        emit(10, [p(6), axial[0], depth[0], -tau * h(4), depth[1], depth[2]])
        emit(16, [-tau * h(1), -tau * h(3), -tau * h(5)])


def along_y(steps):
    streams, slabs = lax.axis_size("stream"), lax.axis_size("slab")
    count = streams * slabs
    order = order_of(streams)

    def device(y):
        return order[y % streams] * slabs + (y // streams) % slabs

    return [
        (section * count + device(y), section * count + device((y + far) % count))
        for section, far in ((0, steps), (1, 2 * steps))
        for y in range(count)
    ]


def shards(state, source_mask, deriv_x, deriv_z, filter_x, filter_z):
    _, _, xs, own, nz = state.shape
    slabs, streams = lax.axis_size("slab"), lax.axis_size("stream")
    slab = lax.axis_index("slab")
    nx = xs * streams
    upward = [(i, (i + 1) % slabs) for i in range(slabs)]
    downward = [((i + 1) % slabs, i) for i in range(slabs)]
    swap = [(0, 1), (1, 0)]
    inverse = [0] * streams
    for j, stream in enumerate(order_of(streams)):
        inverse[stream] = j
    y = slab * streams + jnp.asarray(inverse, jnp.int32)[lax.axis_index("stream")]
    last_y = slabs * streams - 1
    flags = [slab > 0, slab < slabs - 1, lax.axis_index("section") == 0]
    flags += [y < last_y, y > 0, y < last_y - 1, y > 1]
    edges = jnp.concatenate([jnp.stack(flags).astype(f32), source_mask[:, 0].astype(f32)])
    reaches = (IN_P, IN_U, IN_V, IN_W)
    top = jnp.concatenate([state[0, i, :, own - reach :] for i, reach in enumerate(reaches)], axis=1)
    bottom = jnp.concatenate([state[0, i, :, :reach] for i, reach in enumerate(reaches)], axis=1)
    from_low = jnp.swapaxes(lax.ppermute(top, "slab", upward), 0, 1)
    from_high = jnp.swapaxes(lax.ppermute(bottom, "slab", downward), 0, 1)
    raw = jnp.swapaxes(state[0], 1, 2)
    forms = (
        jax.ShapeDtypeStruct((len(LEFT), nx, 3 * nx), bf16),
        jax.ShapeDtypeStruct((len(RIGHT), 3 * nz, nz), bf16),
    )
    matrices = (deriv_x, deriv_z.T, filter_x, filter_z.T)
    left, right = call(prepare_kernel, forms, *matrices, flops=10**9)

    def shape(*dims):
        return jax.ShapeDtypeStruct(dims, f32)

    def with_edges(body, out_shape, *args):
        return pl.pallas_call(
            body,
            out_shape=out_shape,
            in_specs=[pl.BlockSpec(memory_space=pltpu.SMEM)]
            + [pl.BlockSpec(memory_space=pltpu.VMEM)] * len(args),
            compiler_params=pltpu.CompilerParams(vmem_limit_bytes=24 * 2**20),
        )(edges, *args)

    spread = with_edges(spread_kernel, shape(own, 13, xs, nz), raw, from_low, from_high, right)
    planes = lax.all_to_all(spread, "stream", split_axis=0, concat_axis=0, tiled=True)
    waves, sums = call(
        waves_kernel, (shape(2, nx, nz), shape(3, nx, nz)), planes, left, right, flops=2 * 10**9
    )
    across = lax.ppermute(sums, "section", swap)
    carried = jnp.where(edges[2] > 0, sums, across)
    up, down = [lax.ppermute(carried, AXES, along_y(steps)) for steps in (-1, 1)]
    vmem, anywhere = pl.BlockSpec(memory_space=pltpu.VMEM), pl.BlockSpec(memory_space=pl.ANY)
    left, right = pl.pallas_call(
        prepare_later_kernel,
        out_shape=forms,
        in_specs=[anywhere] + [vmem] * 4,
        compiler_params=pltpu.CompilerParams(vmem_limit_bytes=24 * 2**20),
        cost_estimate=pl.CostEstimate(flops=10**9, bytes_accessed=8 * 10**6, transcendentals=0),
    )(sums, *matrices)
    held, later = call(
        held_kernel, (shape(3, 5, nx, nz), shape(3, nx, nz)), planes, sums, left, right, flops=10**9)
    far = pl.pallas_call(
        far_kernel,
        out_shape=shape(3, nx, nz),
        in_specs=[pl.BlockSpec(memory_space=pltpu.SMEM), vmem, vmem, anywhere],
        compiler_params=pltpu.CompilerParams(vmem_limit_bytes=8 * 2**20),
    )(edges, up, down, held)
    far = lax.ppermute(far, "section", swap)
    source = with_edges(
        source_kernel, shape(4, 3, nx, nz), planes, held, up, down, far, left, right
    )
    moved = lax.ppermute(source, "section", swap)
    driven = with_edges(driven_kernel, shape(12, nx, nz), waves, sums, source, moved, left, right)
    last = with_edges(finish_kernel, shape(17, nx, nz), later, driven, source, moved, left, right)
    done = with_edges(filter_kernel, shape(streams, SLOTS, xs, nz), last, left, right)
    back = lax.all_to_all(done, "stream", split_axis=0, concat_axis=0, tiled=True)
    border = OUT_P + OUT_U + OUT_V + OUT_W
    rows = ((OUT_P, 0), (OUT_U, 1), (2, 3))
    odd = with_edges(gather_odd_kernel, shape(sum(own + 2 * reach for reach, _ in rows), xs, nz), back)
    odd = lax.ppermute(odd, "section", swap)
    mine, high, low = with_edges(
        gather_kernel, (shape(4, own, xs, nz), shape(border, xs, nz), shape(border, xs, nz)), back
    )
    starts = (0, OUT_P, OUT_P + OUT_U, OUT_P + OUT_U + OUT_V)
    reaches = (OUT_P, OUT_U, OUT_V, OUT_W)
    lead = 0
    more_high, more_low, more_own = [], [], [jnp.zeros((own, xs, nz), f32)] * 4
    for reach, output in rows:
        part = odd[lead : lead + own + 2 * reach]
        start, room = starts[output], reaches[output]
        more_low.append(jnp.pad(part[:reach], ((start + room - reach, border - start - room), (0, 0), (0, 0))))
        more_high.append(jnp.pad(part[reach + own :], ((start, border - start - reach), (0, 0), (0, 0))))
        more_own[output] = part[reach : reach + own]
        lead += own + 2 * reach
    from_low = lax.ppermute(high + sum(more_high), "slab", upward)
    from_high = lax.ppermute(low + sum(more_low), "slab", downward)
    outs = []
    for i, (start, reach) in enumerate(zip(starts, reaches)):
        from_below = jnp.pad(from_low[start : start + reach], ((0, own - reach), (0, 0), (0, 0)))
        from_above = jnp.pad(from_high[start : start + reach], ((own - reach, 0), (0, 0), (0, 0)))
        outs.append(mine[i] + more_own[i] + from_below + from_above)
    return jnp.swapaxes(jnp.stack(outs), 1, 2)[None]


def solution(mesh):
    placed = (P("section", None, "stream", "slab", None), P(None, "slab"), P(), P(), P(), P())
    return jax.shard_map(
        shards,
        mesh=mesh,
        in_specs=placed,
        out_specs=P("section", None, "stream", "slab", None),
        check_vma=False,
    )
```

```python
import functools

import jax
import jax.numpy as jnp
from jax import lax
from jax.experimental import pallas as pl
from jax.experimental.pallas import tpu as pltpu
from jax.sharding import PartitionSpec as P

mach_number = 0.5
tau = 0.05
filter_weight = 0.25
IN_P, IN_U, IN_V, IN_W = 8, 8, 10, 8
SLOTS = 19
OUT_P, OUT_U, OUT_V, OUT_W = 14, 10, 12, 10
AXES = ("section", "stream", "slab")
LEFT = ("e1", "ta", "m1", "m2", "e2", "a", "e4", "e6", "e8", "fx")
RIGHT = ("c", "cc", "fz")
f32, bf16 = jnp.float32, jnp.bfloat16


def call(body, out_shape, *args, flops=0, scratch=()):
    moved = sum(a.size * a.dtype.itemsize for a in args)
    return pl.pallas_call(
        body,
        out_shape=out_shape,
        scratch_shapes=scratch,
        compiler_params=pltpu.CompilerParams(vmem_limit_bytes=24 * 2**20),
        cost_estimate=pl.CostEstimate(flops=flops, bytes_accessed=moved, transcendentals=0),
    )(*args)


def order_of(count):
    places = []
    for j in range(count):
        step, rung = j // 2, j % 2
        x, y = (rung, step) if step < 4 else (3 - rung, 7 - step)
        places.append(4 * x + y)
    return places


def halves(value):
    high = value.astype(bf16)
    return high, (value - high.astype(f32)).astype(bf16)


def left_form(matrix):
    high, low = halves(matrix)
    return jnp.concatenate([high, high, low], axis=1)


def right_form(matrix):
    high, low = halves(matrix)
    return jnp.concatenate([high, high, low], axis=0)


def times_left(form, high, low):
    high, low = jnp.concatenate(high, axis=1), jnp.concatenate(low, axis=1)
    return jnp.dot(form, jnp.concatenate([high, low, high], axis=0), preferred_element_type=f32)


def times_right(high, low, form):
    high, low = jnp.concatenate(high, axis=0), jnp.concatenate(low, axis=0)
    return jnp.dot(jnp.concatenate([high, low, high], axis=1), form, preferred_element_type=f32)


def prepare_kernel(dx_ref, dzt_ref, fx_ref, fzt_ref, left_ref, right_ref):
    def dot(one, two):
        return jnp.dot(one, two, precision=lax.Precision.HIGHEST, preferred_element_type=f32)

    dx, dzt = dx_ref[...], dzt_ref[...]
    square = dot(dx, dx)
    e1 = -tau * mach_number * dx
    e2 = 2.0 * e1 + (tau * mach_number) ** 2 * square
    e4 = 2.0 * e2 + dot(e2, e2)
    values = {
        "e1": e1,
        "ta": -tau * dx,
        "m1": 2.0 * e1,
        "m2": tau**2 * square - e2,
        "e2": e2,
        "a": dx,
        "e4": e4,
        "e6": e2 + e4 + dot(e2, e4),
        "e8": 2.0 * e4 + dot(e4, e4),
        "fx": filter_weight * fx_ref[...],
    }
    for i, name in enumerate(LEFT):
        left_ref[i] = left_form(values[name])
    others = {"c": dzt, "cc": tau**2 * dot(dzt, dzt), "fz": filter_weight * fzt_ref[...]}
    for i, name in enumerate(RIGHT):
        right_ref[i] = right_form(others[name])


def prepare_later_kernel(after_ref, *refs):
    prepare_kernel(*refs)


def far_kernel(flag_ref, up_ref, down_ref, after_ref, later_ref, out_ref):
    for n in range(out_ref.shape[0]):
        out_ref[n] = flag_ref[5] * up_ref[n] - flag_ref[6] * down_ref[n]


class Products:
    def __init__(self, left_ref, right_ref):
        self.left_ref, self.right_ref = left_ref, right_ref
        self.split = {}

    def halves(self, planes):
        for value in planes:
            if id(value) not in self.split:
                self.split[id(value)] = (value, *halves(value))
        found = [self.split[id(value)] for value in planes]
        return [one[1] for one in found], [one[2] for one in found]

    def left(self, name, planes):
        out = times_left(self.left_ref[LEFT.index(name)], *self.halves(planes))
        width = planes[0].shape[1]
        return [out[:, i * width : (i + 1) * width] for i in range(len(planes))]

    def right(self, planes, name):
        out = times_right(*self.halves(planes), self.right_ref[RIGHT.index(name)])
        length = planes[0].shape[0]
        return [out[i * length : (i + 1) * length] for i in range(len(planes))]


def inside(value, reach, low_ok, high_ok):
    rows = value.shape[0]
    return jnp.concatenate(
        [value[:reach] * low_ok, value[reach : rows - reach], value[rows - reach :] * high_ok], axis=0
    )


def shift_rows(value, steps):
    zeros = jnp.zeros((abs(steps),) + value.shape[1:], f32)
    if steps > 0:
        return jnp.concatenate([value[steps:], zeros], axis=0)
    return jnp.concatenate([zeros, value[:steps]], axis=0)


def slope4(value):
    near = shift_rows(value, 1) - shift_rows(value, -1)
    far = shift_rows(value, 2) - shift_rows(value, -2)
    return (2.0 / 3.0) * near - (1.0 / 12.0) * far


def spread_kernel(edge_ref, raw_ref, low_ref, high_ref, right_ref, out_ref):
    low_ok, high_ok = edge_ref[0], edge_ref[1]
    own, xs, nz = raw_ref.shape[1:]
    order = order_of(own)
    ext = []
    lead = 0
    for i, reach in enumerate((IN_P, IN_U, IN_V, IN_W)):
        ext.append(
            jnp.concatenate(
                [low_ref[lead : lead + reach] * low_ok, raw_ref[i], high_ref[lead : lead + reach] * high_ok],
                axis=0,
            )
        )
        lead += reach

    def twice(value):
        once = inside(slope4(value), IN_P, low_ok, high_ok)
        return inside(slope4(once), IN_P, low_ok, high_ok)

    def put(place, value):
        reach = (value.shape[0] - own) // 2
        for j in range(own):
            out_ref[order[j], place] = value[reach + j]

    def slope2(value):
        return 0.5 * (value[IN_P + 1 : IN_P + 1 + own] - value[IN_P - 1 : IN_P - 1 + own])

    rows = ext[3].shape[0]
    high, low = halves(ext[3].reshape(rows * xs, nz))
    through = times_right([high], [low], right_ref[RIGHT.index("c")])
    cut = IN_V - IN_W
    rate = through.reshape(rows, xs, nz) + slope4(ext[2])[cut : cut + rows]
    rate = inside(rate, IN_W, low_ok, high_ok)
    for place, value in ((0, ext[0]), (3, ext[1]), (6, rate)):
        put(place, value)
        value = twice(value)
        put(place + 1, value)
        put(place + 2, twice(value))
    put(9, raw_ref[2])
    put(10, raw_ref[3])
    put(11, slope2(ext[1]))
    put(12, slope2(ext[3]))


class Raiser:
    def __init__(self, edge_ref, back_ref):
        self.low_ok, self.high_ok = edge_ref[0], edge_ref[1]
        self.back_ref = back_ref
        self.own = back_ref.shape[0]
        self.order = order_of(self.own)

    def load(self, slot):
        return jnp.stack([self.back_ref[self.order[j], slot] for j in range(self.own)])

    def total(self, fields):
        total = fields[-1]
        for value in fields[-2::-1]:
            edge = (total.shape[0] - self.own) // 2 + 2
            zeros = jnp.zeros((2,) + total.shape[1:], f32)
            total = slope4(jnp.concatenate([zeros, total, zeros], axis=0))
            centre = total[edge : edge + self.own]
            if value is not None:
                centre = centre + value
            total = jnp.concatenate(
                [total[:edge] * self.low_ok, centre, total[edge + self.own :] * self.high_ok], axis=0
            )
        return total


def gather_odd_kernel(edge_ref, back_ref, out_ref):
    @pl.when(edge_ref[2] > 0)
    def _():
        raiser = Raiser(edge_ref, back_ref)
        p = [raiser.load(10 + i) for i in range(4)]
        u = [raiser.load(14 + i) for i in range(3)]
        lead = 0
        for value in (
            raiser.total([None, p[0], None, p[1], None, p[2], None, p[3]]),
            raiser.total([None, u[0], None, u[1], None, u[2]]),
            raiser.total([None, raiser.load(17)]),
        ):
            out_ref[lead : lead + value.shape[0]] = value
            lead += value.shape[0]

    @pl.when(edge_ref[2] <= 0)
    def _():
        out_ref[...] = jnp.zeros(out_ref.shape, f32)


def gather_kernel(edge_ref, back_ref, own_ref, high_ref, low_ref):
    raiser = Raiser(edge_ref, back_ref)
    own = raiser.own
    sound = 1.0 - edge_ref[2]

    def extra(i):
        return sound * raiser.load(10 + i)

    p = [raiser.load(0), None, raiser.load(1), None, raiser.load(2), None, extra(0)]
    u = [raiser.load(3), None, raiser.load(4), None, extra(1)]
    w = [raiser.load(5), None, raiser.load(6), extra(4), extra(2), extra(5)]
    v = [raiser.load(7), raiser.load(8), extra(6), raiser.load(9), extra(7), extra(3), extra(8)]
    place = 0
    for output, (fields, room) in enumerate(((p, OUT_P), (u, OUT_U), (v, OUT_V), (w, OUT_W))):
        total = raiser.total(fields)
        reach = 2 * (len(fields) - 1)
        own_ref[output] = total[reach : reach + own]
        if room > reach:
            low_ref[place : place + room - reach] = jnp.zeros((room - reach,) + total.shape[1:], f32)
            high_ref[place + reach : place + room] = jnp.zeros((room - reach,) + total.shape[1:], f32)
        low_ref[place + room - reach : place + room] = total[:reach]
        high_ref[place : place + reach] = total[reach + own :]
        place += room


def plane(ref, index):
    blocks, _, xs, nz = ref.shape
    return ref[:, index].reshape(blocks * xs, nz)


def waves_kernel(in_ref, left_ref, right_ref, out_ref, sums_ref):
    do = Products(left_ref, right_ref)
    p0 = [plane(in_ref, i) for i in range(3)]
    u0 = [plane(in_ref, 3 + i) for i in range(3)]

    def advance(now, before):
        count = len(before) - 1
        one = do.left("m1", now[:count])
        two = do.left("m2", before[:count])
        three = do.right(before[:count], "cc")
        return [
            2.0 * now[i] - before[i] + (one[i] + two[i] + three[i] + tau**2 * before[i + 1])
            for i in range(count)
        ], one[0]

    moved = do.left("e1", p0)
    driven = do.left("ta", u0)
    p1 = [p0[i] + (moved[i] + driven[i] - tau * plane(in_ref, 6 + i)) for i in range(3)]
    h2 = p0[0] + moved[0] + p1[0]
    sums_ref[0] = h2
    p2, _ = advance(p1, p0)
    p3, twice = advance(p2, p1)
    h4 = h2 + do.left("e2", [h2])[0] + p2[0] + 0.5 * twice + p3[0]
    sums_ref[1] = h4
    p4, _ = advance(p3, p2)
    p5, twice = advance(p4, p3)
    sums_ref[2] = h4 + do.left("e2", [h4])[0] + p4[0] + 0.5 * twice + p5[0]
    out_ref[0] = p4[0]
    out_ref[1] = p5[0]


def held_kernel(in_ref, sums_ref, left_ref, right_ref, out_ref, later_ref):
    do = Products(left_ref, right_ref)
    start = [plane(in_ref, i) for i in (3, 10, 11, 12, 9)]
    h = [sums_ref[n] for n in range(3)]
    pull_x = do.left("a", h)
    pull_z = do.right(h, "c")
    begin = [start[0], start[4], start[1]]
    kept = do.left("e8", begin)
    for i in range(3):
        later_ref[i] = begin[i] + kept[i]
    for n, growth in enumerate(("e2", "e4", "e6")):
        change = do.left(growth, start)
        out_ref[n, 0] = start[0] + change[0] - tau * pull_x[n]
        out_ref[n, 1] = start[1] + change[1] - tau * pull_z[n]
        for k in (2, 3, 4):
            out_ref[n, k] = start[k] + change[k]


def minus_lamb(flag_ref, u, w, slope_u, slope_w, v):
    nx, nz = u.shape
    row = lax.broadcasted_iota(jnp.int32, (nx, nz), 0)
    lane = lax.broadcasted_iota(jnp.int32, (nx, nz), 1)
    blocks = flag_ref.shape[0] - 7
    region = jnp.concatenate([jnp.full((nx // blocks, nz), flag_ref[7 + i], f32) for i in range(blocks)], axis=0)

    def slope_x(value):
        ahead = jnp.where(row == nx - 1, 0.0, pltpu.roll(value, nx - 1, 0))
        behind = jnp.where(row == 0, 0.0, pltpu.roll(value, 1, 0))
        return 0.5 * (ahead - behind)

    def slope_z(value):
        ahead = jnp.where(lane == nz - 1, 0.0, pltpu.roll(value, nz - 1, 1))
        behind = jnp.where(lane == 0, 0.0, pltpu.roll(value, 1, 1))
        return 0.5 * (ahead - behind)

    o_x = slope_w - slope_z(v)
    o_y = slope_z(u) - slope_x(w)
    o_z = slope_x(v) - slope_u
    return region * (o_z * v - o_y * w), region * (o_x * w - o_z * u), region * (o_y * u - o_x * v)


def first_source_kernel(flag_ref, in_ref, out_ref):
    for k, value in enumerate(minus_lamb(flag_ref, *[plane(in_ref, i) for i in (3, 10, 11, 12, 9)])):
        out_ref[k] = value


def source_kernel(flag_ref, held_ref, up_ref, down_ref, far_ref, left_ref, right_ref, out_ref):
    do = Products(left_ref, right_ref)
    near = [flag_ref[3] * up_ref[n] - flag_ref[4] * down_ref[n] for n in range(3)]
    half = [0.5 * value for value in near]
    pull_x = do.left("a", half)
    pull_z = do.right(half, "c")
    for n in range(3):
        slope_u = held_ref[n, 2] - tau * pull_x[n]
        slope_w = held_ref[n, 3] - tau * pull_z[n]
        v = held_ref[n, 4] - tau * ((2.0 / 3.0) * near[n] - (1.0 / 12.0) * far_ref[n])
        values = minus_lamb(flag_ref, held_ref[n, 0], held_ref[n, 1], slope_u, slope_w, v)
        for k, value in enumerate(values):
            out_ref[n, k] = value


def source_at(refs, n, k):
    return refs[0][k] if n == 0 else refs[1][n - 1, k]


class Chain:
    def __init__(self, left_ref, right_ref):
        self.do = Products(left_ref, right_ref)

    def advance(self, now, before, drive, count):
        m_now = self.do.left("m1", now)
        m_before = self.do.left("m2", before)
        c_before = self.do.right(before, "cc")
        out = []
        for k in range(count):
            terms = []
            if k < len(now):
                terms.append(2.0 * now[k] + m_now[k])
            if k < len(before):
                terms.append(m_before[k] + c_before[k] - before[k])
            if 0 <= k - 2 < len(before):
                terms.append(tau**2 * before[k - 2])
            if k < len(drive):
                terms.append(drive[k])
            out.append(functools.reduce(lambda one, two: one + two, terms))
        return out, m_now

    def grow(self, sums, before, twice, now):
        kept = self.do.left("e2", sums) if sums else []
        out = [before[k] + 0.5 * twice[k] + now[k] for k in range(len(now))]
        return [out[k] + (sums[k] + kept[k]) if k < len(sums) else out[k] for k in range(len(now))]


def drives(do, flag_ref, own, moved, first, last):
    flow = flag_ref[2] > 0
    one = do.left("a", [source_at(moved, n, 0) for n in range(first, last)])
    two = do.right([source_at(moved, n, 2) for n in range(first, last)], "c")
    return [
        (
            jnp.where(flow, 0.0, -(tau**2) * (one[n - first] + two[n - first])),
            -(tau**2) * jnp.where(flow, source_at(own, n, 1), source_at(moved, n, 1)),
        )
        for n in range(first, last)
    ]


def driven_kernel(flag_ref, waves_ref, sums_ref, own0_ref, own_ref, moved0_ref, moved_ref, left_ref, right_ref, out_ref):
    chain = Chain(left_ref, right_ref)
    drive = drives(chain.do, flag_ref, (own0_ref, own_ref), (moved0_ref, moved_ref), 0, 2)
    q2 = list(drive[0])
    moved = chain.do.left("m1", q2)
    q3 = [2.0 * q2[k] + moved[k] + drive[0][k] for k in range(2)]
    g4 = chain.grow([], q2, moved, q3)
    q4, _ = chain.advance(q3, q2, drive[1], 4)
    q5, moved = chain.advance(q4, q3, drive[1], 4)
    g6 = chain.grow(g4, q4, moved, q5)
    for first, values, wave in ((0, q4, waves_ref[0]), (4, q5, waves_ref[1]), (8, g6, sums_ref[2])):
        out_ref[first] = values[0] + wave
        for k in range(1, 4):
            out_ref[first + k] = values[k]


def finish_kernel(flag_ref, later_ref, driven_ref, own_ref, moved0_ref, moved_ref, left_ref, right_ref, out_ref):
    chain = Chain(left_ref, right_ref)
    do = chain.do
    drive = drives(do, flag_ref, (None, own_ref), (moved0_ref, moved_ref), 2, 4)
    q4, q5, g6 = [[driven_ref[first + k] for k in range(4)] for first in (0, 4, 8)]
    q6, _ = chain.advance(q5, q4, drive[0], 6)
    q7, moved = chain.advance(q6, q5, drive[0], 6)
    for k, value in enumerate(chain.grow(g6, q6, moved, q7)):
        out_ref[8 + k] = value
    for k, value in enumerate(chain.advance(q7, q6, drive[1], 8)[0]):
        out_ref[k] = value
    flow = flag_ref[2] > 0

    def arrived(n):
        return [jnp.where(flow, 0.0, source_at((moved0_ref, moved_ref), n, k)) for k in range(3)]

    total = arrived(0)
    for n in (1, 2, 3):
        kept = do.left("e2", total)
        fresh = arrived(n)
        total = [total[k] + kept[k] + fresh[k] for k in range(3)]
    moved = do.left("e1", total)
    for i in range(3):
        out_ref[14 + i] = later_ref[i] + tau * (2.0 * total[i] + moved[i])


def filter_kernel(flag_ref, last_ref, left_ref, right_ref, out_ref):
    do = Products(left_ref, right_ref)
    blocks, _, xs, nz = out_ref.shape

    def emit(place, values):
        fx, fz = do.left("fx", values), do.right(values, "fz")
        for i, value in enumerate(values):
            out_ref[:, place + i] = (value + fx[i] + fz[i]).reshape(blocks, xs, nz)

    loaded = {}

    def load(k):
        if k not in loaded:
            loaded[k] = last_ref[k]
        return loaded[k]

    def p(k):
        return last_ref[k]

    def h(k):
        return load(8 + k)

    def third(*which):
        return [-tau * value for value in do.right([h(k) for k in which], "c")]

    axial = do.left("ta", [h(0), h(2)])
    depth = third(0, 2)
    emit(0, [p(0), p(2), p(4), last_ref[14] + axial[0], axial[1], last_ref[16] + depth[0], depth[1]])
    emit(7, [last_ref[15], -tau * h(0), -tau * h(2)])

    @pl.when(flag_ref[2] > 0)
    def _():
        loaded.clear()
        do.split.clear()
        axial = do.left("ta", [h(1), h(3), h(5)])
        emit(10, [p(1), p(3), p(5), p(7)] + axial + third(1))
        out_ref[:, 18] = jnp.zeros((blocks, xs, nz), f32)

    @pl.when(flag_ref[2] <= 0)
    def _():
        loaded.clear()
        do.split.clear()
        axial = do.left("ta", [h(4)])
        depth = third(4, 3, 5)
        emit(10, [p(6), axial[0], depth[0], -tau * h(4), depth[1], depth[2]])
        emit(16, [-tau * h(1), -tau * h(3), -tau * h(5)])


def along_y(steps):
    streams, slabs = lax.axis_size("stream"), lax.axis_size("slab")
    count = streams * slabs
    order = order_of(streams)

    def device(y):
        return order[y % streams] * slabs + (y // streams) % slabs

    return [
        (section * count + device(y), section * count + device((y + far) % count))
        for section, far in ((0, steps), (1, 2 * steps))
        for y in range(count)
    ]


def shards(state, source_mask, deriv_x, deriv_z, filter_x, filter_z):
    _, _, xs, own, nz = state.shape
    slabs, streams = lax.axis_size("slab"), lax.axis_size("stream")
    slab = lax.axis_index("slab")
    nx = xs * streams
    upward = [(i, (i + 1) % slabs) for i in range(slabs)]
    downward = [((i + 1) % slabs, i) for i in range(slabs)]
    swap = [(0, 1), (1, 0)]
    inverse = [0] * streams
    for j, stream in enumerate(order_of(streams)):
        inverse[stream] = j
    y = slab * streams + jnp.asarray(inverse, jnp.int32)[lax.axis_index("stream")]
    last_y = slabs * streams - 1
    flags = [slab > 0, slab < slabs - 1, lax.axis_index("section") == 0]
    flags += [y < last_y, y > 0, y < last_y - 1, y > 1]
    edges = jnp.concatenate([jnp.stack(flags).astype(f32), source_mask[:, 0].astype(f32)])
    reaches = (IN_P, IN_U, IN_V, IN_W)
    top = jnp.concatenate([state[0, i, :, own - reach :] for i, reach in enumerate(reaches)], axis=1)
    bottom = jnp.concatenate([state[0, i, :, :reach] for i, reach in enumerate(reaches)], axis=1)
    from_low = jnp.swapaxes(lax.ppermute(top, "slab", upward), 0, 1)
    from_high = jnp.swapaxes(lax.ppermute(bottom, "slab", downward), 0, 1)
    raw = jnp.swapaxes(state[0], 1, 2)
    forms = (
        jax.ShapeDtypeStruct((len(LEFT), nx, 3 * nx), bf16),
        jax.ShapeDtypeStruct((len(RIGHT), 3 * nz, nz), bf16),
    )
    matrices = (deriv_x, deriv_z.T, filter_x, filter_z.T)
    left, right = call(prepare_kernel, forms, *matrices, flops=10**9)

    def shape(*dims):
        return jax.ShapeDtypeStruct(dims, f32)

    def with_edges(body, out_shape, *args):
        return pl.pallas_call(
            body,
            out_shape=out_shape,
            in_specs=[pl.BlockSpec(memory_space=pltpu.SMEM)]
            + [pl.BlockSpec(memory_space=pltpu.VMEM)] * len(args),
            compiler_params=pltpu.CompilerParams(vmem_limit_bytes=24 * 2**20),
        )(edges, *args)

    spread = with_edges(spread_kernel, shape(own, 13, xs, nz), raw, from_low, from_high, right)
    planes = lax.all_to_all(spread, "stream", split_axis=0, concat_axis=0, tiled=True)
    waves, sums = call(
        waves_kernel, (shape(2, nx, nz), shape(3, nx, nz)), planes, left, right, flops=2 * 10**9
    )
    source0 = with_edges(first_source_kernel, shape(3, nx, nz), planes)
    moved0 = lax.ppermute(source0, "section", swap)
    across = lax.ppermute(sums, "section", swap)
    carried = jnp.where(edges[2] > 0, sums, across)
    up, down = [lax.ppermute(carried, AXES, along_y(steps)) for steps in (-1, 1)]
    vmem, anywhere = pl.BlockSpec(memory_space=pltpu.VMEM), pl.BlockSpec(memory_space=pl.ANY)
    left, right = pl.pallas_call(
        prepare_later_kernel,
        out_shape=forms,
        in_specs=[anywhere] + [vmem] * 4,
        compiler_params=pltpu.CompilerParams(vmem_limit_bytes=24 * 2**20),
        cost_estimate=pl.CostEstimate(flops=10**9, bytes_accessed=8 * 10**6, transcendentals=0),
    )(sums, *matrices)
    held, later = call(
        held_kernel, (shape(3, 5, nx, nz), shape(3, nx, nz)), planes, sums, left, right, flops=10**9)
    far = pl.pallas_call(
        far_kernel,
        out_shape=shape(3, nx, nz),
        in_specs=[pl.BlockSpec(memory_space=pltpu.SMEM), vmem, vmem, anywhere, anywhere],
        compiler_params=pltpu.CompilerParams(vmem_limit_bytes=8 * 2**20),
    )(edges, up, down, held, moved0)
    far = lax.ppermute(far, "section", swap)
    source = with_edges(source_kernel, shape(3, 3, nx, nz), held, up, down, far, left, right)
    moved = lax.ppermute(source, "section", swap)
    driven = with_edges(
        driven_kernel, shape(12, nx, nz), waves, sums, source0, source, moved0, moved, left, right
    )
    last = with_edges(finish_kernel, shape(17, nx, nz), later, driven, source, moved0, moved, left, right)
    done = with_edges(filter_kernel, shape(streams, SLOTS, xs, nz), last, left, right)
    back = lax.all_to_all(done, "stream", split_axis=0, concat_axis=0, tiled=True)
    border = OUT_P + OUT_U + OUT_V + OUT_W
    rows = ((OUT_P, 0), (OUT_U, 1), (2, 3))
    odd = with_edges(gather_odd_kernel, shape(sum(own + 2 * reach for reach, _ in rows), xs, nz), back)
    odd = lax.ppermute(odd, "section", swap)
    mine, high, low = with_edges(
        gather_kernel, (shape(4, own, xs, nz), shape(border, xs, nz), shape(border, xs, nz)), back
    )
    starts = (0, OUT_P, OUT_P + OUT_U, OUT_P + OUT_U + OUT_V)
    reaches = (OUT_P, OUT_U, OUT_V, OUT_W)
    lead = 0
    more_high, more_low, more_own = [], [], [jnp.zeros((own, xs, nz), f32)] * 4
    for reach, output in rows:
        part = odd[lead : lead + own + 2 * reach]
        start, room = starts[output], reaches[output]
        more_low.append(jnp.pad(part[:reach], ((start + room - reach, border - start - room), (0, 0), (0, 0))))
        more_high.append(jnp.pad(part[reach + own :], ((start, border - start - reach), (0, 0), (0, 0))))
        more_own[output] = part[reach : reach + own]
        lead += own + 2 * reach
    from_low = lax.ppermute(high + sum(more_high), "slab", upward)
    from_high = lax.ppermute(low + sum(more_low), "slab", downward)
    outs = []
    for i, (start, reach) in enumerate(zip(starts, reaches)):
        from_below = jnp.pad(from_low[start : start + reach], ((0, own - reach), (0, 0), (0, 0)))
        from_above = jnp.pad(from_high[start : start + reach], ((own - reach, 0), (0, 0), (0, 0)))
        outs.append(mine[i] + more_own[i] + from_below + from_above)
    return jnp.swapaxes(jnp.stack(outs), 1, 2)[None]


def solution(mesh):
    placed = (P("section", None, "stream", "slab", None), P(None, "slab"), P(), P(), P(), P())
    return jax.shard_map(
        shards,
        mesh=mesh,
        in_specs=placed,
        out_specs=P("section", None, "stream", "slab", None),
        check_vma=False,
    )
```

```python
import functools

import jax
import jax.numpy as jnp
from jax import lax
from jax.experimental import pallas as pl
from jax.experimental.pallas import tpu as pltpu
from jax.sharding import PartitionSpec as P

mach_number = 0.5
tau = 0.05
filter_weight = 0.25
IN_P, IN_U, IN_V, IN_W = 8, 8, 10, 8
SLOTS = 19
OUT_P, OUT_U, OUT_V, OUT_W = 14, 10, 12, 10
AXES = ("section", "stream", "slab")
LEFT = ("e1", "ta", "m1", "m2", "e2", "a", "e4", "e6", "e8", "fx")
RIGHT = ("c", "cc", "fz")
f32, bf16 = jnp.float32, jnp.bfloat16


def call(body, out_shape, *args, flops=0, scratch=()):
    moved = sum(a.size * a.dtype.itemsize for a in args)
    return pl.pallas_call(
        body,
        out_shape=out_shape,
        scratch_shapes=scratch,
        compiler_params=pltpu.CompilerParams(vmem_limit_bytes=24 * 2**20),
        cost_estimate=pl.CostEstimate(flops=flops, bytes_accessed=moved, transcendentals=0),
    )(*args)


def order_of(count):
    places = []
    for j in range(count):
        step, rung = j // 2, j % 2
        x, y = (rung, step) if step < 4 else (3 - rung, 7 - step)
        places.append(4 * x + y)
    return places


def halves(value):
    high = value.astype(bf16)
    return high, (value - high.astype(f32)).astype(bf16)


def left_form(matrix):
    high, low = halves(matrix)
    return jnp.concatenate([high, high, low], axis=1)


def right_form(matrix):
    high, low = halves(matrix)
    return jnp.concatenate([high, high, low], axis=0)


def times_left(form, high, low):
    high, low = jnp.concatenate(high, axis=1), jnp.concatenate(low, axis=1)
    return jnp.dot(form, jnp.concatenate([high, low, high], axis=0), preferred_element_type=f32)


def times_right(high, low, form):
    high, low = jnp.concatenate(high, axis=0), jnp.concatenate(low, axis=0)
    return jnp.dot(jnp.concatenate([high, low, high], axis=1), form, preferred_element_type=f32)


def prepare_kernel(dx_ref, dzt_ref, fx_ref, fzt_ref, left_ref, right_ref):
    def dot(one, two):
        return jnp.dot(one, two, precision=lax.Precision.HIGHEST, preferred_element_type=f32)

    dx, dzt = dx_ref[...], dzt_ref[...]
    square = dot(dx, dx)
    e1 = -tau * mach_number * dx
    e2 = 2.0 * e1 + (tau * mach_number) ** 2 * square
    e4 = 2.0 * e2 + dot(e2, e2)
    values = {
        "e1": e1,
        "ta": -tau * dx,
        "m1": 2.0 * e1,
        "m2": tau**2 * square - e2,
        "e2": e2,
        "a": dx,
        "e4": e4,
        "e6": e2 + e4 + dot(e2, e4),
        "e8": 2.0 * e4 + dot(e4, e4),
        "fx": filter_weight * fx_ref[...],
    }
    for i, name in enumerate(LEFT):
        left_ref[i] = left_form(values[name])
    others = {"c": dzt, "cc": tau**2 * dot(dzt, dzt), "fz": filter_weight * fzt_ref[...]}
    for i, name in enumerate(RIGHT):
        right_ref[i] = right_form(others[name])


def prepare_later_kernel(after_ref, *refs):
    prepare_kernel(*refs)


def far_kernel(flag_ref, up_ref, down_ref, after_ref, later_ref, out_ref):
    for n in range(out_ref.shape[0]):
        out_ref[n] = flag_ref[5] * up_ref[n] - flag_ref[6] * down_ref[n]


class Products:
    def __init__(self, left_ref, right_ref):
        self.left_ref, self.right_ref = left_ref, right_ref
        self.split = {}

    def halves(self, planes):
        for value in planes:
            if id(value) not in self.split:
                self.split[id(value)] = (value, *halves(value))
        found = [self.split[id(value)] for value in planes]
        return [one[1] for one in found], [one[2] for one in found]

    def left(self, name, planes):
        out = times_left(self.left_ref[LEFT.index(name)], *self.halves(planes))
        width = planes[0].shape[1]
        return [out[:, i * width : (i + 1) * width] for i in range(len(planes))]

    def right(self, planes, name):
        out = times_right(*self.halves(planes), self.right_ref[RIGHT.index(name)])
        length = planes[0].shape[0]
        return [out[i * length : (i + 1) * length] for i in range(len(planes))]


def inside(value, reach, low_ok, high_ok):
    rows = value.shape[0]
    return jnp.concatenate(
        [value[:reach] * low_ok, value[reach : rows - reach], value[rows - reach :] * high_ok], axis=0
    )


def shift_rows(value, steps):
    zeros = jnp.zeros((abs(steps),) + value.shape[1:], f32)
    if steps > 0:
        return jnp.concatenate([value[steps:], zeros], axis=0)
    return jnp.concatenate([zeros, value[:steps]], axis=0)


def slope4(value):
    near = shift_rows(value, 1) - shift_rows(value, -1)
    far = shift_rows(value, 2) - shift_rows(value, -2)
    return (2.0 / 3.0) * near - (1.0 / 12.0) * far


def spread_kernel(edge_ref, raw_ref, low_ref, high_ref, right_ref, out_ref):
    low_ok, high_ok = edge_ref[0], edge_ref[1]
    own, xs, nz = raw_ref.shape[1:]
    order = order_of(own)
    ext = []
    lead = 0
    for i, reach in enumerate((IN_P, IN_U, IN_V, IN_W)):
        ext.append(
            jnp.concatenate(
                [low_ref[lead : lead + reach] * low_ok, raw_ref[i], high_ref[lead : lead + reach] * high_ok],
                axis=0,
            )
        )
        lead += reach

    def twice(value):
        once = inside(slope4(value), IN_P, low_ok, high_ok)
        return inside(slope4(once), IN_P, low_ok, high_ok)

    def put(place, value):
        reach = (value.shape[0] - own) // 2
        for j in range(own):
            out_ref[order[j], place] = value[reach + j]

    def slope2(value):
        return 0.5 * (value[IN_P + 1 : IN_P + 1 + own] - value[IN_P - 1 : IN_P - 1 + own])

    rows = ext[3].shape[0]
    high, low = halves(ext[3].reshape(rows * xs, nz))
    through = times_right([high], [low], right_ref[RIGHT.index("c")])
    cut = IN_V - IN_W
    rate = through.reshape(rows, xs, nz) + slope4(ext[2])[cut : cut + rows]
    rate = inside(rate, IN_W, low_ok, high_ok)
    for place, value in ((0, ext[0]), (3, ext[1]), (6, rate)):
        put(place, value)
        value = twice(value)
        put(place + 1, value)
        put(place + 2, twice(value))
    put(9, raw_ref[2])
    put(10, raw_ref[3])
    put(11, slope2(ext[1]))
    put(12, slope2(ext[3]))


class Raiser:
    def __init__(self, edge_ref, back_ref):
        self.low_ok, self.high_ok = edge_ref[0], edge_ref[1]
        self.back_ref = back_ref
        self.own = back_ref.shape[0]
        self.order = order_of(self.own)

    def load(self, slot):
        return jnp.stack([self.back_ref[self.order[j], slot] for j in range(self.own)])

    def total(self, fields):
        total = fields[-1]
        for value in fields[-2::-1]:
            edge = (total.shape[0] - self.own) // 2 + 2
            zeros = jnp.zeros((2,) + total.shape[1:], f32)
            total = slope4(jnp.concatenate([zeros, total, zeros], axis=0))
            centre = total[edge : edge + self.own]
            if value is not None:
                centre = centre + value
            total = jnp.concatenate(
                [total[:edge] * self.low_ok, centre, total[edge + self.own :] * self.high_ok], axis=0
            )
        return total


def gather_odd_kernel(edge_ref, back_ref, out_ref):
    @pl.when(edge_ref[2] > 0)
    def _():
        raiser = Raiser(edge_ref, back_ref)
        p = [raiser.load(10 + i) for i in range(4)]
        u = [raiser.load(14 + i) for i in range(3)]
        lead = 0
        for value in (
            raiser.total([None, p[0], None, p[1], None, p[2], None, p[3]]),
            raiser.total([None, u[0], None, u[1], None, u[2]]),
            raiser.total([None, raiser.load(17)]),
        ):
            out_ref[lead : lead + value.shape[0]] = value
            lead += value.shape[0]

    @pl.when(edge_ref[2] <= 0)
    def _():
        out_ref[...] = jnp.zeros(out_ref.shape, f32)


def gather_kernel(edge_ref, back_ref, own_ref, high_ref, low_ref):
    raiser = Raiser(edge_ref, back_ref)
    own = raiser.own
    sound = 1.0 - edge_ref[2]

    def extra(i):
        return sound * raiser.load(10 + i)

    p = [raiser.load(0), None, raiser.load(1), None, raiser.load(2), None, extra(0)]
    u = [raiser.load(3), None, raiser.load(4), None, extra(1)]
    w = [raiser.load(5), None, raiser.load(6), extra(4), extra(2), extra(5)]
    v = [raiser.load(7), raiser.load(8), extra(6), raiser.load(9), extra(7), extra(3), extra(8)]
    place = 0
    for output, (fields, room) in enumerate(((p, OUT_P), (u, OUT_U), (v, OUT_V), (w, OUT_W))):
        total = raiser.total(fields)
        reach = 2 * (len(fields) - 1)
        own_ref[output] = total[reach : reach + own]
        if room > reach:
            low_ref[place : place + room - reach] = jnp.zeros((room - reach,) + total.shape[1:], f32)
            high_ref[place + reach : place + room] = jnp.zeros((room - reach,) + total.shape[1:], f32)
        low_ref[place + room - reach : place + room] = total[:reach]
        high_ref[place : place + reach] = total[reach + own :]
        place += room


def plane(ref, index):
    blocks, _, xs, nz = ref.shape
    return ref[:, index].reshape(blocks * xs, nz)


def waves_kernel(in_ref, left_ref, right_ref, out_ref, sums_ref):
    do = Products(left_ref, right_ref)
    p0 = [plane(in_ref, i) for i in range(3)]
    u0 = [plane(in_ref, 3 + i) for i in range(3)]

    def advance(now, before):
        count = len(before) - 1
        one = do.left("m1", now[:count])
        two = do.left("m2", before[:count])
        three = do.right(before[:count], "cc")
        return [
            2.0 * now[i] - before[i] + (one[i] + two[i] + three[i] + tau**2 * before[i + 1])
            for i in range(count)
        ], one[0]

    moved = do.left("e1", p0)
    driven = do.left("ta", u0)
    p1 = [p0[i] + (moved[i] + driven[i] - tau * plane(in_ref, 6 + i)) for i in range(3)]
    h2 = p0[0] + moved[0] + p1[0]
    sums_ref[0] = h2
    p2, _ = advance(p1, p0)
    p3, twice = advance(p2, p1)
    h4 = h2 + do.left("e2", [h2])[0] + p2[0] + 0.5 * twice + p3[0]
    sums_ref[1] = h4
    p4, _ = advance(p3, p2)
    p5, twice = advance(p4, p3)
    sums_ref[2] = h4 + do.left("e2", [h4])[0] + p4[0] + 0.5 * twice + p5[0]
    out_ref[0] = p4[0]
    out_ref[1] = p5[0]


def held_kernel(in_ref, sums_ref, left_ref, right_ref, out_ref, later_ref):
    do = Products(left_ref, right_ref)
    start = [plane(in_ref, i) for i in (3, 10, 11, 12, 9)]
    h = [sums_ref[n] for n in range(3)]
    pull_x = do.left("a", h)
    pull_z = do.right(h, "c")
    begin = [start[0], start[4], start[1]]
    kept = do.left("e8", begin)
    for i in range(3):
        later_ref[i] = begin[i] + kept[i]
    for n, growth in enumerate(("e2", "e4", "e6")):
        change = do.left(growth, start)
        out_ref[n, 0] = start[0] + change[0] - tau * pull_x[n]
        out_ref[n, 1] = start[1] + change[1] - tau * pull_z[n]
        for k in (2, 3, 4):
            out_ref[n, k] = start[k] + change[k]


def minus_lamb(flag_ref, u, w, slope_u, slope_w, v):
    nx, nz = u.shape
    row = lax.broadcasted_iota(jnp.int32, (nx, nz), 0)
    lane = lax.broadcasted_iota(jnp.int32, (nx, nz), 1)
    blocks = flag_ref.shape[0] - 7
    region = jnp.concatenate([jnp.full((nx // blocks, nz), flag_ref[7 + i], f32) for i in range(blocks)], axis=0)

    def slope_x(value):
        ahead = jnp.where(row == nx - 1, 0.0, pltpu.roll(value, nx - 1, 0))
        behind = jnp.where(row == 0, 0.0, pltpu.roll(value, 1, 0))
        return 0.5 * (ahead - behind)

    def slope_z(value):
        ahead = jnp.where(lane == nz - 1, 0.0, pltpu.roll(value, nz - 1, 1))
        behind = jnp.where(lane == 0, 0.0, pltpu.roll(value, 1, 1))
        return 0.5 * (ahead - behind)

    o_x = slope_w - slope_z(v)
    o_y = slope_z(u) - slope_x(w)
    o_z = slope_x(v) - slope_u
    return region * (o_z * v - o_y * w), region * (o_x * w - o_z * u), region * (o_y * u - o_x * v)


def first_source_kernel(flag_ref, in_ref, after_ref, out_ref):
    for k, value in enumerate(minus_lamb(flag_ref, *[plane(in_ref, i) for i in (3, 10, 11, 12, 9)])):
        out_ref[k] = value


def source_kernel(flag_ref, held_ref, up_ref, down_ref, far_ref, left_ref, right_ref, out_ref):
    do = Products(left_ref, right_ref)
    near = [flag_ref[3] * up_ref[n] - flag_ref[4] * down_ref[n] for n in range(3)]
    half = [0.5 * value for value in near]
    pull_x = do.left("a", half)
    pull_z = do.right(half, "c")
    for n in range(3):
        slope_u = held_ref[n, 2] - tau * pull_x[n]
        slope_w = held_ref[n, 3] - tau * pull_z[n]
        v = held_ref[n, 4] - tau * ((2.0 / 3.0) * near[n] - (1.0 / 12.0) * far_ref[n])
        values = minus_lamb(flag_ref, held_ref[n, 0], held_ref[n, 1], slope_u, slope_w, v)
        for k, value in enumerate(values):
            out_ref[n, k] = value


def source_at(refs, n, k):
    return refs[0][k] if n == 0 else refs[1][n - 1, k]


class Chain:
    def __init__(self, left_ref, right_ref):
        self.do = Products(left_ref, right_ref)

    def advance(self, now, before, drive, count):
        m_now = self.do.left("m1", now)
        m_before = self.do.left("m2", before)
        c_before = self.do.right(before, "cc")
        out = []
        for k in range(count):
            terms = []
            if k < len(now):
                terms.append(2.0 * now[k] + m_now[k])
            if k < len(before):
                terms.append(m_before[k] + c_before[k] - before[k])
            if 0 <= k - 2 < len(before):
                terms.append(tau**2 * before[k - 2])
            if k < len(drive):
                terms.append(drive[k])
            out.append(functools.reduce(lambda one, two: one + two, terms))
        return out, m_now

    def grow(self, sums, before, twice, now):
        kept = self.do.left("e2", sums) if sums else []
        out = [before[k] + 0.5 * twice[k] + now[k] for k in range(len(now))]
        return [out[k] + (sums[k] + kept[k]) if k < len(sums) else out[k] for k in range(len(now))]


def drives(do, flag_ref, own, moved, first, last):
    flow = flag_ref[2] > 0
    one = do.left("a", [source_at(moved, n, 0) for n in range(first, last)])
    two = do.right([source_at(moved, n, 2) for n in range(first, last)], "c")
    return [
        (
            jnp.where(flow, 0.0, -(tau**2) * (one[n - first] + two[n - first])),
            -(tau**2) * jnp.where(flow, source_at(own, n, 1), source_at(moved, n, 1)),
        )
        for n in range(first, last)
    ]


def driven_kernel(flag_ref, waves_ref, sums_ref, own0_ref, own_ref, moved0_ref, moved_ref, left_ref, right_ref, out_ref):
    chain = Chain(left_ref, right_ref)
    drive = drives(chain.do, flag_ref, (own0_ref, own_ref), (moved0_ref, moved_ref), 0, 2)
    q2 = list(drive[0])
    moved = chain.do.left("m1", q2)
    q3 = [2.0 * q2[k] + moved[k] + drive[0][k] for k in range(2)]
    g4 = chain.grow([], q2, moved, q3)
    q4, _ = chain.advance(q3, q2, drive[1], 4)
    q5, moved = chain.advance(q4, q3, drive[1], 4)
    g6 = chain.grow(g4, q4, moved, q5)
    for first, values, wave in ((0, q4, waves_ref[0]), (4, q5, waves_ref[1]), (8, g6, sums_ref[2])):
        out_ref[first] = values[0] + wave
        for k in range(1, 4):
            out_ref[first + k] = values[k]


def finish_kernel(flag_ref, later_ref, driven_ref, own_ref, moved0_ref, moved_ref, left_ref, right_ref, out_ref):
    chain = Chain(left_ref, right_ref)
    do = chain.do
    drive = drives(do, flag_ref, (None, own_ref), (moved0_ref, moved_ref), 2, 4)
    q4, q5, g6 = [[driven_ref[first + k] for k in range(4)] for first in (0, 4, 8)]
    q6, _ = chain.advance(q5, q4, drive[0], 6)
    q7, moved = chain.advance(q6, q5, drive[0], 6)
    for k, value in enumerate(chain.grow(g6, q6, moved, q7)):
        out_ref[8 + k] = value
    for k, value in enumerate(chain.advance(q7, q6, drive[1], 8)[0]):
        out_ref[k] = value
    flow = flag_ref[2] > 0

    def arrived(n):
        return [jnp.where(flow, 0.0, source_at((moved0_ref, moved_ref), n, k)) for k in range(3)]

    total = arrived(0)
    for n in (1, 2, 3):
        kept = do.left("e2", total)
        fresh = arrived(n)
        total = [total[k] + kept[k] + fresh[k] for k in range(3)]
    moved = do.left("e1", total)
    for i in range(3):
        out_ref[14 + i] = later_ref[i] + tau * (2.0 * total[i] + moved[i])


def filter_kernel(flag_ref, last_ref, left_ref, right_ref, out_ref):
    do = Products(left_ref, right_ref)
    blocks, _, xs, nz = out_ref.shape

    def emit(place, values):
        fx, fz = do.left("fx", values), do.right(values, "fz")
        for i, value in enumerate(values):
            out_ref[:, place + i] = (value + fx[i] + fz[i]).reshape(blocks, xs, nz)

    loaded = {}

    def load(k):
        if k not in loaded:
            loaded[k] = last_ref[k]
        return loaded[k]

    def p(k):
        return last_ref[k]

    def h(k):
        return load(8 + k)

    def third(*which):
        return [-tau * value for value in do.right([h(k) for k in which], "c")]

    axial = do.left("ta", [h(0), h(2)])
    depth = third(0, 2)
    emit(0, [p(0), p(2), p(4), last_ref[14] + axial[0], axial[1], last_ref[16] + depth[0], depth[1]])
    emit(7, [last_ref[15], -tau * h(0), -tau * h(2)])

    @pl.when(flag_ref[2] > 0)
    def _():
        loaded.clear()
        do.split.clear()
        axial = do.left("ta", [h(1), h(3), h(5)])
        emit(10, [p(1), p(3), p(5), p(7)] + axial + third(1))
        out_ref[:, 18] = jnp.zeros((blocks, xs, nz), f32)

    @pl.when(flag_ref[2] <= 0)
    def _():
        loaded.clear()
        do.split.clear()
        axial = do.left("ta", [h(4)])
        depth = third(4, 3, 5)
        emit(10, [p(6), axial[0], depth[0], -tau * h(4), depth[1], depth[2]])
        emit(16, [-tau * h(1), -tau * h(3), -tau * h(5)])


def along_y(steps):
    streams, slabs = lax.axis_size("stream"), lax.axis_size("slab")
    count = streams * slabs
    order = order_of(streams)

    def device(y):
        return order[y % streams] * slabs + (y // streams) % slabs

    return [
        (section * count + device(y), section * count + device((y + far) % count))
        for section, far in ((0, steps), (1, 2 * steps))
        for y in range(count)
    ]


def shards(state, source_mask, deriv_x, deriv_z, filter_x, filter_z):
    _, _, xs, own, nz = state.shape
    slabs, streams = lax.axis_size("slab"), lax.axis_size("stream")
    slab = lax.axis_index("slab")
    nx = xs * streams
    upward = [(i, (i + 1) % slabs) for i in range(slabs)]
    downward = [((i + 1) % slabs, i) for i in range(slabs)]
    swap = [(0, 1), (1, 0)]
    inverse = [0] * streams
    for j, stream in enumerate(order_of(streams)):
        inverse[stream] = j
    y = slab * streams + jnp.asarray(inverse, jnp.int32)[lax.axis_index("stream")]
    last_y = slabs * streams - 1
    flags = [slab > 0, slab < slabs - 1, lax.axis_index("section") == 0]
    flags += [y < last_y, y > 0, y < last_y - 1, y > 1]
    edges = jnp.concatenate([jnp.stack(flags).astype(f32), source_mask[:, 0].astype(f32)])
    reaches = (IN_P, IN_U, IN_V, IN_W)
    top = jnp.concatenate([state[0, i, :, own - reach :] for i, reach in enumerate(reaches)], axis=1)
    bottom = jnp.concatenate([state[0, i, :, :reach] for i, reach in enumerate(reaches)], axis=1)
    from_low = jnp.swapaxes(lax.ppermute(top, "slab", upward), 0, 1)
    from_high = jnp.swapaxes(lax.ppermute(bottom, "slab", downward), 0, 1)
    raw = jnp.swapaxes(state[0], 1, 2)
    forms = (
        jax.ShapeDtypeStruct((len(LEFT), nx, 3 * nx), bf16),
        jax.ShapeDtypeStruct((len(RIGHT), 3 * nz, nz), bf16),
    )
    matrices = (deriv_x, deriv_z.T, filter_x, filter_z.T)
    left, right = call(prepare_kernel, forms, *matrices, flops=10**9)

    def shape(*dims):
        return jax.ShapeDtypeStruct(dims, f32)

    def with_edges(body, out_shape, *args):
        return pl.pallas_call(
            body,
            out_shape=out_shape,
            in_specs=[pl.BlockSpec(memory_space=pltpu.SMEM)]
            + [pl.BlockSpec(memory_space=pltpu.VMEM)] * len(args),
            compiler_params=pltpu.CompilerParams(vmem_limit_bytes=24 * 2**20),
        )(edges, *args)

    spread = with_edges(spread_kernel, shape(own, 13, xs, nz), raw, from_low, from_high, right)
    planes = lax.all_to_all(spread, "stream", split_axis=0, concat_axis=0, tiled=True)
    waves, sums = call(
        waves_kernel, (shape(2, nx, nz), shape(3, nx, nz)), planes, left, right, flops=2 * 10**9
    )
    across = lax.ppermute(sums, "section", swap)
    carried = jnp.where(edges[2] > 0, sums, across)
    up, down = [lax.ppermute(carried, AXES, along_y(steps)) for steps in (-1, 1)]
    vmem, anywhere = pl.BlockSpec(memory_space=pltpu.VMEM), pl.BlockSpec(memory_space=pl.ANY)
    left, right = pl.pallas_call(
        prepare_later_kernel,
        out_shape=forms,
        in_specs=[anywhere] + [vmem] * 4,
        compiler_params=pltpu.CompilerParams(vmem_limit_bytes=24 * 2**20),
        cost_estimate=pl.CostEstimate(flops=10**9, bytes_accessed=8 * 10**6, transcendentals=0),
    )(across, *matrices)
    held, later = call(
        held_kernel, (shape(3, 5, nx, nz), shape(3, nx, nz)), planes, sums, left, right, flops=10**9)
    source0 = pl.pallas_call(
        first_source_kernel,
        out_shape=shape(3, nx, nz),
        in_specs=[pl.BlockSpec(memory_space=pltpu.SMEM), vmem, anywhere],
        compiler_params=pltpu.CompilerParams(vmem_limit_bytes=24 * 2**20),
    )(edges, planes, held)
    moved0 = lax.ppermute(source0, "section", swap)
    far = pl.pallas_call(
        far_kernel,
        out_shape=shape(3, nx, nz),
        in_specs=[pl.BlockSpec(memory_space=pltpu.SMEM), vmem, vmem, anywhere, anywhere],
        compiler_params=pltpu.CompilerParams(vmem_limit_bytes=8 * 2**20),
    )(edges, up, down, held, moved0)
    far = lax.ppermute(far, "section", swap)
    source = with_edges(source_kernel, shape(3, 3, nx, nz), held, up, down, far, left, right)
    moved = lax.ppermute(source, "section", swap)
    driven = with_edges(
        driven_kernel, shape(12, nx, nz), waves, sums, source0, source, moved0, moved, left, right
    )
    last = with_edges(finish_kernel, shape(17, nx, nz), later, driven, source, moved0, moved, left, right)
    done = with_edges(filter_kernel, shape(streams, SLOTS, xs, nz), last, left, right)
    back = lax.all_to_all(done, "stream", split_axis=0, concat_axis=0, tiled=True)
    border = OUT_P + OUT_U + OUT_V + OUT_W
    rows = ((OUT_P, 0), (OUT_U, 1), (2, 3))
    odd = with_edges(gather_odd_kernel, shape(sum(own + 2 * reach for reach, _ in rows), xs, nz), back)
    odd = lax.ppermute(odd, "section", swap)
    mine, high, low = with_edges(
        gather_kernel, (shape(4, own, xs, nz), shape(border, xs, nz), shape(border, xs, nz)), back
    )
    starts = (0, OUT_P, OUT_P + OUT_U, OUT_P + OUT_U + OUT_V)
    reaches = (OUT_P, OUT_U, OUT_V, OUT_W)
    lead = 0
    more_high, more_low, more_own = [], [], [jnp.zeros((own, xs, nz), f32)] * 4
    for reach, output in rows:
        part = odd[lead : lead + own + 2 * reach]
        start, room = starts[output], reaches[output]
        more_low.append(jnp.pad(part[:reach], ((start + room - reach, border - start - room), (0, 0), (0, 0))))
        more_high.append(jnp.pad(part[reach + own :], ((start, border - start - reach), (0, 0), (0, 0))))
        more_own[output] = part[reach : reach + own]
        lead += own + 2 * reach
    from_low = lax.ppermute(high + sum(more_high), "slab", upward)
    from_high = lax.ppermute(low + sum(more_low), "slab", downward)
    outs = []
    for i, (start, reach) in enumerate(zip(starts, reaches)):
        from_below = jnp.pad(from_low[start : start + reach], ((0, own - reach), (0, 0), (0, 0)))
        from_above = jnp.pad(from_high[start : start + reach], ((own - reach, 0), (0, 0), (0, 0)))
        outs.append(mine[i] + more_own[i] + from_below + from_above)
    return jnp.swapaxes(jnp.stack(outs), 1, 2)[None]


def solution(mesh):
    placed = (P("section", None, "stream", "slab", None), P(None, "slab"), P(), P(), P(), P())
    return jax.shard_map(
        shards,
        mesh=mesh,
        in_specs=placed,
        out_specs=P("section", None, "stream", "slab", None),
        check_vma=False,
    )
```
